128 devices in a mesh: role: 2 (over core), rep: 2 (over z_hi), tile: 32 (over x, y, z_lo).
Axes of the slice: x: 4, y: 4, z: 4 (z_hi: 2, z_lo: 2; z = z_hi * 2 + z_lo), core: 2. Of those that a mesh axis runs over, the one named last changes fastest.
Arguments:
- fields: float32 [2, 3, 128, 32, 512], P(None, None, 'tile', 'role', 'rep'), may hold values from -6 to 6
- material: int32 [128, 32, 512], P('tile', 'role', 'rep'), may hold values from 0 to 3
- permittivity: float32 [4], replicated, may hold values from 1 to 4
- conductivity: float32 [4], replicated, may hold values from 0 to 1
- plan: int32 [4], replicated, may hold values from 1 to 3
- mode_counts: int32 [2, 3], replicated, may hold values from 4 to 8
- lift_weight: float32 [64, 6], replicated, may hold values from -2.5 to 2.5
- pointwise: float32 [2, 64, 64], replicated, may hold values from -0.75 to 0.75
- spectral_weight: float32 [2, 256, 16, 64, 64], P(None, 'tile'), may hold values from -6 to 6
- project_weight: float32 [6, 64], replicated, may hold values from -0.75 to 0.75
Outputs:
- new_fields: float32 [2, 3, 128, 32, 512], P(None, None, 'tile', 'role', 'rep')
- lift_grad: float32 [64, 6], replicated
- pointwise_grad: float32 [2, 64, 64], replicated
- spectral_grad: float32 [2, 256, 16, 64, 64], P(None, 'tile')
- project_grad: float32 [6, 64], replicated
- total_loss: float32 [], replicated
The draws below stay inside these ranges and needn't reach their ends.
All inputs are finite; a program needn't handle non-finite values.
Results may differ from the reference program's by a relative error of at most 0.0003.
Values sent between devices are 32-bit elements; how exact they have to be, the bound alone decides.
No kernel may reach another device: no remote copies, remote signals or barrier semaphores. Data moves between devices by JAX's collectives and lax.ppermute only.
A program may use at most 192 MiB of HBM per device.

```python
import math
import jax
import jax.numpy as jnp
from jax import lax

NY = 32
STEPS = 4
NMAT = 4
C = 64
MODES = 8
LAYERS = 2
NX = 128
NZ = 512
SX = 64
SY = 16
SZ = 256
SAMPLES = 4


def draw_mode_counts(key, part):
    key = jax.random.fold_in(key, 5)
    counts = jax.random.randint(key, (LAYERS, 3), MODES // 2, MODES + 1, dtype=jnp.int32)
    return counts.at[0, 0].set(MODES)


def with_ends(drawn, key, least, high):
    place = [jax.random.randint(jax.random.fold_in(key, axis), (), 0, length) for axis, length in enumerate(drawn.shape)]
    longest = drawn.shape.index(max(drawn.shape))
    neighbour = place[:longest] + [(place[longest] + 1) % drawn.shape[longest]] + place[longest + 1:]
    return drawn.at[tuple(place)].set(least).at[tuple(neighbour)].set(high)


def block_scale(own_key, shape, pieces, low, top_value):
    level, own = 1.0, jax.random.fold_in(own_key, 6)
    for axis_at, parts in pieces:
        heights = jnp.exp(jax.random.uniform(jax.random.fold_in(own, axis_at), (parts,), jnp.float32, low / len(pieces), top_value / len(pieces)))
        level = level * jnp.repeat(heights, shape[axis_at] // parts).reshape([-1 if axis == axis_at else 1 for axis in range(len(shape))])
    return level


def centred(rng, shape, width, limit, cuts=(), held_as=jnp.bfloat16):
    drawn = jax.random.normal(rng, shape, jnp.float32) * width
    if len(cuts) > 0:
        drawn = block_scale(rng, shape, cuts, -0.22, 0.18) * drawn
    return jnp.clip(drawn, min=-limit, max=limit).astype(held_as)


def setup_inputs(seed: int = 0) -> dict:
    splits = jax.random.split(jax.random.key(seed), 11)
    return {
        "fields": centred(splits[0], (2, 3, NX, NY, NZ), 1.0, 6.0, ((2, 32), (3, 2), (4, 2)), jnp.float32),
        "material": with_ends(jax.random.randint(splits[1], (NX, NY, NZ), 0, NMAT), jax.random.fold_in(splits[1], 1), 0, NMAT - 1).astype(jnp.int32),
        "permittivity": jnp.clip(jnp.exp(jax.random.uniform(splits[2], (NMAT,), jnp.float32, math.log(1.0), math.log(4.0))), 1.0, 4.0),
        "conductivity": jnp.clip(jax.random.uniform(splits[3], (NMAT,), jnp.float32, 0.0, 1.0), 0.0, 1.0),
        "plan": with_ends(jax.random.randint(splits[4], (SAMPLES,), 1, STEPS), jax.random.fold_in(splits[4], 1), 1, STEPS - 1).astype(jnp.int32),
        "mode_counts": draw_mode_counts(jax.random.fold_in(splits[10], 71), 0),
        "lift_weight": centred(splits[6], (C, 6), 6 ** -0.5, 2.5, (), jnp.float32),
        "pointwise": centred(splits[7], (LAYERS, C, C), C ** -0.5, 0.75, (), jnp.float32),
        "spectral_weight": centred(splits[8], (LAYERS, 4 * MODES * MODES, 2 * MODES, C, C), (max(1, SX * SY * SZ // (4 * C * (2 * MODES) ** 3)) ** 0.5), 6.0, ((1, 32),), jnp.float32),
        "project_weight": centred(splits[9], (6, C), C ** -0.5, 0.75, (), jnp.float32),
    }


STEP_TIME = 0.5
PRECISE = lax.Precision.HIGHEST

def forward_diff(grid_field, along, border):
    remainder = lax.slice_in_dim(grid_field, 1, grid_field.shape[along], axis=along)
    return jnp.concatenate([remainder, border], axis=along) - grid_field

def backward_diff(grid_field, along, border):
    remainder = lax.slice_in_dim(grid_field, 0, grid_field.shape[along] - 1, axis=along)
    return grid_field - jnp.concatenate([border, remainder], axis=along)

def curl_of(components, x_plane, y_plane, z_plane, difference):
    d_zy = difference(components[2], 1, y_plane[1])
    d_yz = difference(components[1], 2, z_plane[1])
    d_xz = difference(components[0], 2, z_plane[0])
    d_zx = difference(components[2], 0, x_plane[1])
    d_yx = difference(components[1], 0, x_plane[0])
    d_xy = difference(components[0], 1, y_plane[0])
    return jnp.stack([d_zy - d_yz, d_xz - d_zx, d_yx - d_xy])

def coarsen(components):
    a, b, c, d = components.shape
    return components.reshape(a, b // 2, 2, c // 2, 2, d // 2, 2).mean(axis=(2, 4, 6))

def mode_table(number_kept, length):
    frequency = jnp.arange(MODES, dtype=jnp.int32)
    position = jnp.arange(length, dtype=jnp.int32)
    angles = 2.0 * math.pi / length * (frequency[:, None] * position[None, :] % length).astype(jnp.float32)
    retained = (frequency < number_kept).astype(jnp.float32)[:, None] * math.sqrt(2.0 / length)
    return jnp.concatenate([jnp.cos(angles) * retained, jnp.sin(angles) * retained], axis=0)

def spectral_layer(hidden, tables, weights):
    table_x, table_y, table_z = tables
    a = jnp.einsum('cxyz,kz->cxyk', hidden, table_z, precision=PRECISE)
    b = jnp.einsum('cxyk,jy->cxjk', a, table_y, precision=PRECISE)
    b = b.reshape(b.shape[0], b.shape[1], b.shape[2] * b.shape[3])
    coefficients = jnp.einsum('cxm,lx->clm', b, table_x, precision=PRECISE)
    mixed_modes = jnp.einsum('mloi,ilm->olm', weights, coefficients, precision=PRECISE)
    spatial = jnp.einsum('olm,lx->oxm', mixed_modes, table_x, precision=PRECISE)
    k = table_z.shape[0]
    spatial = spatial.reshape(spatial.shape[0], spatial.shape[1], k, k)
    a = jnp.einsum('cxjk,jy->cxyk', spatial, table_y, precision=PRECISE)
    return jnp.einsum('cxyk,kz->cxyz', a, table_z, precision=PRECISE)

def sample_loss(params, inputs, target, tables):
    lift_weight, pointwise, spectral_weight, project_weight = params
    hidden = jnp.einsum('ca,axyz->cxyz', lift_weight, inputs, precision=PRECISE)
    for layer_idx in range(LAYERS):
        pre_act = spectral_layer(hidden, tables[layer_idx], spectral_weight[layer_idx])
        pre_act = pre_act + jnp.einsum('oi,ixyz->oxyz', pointwise[layer_idx], hidden, precision=PRECISE)
        hidden = jax.nn.gelu(pre_act)
    predicted = jnp.einsum('ac,cxyz->axyz', project_weight, hidden, precision=PRECISE)
    errors = predicted - target
    return jnp.sum(errors * errors) / (6.0 * SX * SY * SZ * SAMPLES)

def reference(fields, material, permittivity, conductivity, plan, mode_counts, lift_weight, pointwise, spectral_weight, project_weight):
    permit = permittivity[material]
    conduct = conductivity[material]
    damping = conduct * (0.5 * STEP_TIME) / permit
    keep_e = (1.0 - damping) / (1.0 + damping)
    gain_e = STEP_TIME / (permit * (1.0 + damping))
    electric = fields[0]
    magnetic = fields[1]
    x_zero = jnp.zeros((2, 1, NY, NZ), jnp.float32)
    y_zero = jnp.zeros((2, NX, 1, NZ), jnp.float32)
    z_zero = jnp.zeros((2, NX, NY, 1), jnp.float32)
    history = []
    for step_num in range(STEPS):
        magnetic = magnetic - STEP_TIME * curl_of(electric, x_zero, y_zero, z_zero, forward_diff)
        electric = keep_e * electric + gain_e * curl_of(magnetic, x_zero, y_zero, z_zero, backward_diff)
        history.append(jnp.concatenate([coarsen(electric), coarsen(magnetic)], axis=0))
    target = history[-1]
    earlier = jnp.stack(history[:-1])
    tables = []
    for layer_idx in range(LAYERS):
        tables.append(tuple((mode_table(mode_counts[layer_idx, dim_idx], extent) for dim_idx, extent in enumerate((SX, SY, SZ)))))
    params = (lift_weight, pointwise, spectral_weight, project_weight)
    zero_grads = jax.tree.map(jnp.zeros_like, params)

    def accumulate(running, sample_idx):
        gradients, loss_sum = running
        inputs = lax.dynamic_index_in_dim(earlier, plan[sample_idx] - 1, 0, keepdims=False)

        def one_loss(weights_now):
            return sample_loss(weights_now, inputs, target, tables)
        sample_value, pullback = jax.vjp(one_loss, params)
        grads_now = pullback(jnp.ones_like(sample_value))[0]
        gradients = jax.tree.map(lambda a, b: a + b, gradients, grads_now)
        return ((gradients, loss_sum + sample_value), None)
    start = (zero_grads, jnp.zeros((), jnp.float32))
    (gradients, loss_sum), _ = lax.scan(accumulate, start, jnp.arange(SAMPLES, dtype=jnp.int32))
    new_fields = jnp.stack([electric, magnetic])
    return (new_fields, gradients[0], gradients[1], gradients[2], gradients[3], loss_sum)
```

```python
import functools
import math

import jax
import jax.numpy as jnp
import ml_dtypes
import numpy as np
from jax import lax
from jax.experimental import pallas as pl
from jax.experimental.pallas import tpu as pltpu
from jax.sharding import PartitionSpec as P

STEPS = 4
MODES = 8
LAYERS = 2
STEP_TIME = 0.5
PRECISE = lax.Precision.HIGHEST
F32 = jnp.float32
BF16 = jnp.bfloat16
NN = (((1,), (0,)), ((), ()))
NT = (((1,), (1,)), ((), ()))
TN = (((0,), (0,)), ((), ()))
ROOM = 56 * 1024 * 1024
GROUP = ("role", "rep")
EVERY = ("role", "rep", "tile")
SX, SY, SZ = 64, 16, 256
CELLS = SY * SZ
TILES = 32


def basis(length):
    frequency = np.arange(MODES)[:, None]
    position = np.arange(length)[None, :]
    angles = 2.0 * np.pi * ((frequency * position) % length) / length
    return np.concatenate([np.cos(angles), np.sin(angles)], axis=0) * math.sqrt(2.0 / length)


def split_const(table):
    table = table.astype(np.float32)
    high = table.astype(ml_dtypes.bfloat16)
    low = (table - high.astype(np.float32)).astype(ml_dtypes.bfloat16)
    return high, low


def both_const(table):
    return np.stack(split_const(table))


TABLE_X, TABLE_Y, TABLE_Z = basis(SX), basis(SY), basis(SZ)
KRON_X = both_const(
    np.einsum("ptx,mn->xmptn", TABLE_X.reshape(16, TILES, 2), np.eye(8)).reshape(256, 256)
)
KRON_XT = np.ascontiguousarray(KRON_X.transpose(0, 2, 1))
KRON_Y = both_const(np.einsum("jy,kl->jkyl", TABLE_Y, np.eye(16)).reshape(256, 256))
KRON_YT = np.ascontiguousarray(KRON_Y.transpose(0, 2, 1))
KRON_Y_HALF = np.stack(
    [
        both_const(
            np.einsum("jy,kl->jkyl", TABLE_Y[:, r * 8 : r * 8 + 8], np.eye(16)).reshape(256, 128)
        )
        for r in range(2)
    ]
)
Z_HIGH, Z_LOW = split_const(TABLE_Z)
Z_ROWS = np.concatenate([Z_HIGH, Z_LOW], axis=0)
Z_COLS = np.concatenate([Z_HIGH.T, Z_HIGH.T, Z_LOW.T], axis=1)
Z_HALF = np.stack([Z_ROWS[:, r * 128 : r * 128 + 128] for r in range(2)])
POOL_Z = np.kron(np.eye(128), np.full((2, 1), 0.125)).astype(np.float32)


def halves(value):
    high = value.astype(BF16)
    return high, (value - high.astype(F32)).astype(BF16)


def dot(a, b, dims=NN):
    return lax.dot_general(a, b, dims, preferred_element_type=F32)


def dot3(a, b, dims=NN):
    return dot(a[0], b[0], dims) + dot(a[0], b[1], dims) + dot(a[1], b[0], dims)


def lanes_of(shape):
    return lax.broadcasted_iota(jnp.int32, shape, len(shape) - 1)


def rows_of(shape):
    return lax.broadcasted_iota(jnp.int32, shape, len(shape) - 2)


def square_weight(matrix):
    high, low = halves(matrix)
    one = jnp.concatenate([high, low], axis=1)
    return jnp.concatenate([one, one], axis=0)


def rows_times(value, weight):
    high, low = halves(value)
    out = dot(jnp.concatenate([high, low], axis=1), weight)
    return out[:, :128] + out[:, 128:]


def vmem(shape, dtype=F32):
    return pltpu.VMEM(shape, dtype)


def params():
    return pltpu.CompilerParams(vmem_limit_bytes=ROOM)


def full(shape):
    return pl.BlockSpec(shape, lambda *_: (0,) * len(shape))


SMEM = pl.BlockSpec(memory_space=pltpu.SMEM)


def shape_of(*shape):
    return jax.ShapeDtypeStruct(shape, F32)


def pack_kernel(fields, material, packed, strip, left, right):
    packed[0:6] = fields[...]
    packed[6] = material[...].astype(F32)
    left[...] = jnp.zeros_like(left)
    right[...] = jnp.zeros_like(right)
    left[0:448] = packed[:, :, :, 0:128].reshape(448, 128)
    right[0:448] = packed[:, :, :, 128:256].reshape(448, 128)
    for b in range(4):
        rows = pl.ds(b * 128, 128)
        strip[0:4, rows] = jnp.transpose(left[rows, :])[0:4]
        strip[4:8, rows] = jnp.transpose(right[rows, :])[124:128]


def pack(fields, material):
    return pl.pallas_call(
        pack_kernel,
        out_shape=[shape_of(7, 4, 16, 256), shape_of(8, 512)],
        scratch_shapes=[vmem((512, 128)), vmem((512, 128))],
        compiler_params=params(),
        name="pack",
    )(fields, material)


def leap_kernel(
    place,
    plan,
    coefs,
    own0,
    own1,
    low0,
    low1,
    high0,
    high1,
    strip_own0,
    strip_own1,
    strip_low0,
    strip_low1,
    strip_high0,
    strip_high1,
    pool,
    kron,
    z_half,
    out_fields,
    out_pieces,
    out_coef,
    grid_f,
    keep,
    gain,
    dt_mask,
    edge0,
    edge1,
    sums0,
    sums1,
    reduced,
    chosen,
    staged,
):
    role, rep, tile = place[0], place[1], place[2]
    shape8 = (8, 384)
    row8 = rows_of(shape8)
    top = jnp.where((row8 < 4) & (role == 0), 1.0, 0.0)
    bottom = jnp.where((row8 >= 4) & (role == 1), 1.0, 0.0)

    def column(strip_ref, edge):
        strip = strip_ref[...]
        row = rows_of((8, 512))
        first = jnp.where((row < 4) & (rep == 0), strip, 0.0)
        last = jnp.where((row >= 4) & (rep == 1), strip, 0.0)
        whole = jnp.concatenate([first, jnp.zeros((112, 512), F32), last], axis=0)
        for b in range(4):
            edge[b * 128 : (b + 1) * 128, :] = jnp.transpose(whole[:, b * 128 : (b + 1) * 128])

    sources = (
        (low0, low1, strip_low0, strip_low1),
        (own0, own1, strip_own0, strip_own1),
        (high0, high1, strip_high0, strip_high1),
    )
    for number, (mine, mate, strip_mine, strip_mate) in enumerate(sources):
        column(strip_mine, edge0)
        column(strip_mate, edge1)

        def fill(n, carry, mine=mine, mate=mate, number=number):
            c = n // 4
            i = n % 4
            at = pl.multiple_of(n * 16, 16)
            plane = jnp.concatenate([mine[c, i], edge0[pl.ds(at, 16), :]], axis=1)
            other = jnp.concatenate([mate[c, i], edge1[pl.ds(at, 16), :]], axis=1)
            halo = other[0:8] * top + other[8:16] * bottom
            grid_f[c, 4 * number + i] = jnp.concatenate([plane, halo], axis=0)
            return carry

        lax.fori_loop(0, 28, fill, 0)

    row = rows_of((24, 384))
    lane = lanes_of((24, 384))
    row_ok = (row < 16) | ((row < 20) & (role == 0)) | ((row >= 20) & (role == 1))
    lane_ok = (lane < 256) | ((lane < 320) & (rep == 0)) | ((lane >= 320) & (rep == 1))
    inside = jnp.where(row_ok & lane_ok, 1.0, 0.0)
    dt_mask[...] = inside * STEP_TIME
    below = jnp.where(tile > 0, 1.0, 0.0)
    above = jnp.where(tile < TILES - 1, 1.0, 0.0)

    def media(p, carry):
        kind = grid_f[6, p]
        level = inside * jnp.where(p >= 8, above, 1.0)

        def choose(base):
            return jnp.where(
                kind < 0.5,
                coefs[base],
                jnp.where(
                    kind < 1.5,
                    coefs[base + 1],
                    jnp.where(kind < 2.5, coefs[base + 2], coefs[base + 3]),
                ),
            )

        keep[p] = choose(0)
        gain[p] = choose(4) * level
        return carry

    lax.fori_loop(1, 11, media, 0)

    def back(value, axis):
        return pltpu.roll(value, value.shape[axis] - 1, axis)

    def step_h(p, carry):
        ex, ey, ez = grid_f[0, p], grid_f[1, p], grid_f[2, p]
        s = dt_mask[...] * jnp.where(p < 4, below, 1.0)
        d_zy = back(ez, 0) - ez
        d_yz = back(ey, 1) - ey
        d_xz = back(ex, 1) - ex
        d_zx = grid_f[2, p + 1] - ez
        d_yx = grid_f[1, p + 1] - ey
        d_xy = back(ex, 0) - ex
        grid_f[3, p] = grid_f[3, p] - s * (d_zy - d_yz)
        grid_f[4, p] = grid_f[4, p] - s * (d_xz - d_zx)
        grid_f[5, p] = grid_f[5, p] - s * (d_yx - d_xy)
        return carry

    def step_e(p, carry):
        hx, hy, hz = grid_f[3, p], grid_f[4, p], grid_f[5, p]
        k, g = keep[p], gain[p]
        d_zy = hz - pltpu.roll(hz, 1, 0)
        d_yz = hy - pltpu.roll(hy, 1, 1)
        d_xz = hx - pltpu.roll(hx, 1, 1)
        d_zx = hz - grid_f[5, p - 1]
        d_yx = hy - grid_f[4, p - 1]
        d_xy = hx - pltpu.roll(hx, 1, 0)
        grid_f[0, p] = k * grid_f[0, p] + g * (d_zy - d_yz)
        grid_f[1, p] = k * grid_f[1, p] + g * (d_xz - d_zx)
        grid_f[2, p] = k * grid_f[2, p] + g * (d_yx - d_xy)
        return carry

    sums0[...] = jnp.zeros_like(sums0)
    sums1[...] = jnp.zeros_like(sums1)
    for step in range(STEPS):
        lax.fori_loop(step, 11 - step, step_h, 0)
        lax.fori_loop(1 + step, 11 - step, step_e, 0)
        for x in range(2):
            for c in range(6):
                at = (x * 8 + c) * 16
                pair = grid_f[c, 4 + 2 * x, 0:16, 0:256] + grid_f[c, 5 + 2 * x, 0:16, 0:256]
                sums0[at : at + 16, :] = pair[:, 0:128]
                sums1[at : at + 16, :] = pair[:, 128:256]
        for part, sums in enumerate((sums0, sums1)):
            staged[:, part * 128 : (part + 1) * 128] = (
                sums[pl.ds(0, 128, stride=2), :] + sums[pl.ds(1, 128, stride=2), :]
            )
        reduced[step] = lax.dot_general(
            staged[...], pool[...], NN, precision=PRECISE, preferred_element_type=F32
        )
    for c in range(6):
        out_fields[c] = grid_f[c, 4:8, 0:16, 0:256]

    me = role * 2 + rep
    for d in range(4):
        own = plan[me ^ d] - 1
        out_pieces[d, 0:128] = reduced[own]
        out_pieces[d, 128:256] = reduced[STEPS - 1]
        chosen[d * 128 : (d + 1) * 128] = reduced[plan[d] - 1]
    parts = []
    z_rows = z_half[rep]
    for y in range(8):
        high, low = halves(chosen[pl.ds(y, 64, stride=8), :])
        out = dot(z_rows, high, NT)
        parts.append(out[0:16] + out[16:32] + dot(z_rows[0:16], low, NT))
    mixed = jnp.concatenate(parts, axis=0)
    coef = dot3((kron[role, 0], kron[role, 1]), halves(mixed))
    out_coef[...] = jnp.zeros_like(out_coef)
    for s in range(4):
        out_coef[s, :, 0:16] = coef[:, s * 16 : (s + 1) * 16]


def leapfrog(place, plan, coefs, blocks):
    count = len(blocks)
    return pl.pallas_call(
        leap_kernel,
        out_shape=[shape_of(6, 4, 16, 256), shape_of(4, 256, 128), shape_of(4, 256, 128)],
        in_specs=[SMEM, SMEM, SMEM] + [pl.BlockSpec(memory_space=pltpu.VMEM)] * (count + 3),
        scratch_shapes=[
            vmem((7, 12, 24, 384)),
            vmem((12, 24, 384)),
            vmem((12, 24, 384)),
            vmem((24, 384)),
            vmem((512, 128)),
            vmem((512, 128)),
            vmem((256, 128)),
            vmem((256, 128)),
            vmem((4, 128, 128)),
            vmem((512, 128)),
            vmem((128, 256)),
        ],
        compiler_params=params(),
        name="leapfrog",
    )(place, plan, coefs, *blocks, jnp.asarray(POOL_Z), jnp.asarray(KRON_Y_HALF), jnp.asarray(Z_HALF))


def prep_kernel(place, piece0, piece1, piece2, piece3, weight, out_pre, out_in, out_target):
    me = place[0] * 2 + place[1]
    weights = square_weight(weight[...])
    lane = lanes_of((128, 128))
    for d, piece in enumerate((piece0, piece1, piece2, piece3)):
        source = me ^ d
        role, rep = source // 2, source % 2
        for kind in range(2):
            whole = jnp.concatenate(
                [piece[pl.ds(kind * 128 + y, 16, stride=8), :] for y in range(8)], axis=0
            )
            turned = jnp.transpose(whole)
            for y in range(8):
                at = pl.multiple_of((role * 8 + y) * 256 + rep * 128, 128)
                own = turned if y == 0 else pltpu.roll(turned, 128 - 16 * y, 1)
                own = jnp.where(lane < 16, own, 0.0)
                if kind == 0:
                    out_in[pl.ds(at, 128), :] = own
                    out_pre[pl.ds(at, 128), :] = rows_times(own, weights)
                else:
                    out_target[pl.ds(at, 128), :] = own


def prepare(place, pieces, weight):
    return pl.pallas_call(
        prep_kernel,
        out_shape=[shape_of(CELLS, 128)] * 3,
        in_specs=[SMEM] + [pl.BlockSpec(memory_space=pltpu.VMEM)] * 5,
        compiler_params=params(),
        name="prepare",
    )(place, *pieces, weight)


GELU_A = math.sqrt(2.0 / math.pi)
GELU_B = 0.044715


def gelu_both(value):
    square = value * value
    t = jnp.tanh(GELU_A * value * (1.0 + GELU_B * square))
    half = 0.5 * (1.0 + t)
    slope = half + 0.5 * value * (1.0 - t * t) * (GELU_A * (1.0 + 3.0 * GELU_B * square))
    return value * half, slope


def open_cells(spectrum, kron_t, c_scr):
    c_scr[...] = dot3((kron_t[0], kron_t[1]), halves(spectrum[...]))


def cells_from(c_scr, z_cols, y):
    high, low = halves(c_scr[pl.ds(pl.multiple_of(y * 16, 16), 16), :])
    return dot(z_cols[...], jnp.concatenate([high, low, high], axis=0))


def cells_to(value, z_rows, d_scr, y):
    high, low = halves(value)
    out = dot(z_rows[...], jnp.concatenate([high, low], axis=1))
    d_scr[pl.ds(pl.multiple_of(y * 16, 16), 16), :] = (
        out[0:16, 0:128] + out[0:16, 128:256] + out[16:32, 0:128]
    )


def close_cells(kron, d_scr, out_coef):
    out_coef[...] = dot3((kron[0], kron[1]), halves(d_scr[...]))


BLOCK_Y = 4


def each_y(step, body):
    for n in range(BLOCK_Y):
        body(step * BLOCK_Y + n, pl.ds(n * SZ, SZ))


def cells0_kernel(spectrum, pre, kron, kron_t, z_rows, z_cols, out_coef, out_h, out_slope, c_scr, d_scr):
    step = pl.program_id(0)

    @pl.when(step == 0)
    def _():
        open_cells(spectrum, kron_t, c_scr)

    def body(y, rows):
        hidden, slope = gelu_both(cells_from(c_scr, z_cols, y) + pre[rows, :])
        out_h[rows, :] = hidden
        out_slope[rows, :] = slope
        cells_to(hidden, z_rows, d_scr, y)

    each_y(step, body)

    @pl.when(step == pl.num_programs(0) - 1)
    def _():
        close_cells(kron, d_scr, out_coef)


def cells1_kernel(
    scale,
    spectrum,
    h1,
    target,
    w_point,
    w_proj,
    w_proj_t,
    kron,
    kron_t,
    z_rows,
    z_cols,
    out_coef,
    out_pre,
    out_h,
    out_err,
    out_loss,
    c_scr,
    d_scr,
    wide,
):
    step = pl.program_id(0)

    @pl.when(step == 0)
    def _():
        open_cells(spectrum, kron_t, c_scr)
        wide[0] = square_weight(w_point[...])
        wide[1] = square_weight(w_proj[...])
        wide[2] = square_weight(w_proj_t[...])
        out_loss[...] = jnp.zeros_like(out_loss)

    def body(y, rows):
        value = cells_from(c_scr, z_cols, y) + rows_times(h1[rows, :], wide[0])
        hidden, slope = gelu_both(value)
        err = rows_times(hidden, wide[1]) - target[rows, :]
        out_loss[...] += jnp.sum((err * err).reshape(SZ // 8, 8, 128), axis=0)
        err = err * scale
        grad = rows_times(err, wide[2]) * slope
        out_h[rows, :] = hidden
        out_err[rows, :] = err
        out_pre[rows, :] = grad
        cells_to(grad, z_rows, d_scr, y)

    each_y(step, body)

    @pl.when(step == pl.num_programs(0) - 1)
    def _():
        close_cells(kron, d_scr, out_coef)


def cells2_kernel(
    spectrum, grad1, slope0, w_point, kron, kron_t, z_rows, z_cols, out_coef, out_pre, c_scr, d_scr, wide
):
    step = pl.program_id(0)

    @pl.when(step == 0)
    def _():
        open_cells(spectrum, kron_t, c_scr)
        wide[...] = square_weight(w_point[...])

    def body(y, rows):
        value = cells_from(c_scr, z_cols, y) + rows_times(grad1[rows, :], wide[...])
        grad = value * slope0[rows, :]
        out_pre[rows, :] = grad
        cells_to(grad, z_rows, d_scr, y)

    each_y(step, body)

    @pl.when(step == pl.num_programs(0) - 1)
    def _():
        close_cells(kron, d_scr, out_coef)


def cell_call(kernel, name, spectrum, streams, weights, n_out, loss=False, wide=None):
    block = pl.BlockSpec((BLOCK_Y * SZ, 128), lambda g: (g, 0))
    consts = (KRON_Y, KRON_YT, Z_ROWS, Z_COLS)
    out_shape = [shape_of(256, 128)] + [shape_of(CELLS, 128)] * n_out
    out_specs = [full((256, 128))] + [block] * n_out
    if loss:
        out_shape.append(shape_of(8, 128))
        out_specs.append(full((8, 128)))
    scratch = [vmem((256, 128)), vmem((256, 128))]
    if wide is not None:
        scratch.append(vmem(wide, BF16))
    return pl.pallas_call(
        kernel,
        grid=(SY // BLOCK_Y,),
        out_shape=out_shape,
        in_specs=[full((256, 128))]
        + [block] * len(streams)
        + [full((128, 128))] * len(weights)
        + [full(c.shape) for c in consts],
        out_specs=out_specs,
        scratch_shapes=scratch,
        compiler_params=params(),
        name=name,
    )(spectrum, *streams, *weights, *[jnp.asarray(c) for c in consts])


def pair_up(rows, low_lanes):
    picked = jnp.where(low_lanes, rows[0:128], rows[128:256])
    return picked + pltpu.roll(picked, 64, 1)


def mix_forward(a_scr, b_scr, mask, weights, step):
    at = pl.multiple_of(step * 16, 16)
    own = halves(a_scr[pl.ds(at, 16), 0:64])
    row, lane = rows_of((16, 256)), lanes_of((16, 256))
    total = jnp.zeros((16, 256), F32)
    for q in range(4):
        out = dot3(own, halves(weights[q * 256 : (q + 1) * 256, :]), NT)
        total = total + jnp.where(row == 4 * q + lane // 64, out, 0.0)
    folded = total[:, 0:128] + total[:, 128:256]
    folded = folded + pltpu.roll(folded, 64, 1)
    b_scr[pl.ds(at, 16), :] = folded * mask[pl.ds(at, 16), :]


def mix_backward(g_scr, b_scr, mask, weights, step):
    at = pl.multiple_of(step * 16, 16)
    one = g_scr[pl.ds(at, 16), :]
    wide = jnp.concatenate([one, one], axis=1)
    row, lane = rows_of((16, 256)), lanes_of((16, 256))
    total = jnp.zeros((16, 64), F32)
    for q in range(4):
        own = jnp.where(row == 4 * q + lane // 64, wide, 0.0)
        total = total + dot3(halves(own), halves(weights[q * 256 : (q + 1) * 256, :]))
    masked = total * mask[pl.ds(at, 16), 0:64]
    b_scr[pl.ds(at, 16), 0:64] = masked
    b_scr[pl.ds(at, 16), 64:128] = masked


def close_modes(b_scr, kron_t, out):
    both = b_scr[...]
    low = lanes_of((128, 128)) < 64
    blocks = jnp.concatenate([jnp.where(low, both, 0.0), jnp.where(low, 0.0, both)], axis=0)
    out[...] = dot3((kron_t[0], kron_t[1]), halves(blocks))


def modes_first_kernel(coef, mask, lift, weights, kron, kron_t, out, out_in, out_a, a_scr, b_scr):
    step = pl.program_id(0)

    @pl.when(step == 0)
    def _():
        value = coef[0] + coef[1] + coef[2] + coef[3]
        rows = dot3((kron[0], kron[1]), halves(value))
        picked = jnp.where(lanes_of((128, 128)) < 8, rows[0:128], rows[128:256]) * mask[...]
        out_in[...] = picked
        lifted = dot3(halves(picked), halves(lift[...]))
        a_scr[...] = lifted
        out_a[...] = lifted

    mix_forward(a_scr, b_scr, mask, weights, step)

    @pl.when(step == pl.num_programs(0) - 1)
    def _():
        close_modes(b_scr, kron_t, out)


def modes_forward_kernel(coef, mask, weights, kron, kron_t, out, out_a, a_scr, b_scr):
    step = pl.program_id(0)

    @pl.when(step == 0)
    def _():
        rows = dot3((kron[0], kron[1]), halves(coef[...]))
        a = pair_up(rows, lanes_of((128, 128)) < 64) * mask[...]
        a_scr[...] = a
        out_a[...] = a

    mix_forward(a_scr, b_scr, mask, weights, step)

    @pl.when(step == pl.num_programs(0) - 1)
    def _():
        close_modes(b_scr, kron_t, out)


def modes_backward_kernel(coef, mask, saved, weights, kron, kron_t, out, out_pair, g_scr, b_scr):
    step = pl.program_id(0)

    @pl.when(step == 0)
    def _():
        rows = dot3((kron[0], kron[1]), halves(coef[...]))
        low = lanes_of((128, 128)) < 64
        g = pair_up(rows, low) * mask[...]
        g_scr[...] = g
        out_pair[...] = jnp.where(low, g, saved[...])

    mix_backward(g_scr, b_scr, mask, weights, step)

    @pl.when(step == pl.num_programs(0) - 1)
    def _():
        close_modes(b_scr, kron_t, out)


def modes_last_kernel(
    coef, mask, saved, inputs, point, weights, kron, kron_t, out_late, out_pair, g_scr, b_scr
):
    step = pl.program_id(0)

    @pl.when(step == 0)
    def _():
        rows = dot3((kron[0], kron[1]), halves(coef[...]))
        low = lanes_of((128, 128)) < 64
        g = pair_up(rows, low) * mask[...]
        g_scr[...] = g
        out_pair[...] = jnp.where(low, g, saved[...])

    mix_backward(g_scr, b_scr, mask, weights, step)

    @pl.when(step == pl.num_programs(0) - 1)
    def _():
        turned = jnp.transpose(inputs[...])[0:16]
        lift = dot3(halves(turned), halves(b_scr[...]))
        lift = lift[0:8] + lift[8:16]
        direct = point[0:8, :] + pltpu.roll(point[8:16, :], 64, 1)
        out_late[...] = jnp.where(lanes_of((8, 128)) < 64, lift, pltpu.roll(direct, 64, 1))


def mode_call(kernel, name, layer, smalls, weights, outs):
    consts = (KRON_X, KRON_XT)
    return pl.pallas_call(
        kernel,
        grid=(8,),
        out_shape=[shape_of(*o) for o in outs],
        in_specs=[full(v.shape) for v in smalls]
        + [pl.BlockSpec((None, None, 1024, 64), lambda m: (layer, m, 0, 0))]
        + [full(c.shape) for c in consts],
        out_specs=[full(o) for o in outs],
        scratch_shapes=[vmem((128, 128)), vmem((128, 128))],
        compiler_params=params(),
        name=name,
    )(*smalls, weights, *[jnp.asarray(c) for c in consts])


def outer_kernel(pair0, pair1, pair2, pair3, out):
    blocks = [p[...] for p in (pair0, pair1, pair2, pair3)]
    turned = [jnp.transpose(b)[0:64] for b in blocks]
    for r in range(16):
        total = None
        for b, t in zip(blocks, turned):
            term = t[:, r : r + 1] * b[r : r + 1, 64:128]
            total = term if total is None else total + term
        out[r] = total


def outer_products(pairs):
    block = pl.BlockSpec((None, 16, 128), lambda l, m: (l, m, 0))
    return pl.pallas_call(
        outer_kernel,
        grid=(LAYERS, 8),
        out_shape=shape_of(LAYERS, 8, 16, 64, 64),
        in_specs=[block] * 4,
        out_specs=pl.BlockSpec((None, None, 16, 64, 64), lambda l, m: (l, m, 0, 0, 0)),
        compiler_params=params(),
        name="outer",
    )(*pairs)


def passed(value, axis, by):
    length = lax.axis_size(axis)
    return lax.ppermute(value, axis, [(i, i + by) for i in range(length) if 0 <= i + by < length])


def across(value, axis):
    return lax.ppermute(value, axis, [(0, 1), (1, 0)])


def diagonal(value, by):
    pairs = []
    for q in range(2):
        for t in range(TILES):
            if 0 <= t + by < TILES:
                pairs.append((q * TILES + t, (1 - q) * TILES + t + by))
    return lax.ppermute(value, ("rep", "tile"), pairs)


def xor_group(value, d):
    return lax.ppermute(value, GROUP, [(i, i ^ d) for i in range(4)])


def parity_blocks(matrix):
    zero = jnp.zeros_like(matrix)
    return jnp.concatenate(
        [jnp.concatenate([matrix, zero], axis=1), jnp.concatenate([zero, matrix], axis=1)], axis=0
    )


def mode_masks(mode_counts):
    row = jnp.arange(128, dtype=jnp.int32)
    pair = lax.axis_index("tile") * 8 + row // 16
    masks = []
    for layer in range(LAYERS):
        kept = (
            (row % 8 < mode_counts[layer, 0])
            & (pair // 16 % 8 < mode_counts[layer, 1])
            & (pair % 8 < mode_counts[layer, 2])
        )
        masks.append(jnp.broadcast_to(kept.astype(F32)[:, None], (128, 128)))
    return masks


def local(
    fields,
    material,
    permittivity,
    conductivity,
    plan,
    mode_counts,
    lift_weight,
    pointwise,
    spectral_weight,
    project_weight,
):
    damping = conductivity * (0.5 * STEP_TIME) / permittivity
    coefs = jnp.concatenate(
        [(1.0 - damping) / (1.0 + damping), STEP_TIME / (permittivity * (1.0 + damping))]
    )
    place = jnp.stack([lax.axis_index("role"), lax.axis_index("rep"), lax.axis_index("tile")])
    weights = spectral_weight.reshape(LAYERS, 8, 1024, 64)

    packed, strip = pack(fields.reshape(6, 4, 16, 256), material)
    low0, high0 = passed(packed, "tile", 1), passed(packed, "tile", -1)
    strip_own0 = across(strip, "rep")
    strip_low0, strip_high0 = diagonal(strip, 1), diagonal(strip, -1)
    blocks = []
    for value in (packed, low0, high0, strip_own0, strip_low0, strip_high0):
        blocks += [value, across(value, "role")]
    new_fields, pieces, coef = leapfrog(place, plan, coefs, blocks)

    masks = mode_masks(mode_counts)
    lift8 = jnp.pad(lift_weight.T, ((0, 2), (0, 0)))
    lift16 = jnp.concatenate([lift8, lift8], axis=0)
    lift_pad = jnp.pad(lift16, ((0, 112), (0, 64)))
    first8 = jnp.dot(lift8, pointwise[0].T, precision=PRECISE)
    first = jnp.pad(parity_blocks(first8), ((0, 112), (0, 0)))
    point1 = parity_blocks(pointwise[1])
    proj8 = jnp.pad(project_weight, ((0, 2), (0, 0)))
    proj_t = jnp.pad(parity_blocks(proj8), ((0, 112), (0, 0)))

    coef = lax.all_to_all(coef.reshape(128, 8, 128), EVERY, 0, 0, tiled=True)
    received = [pieces[0]] + [xor_group(pieces[d], d) for d in range(1, 4)]
    pre0, inputs, target = prepare(place, received, first)

    def swap(value):
        value = value.reshape(TILES, 8, 128)
        return lax.all_to_all(value, "tile", 0, 0, tiled=True).reshape(256, 128)

    spectrum, a_in, a0 = mode_call(
        modes_first_kernel,
        "modes_first",
        0,
        (coef.reshape(4, 256, 128), masks[0], lift_pad),
        weights,
        ((256, 128), (128, 128), (128, 128)),
    )
    a0 = jnp.concatenate([a0[:, 0:64], a0[:, 0:64]], axis=1)
    coef, h1, slope0 = cell_call(cells0_kernel, "cells0", swap(spectrum), (pre0,), (), 2)
    spectrum, a1 = mode_call(
        modes_forward_kernel,
        "modes_forward",
        1,
        (swap(coef), masks[1]),
        weights,
        ((256, 128), (128, 128)),
    )
    norm_count = 6.0 * SX * SY * SZ * plan.shape[0]
    coef, grad1, h2, err, loss = cell_call(
        functools.partial(cells1_kernel, 2.0 / norm_count),
        "cells1",
        swap(spectrum),
        (h1, target),
        (point1.T, proj_t.T, proj_t),
        3,
        loss=True,
        wide=(3, 256, 256),
    )
    spectrum, pair1 = mode_call(
        modes_backward_kernel,
        "modes_backward",
        1,
        (swap(coef), masks[1], a1),
        weights,
        ((256, 128), (128, 128)),
    )
    coef, grad0 = cell_call(
        cells2_kernel,
        "cells2",
        swap(spectrum),
        (grad1, slope0),
        (point1,),
        1,
        wide=(256, 256),
    )

    def over_cells(a, b):
        return lax.dot_general(a, b, TN, precision=PRECISE, preferred_element_type=F32)

    point_blocks = over_cells(grad1, h1)
    point_grad1 = point_blocks[0:64, 0:64] + point_blocks[64:128, 64:128]
    proj_blocks = over_cells(err, h2)
    proj_grad = proj_blocks[0:6, 0:64] + proj_blocks[8:14, 64:128]
    point_grad1, proj_grad, loss = lax.psum(
        (point_grad1, proj_grad, jnp.sum(loss) / norm_count), EVERY
    )
    direct = over_cells(inputs, grad0)[0:16]
    late, pair0 = mode_call(
        modes_last_kernel,
        "modes_last",
        0,
        (swap(coef), masks[0], a0, a_in, direct),
        weights,
        ((8, 128), (128, 128)),
    )
    pairs = jnp.stack([pair0, pair1])
    spectral_grad = outer_products([pairs] + [xor_group(pairs, d) for d in range(1, 4)])
    late = lax.all_to_all(jnp.broadcast_to(late, (128, 8, 128)), EVERY, 0, 0, tiled=True)
    late = jnp.sum(late, axis=0)[0:6]
    through, direct = late[:, 0:64], late[:, 64:128]
    lift_grad = (through + jnp.dot(direct, pointwise[0], precision=PRECISE)).T
    point_grad0 = jnp.dot(direct.T, lift_weight.T, precision=PRECISE)
    return (
        new_fields.reshape(2, 3, 4, 16, 256),
        lift_grad,
        jnp.stack([point_grad0, point_grad1]),
        spectral_grad,
        proj_grad,
        loss,
    )


def solution(mesh):
    return jax.shard_map(
        local,
        mesh=mesh,
        in_specs=(
            P(None, None, "tile", "role", "rep"),
            P("tile", "role", "rep"),
            P(),
            P(),
            P(),
            P(),
            P(),
            P(),
            P(None, "tile", None, None, None),
            P(),
        ),
        out_specs=(
            P(None, None, "tile", "role", "rep"),
            P(),
            P(),
            P(None, "tile", None, None, None),
            P(),
            P(),
        ),
        check_vma=False,
    )
```

```python
import functools
import math

import jax
import jax.numpy as jnp
import ml_dtypes
import numpy as np
from jax import lax
from jax.experimental import pallas as pl
from jax.experimental.pallas import tpu as pltpu
from jax.sharding import PartitionSpec as P

STEPS = 4
MODES = 8
LAYERS = 2
STEP_TIME = 0.5
PRECISE = lax.Precision.HIGHEST
F32 = jnp.float32
BF16 = jnp.bfloat16
NN = (((1,), (0,)), ((), ()))
NT = (((1,), (1,)), ((), ()))
TN = (((0,), (0,)), ((), ()))
ROOM = 62 * 1024 * 1024
LEAP_ROOM = 24 * 1024 * 1024
CELL_ROOM = 62 * 1024 * 1024
MODE_ROOM = 62 * 1024 * 1024
GROUP = ("role", "rep")
EVERY = ("role", "rep", "tile")
SX, SY, SZ = 64, 16, 256
CELLS = SY * SZ
TILES = 32


def basis(length):
    frequency = np.arange(MODES)[:, None]
    position = np.arange(length)[None, :]
    angles = 2.0 * np.pi * ((frequency * position) % length) / length
    return np.concatenate([np.cos(angles), np.sin(angles)], axis=0) * math.sqrt(2.0 / length)


def split_const(table):
    table = table.astype(np.float32)
    high = table.astype(ml_dtypes.bfloat16)
    low = (table - high.astype(np.float32)).astype(ml_dtypes.bfloat16)
    return high, low


def both_const(table):
    return np.stack(split_const(table))


TABLE_X, TABLE_Y, TABLE_Z = basis(SX), basis(SY), basis(SZ)
KRON_X = both_const(
    np.einsum("ptx,mn->xmptn", TABLE_X.reshape(16, TILES, 2), np.eye(8)).reshape(256, 256)
)
KRON_XT = np.ascontiguousarray(KRON_X.transpose(0, 2, 1))
KRON_Y = both_const(np.einsum("jy,kl->jkyl", TABLE_Y, np.eye(16)).reshape(256, 256))
KRON_YT = np.ascontiguousarray(KRON_Y.transpose(0, 2, 1))
Z_HIGH, Z_LOW = split_const(TABLE_Z)
Z_ROWS = np.concatenate([Z_HIGH, Z_LOW], axis=0)
Z_COLS = np.concatenate([Z_HIGH.T, Z_HIGH.T, Z_LOW.T], axis=1)
Z_HALF = np.stack([Z_ROWS[:, r * 128 : r * 128 + 128] for r in range(2)])
POOL_Z = np.kron(np.eye(128), np.full((2, 1), 0.125)).astype(np.float32)


def halves(value):
    high = value.astype(BF16)
    return high, (value - high.astype(F32)).astype(BF16)


def dot(a, b, dims=NN):
    return lax.dot_general(a, b, dims, preferred_element_type=F32)


def dot3(a, b, dims=NN):
    return dot(a[0], b[0], dims) + dot(a[0], b[1], dims) + dot(a[1], b[0], dims)


def lanes_of(shape):
    return lax.broadcasted_iota(jnp.int32, shape, len(shape) - 1)


def rows_of(shape):
    return lax.broadcasted_iota(jnp.int32, shape, len(shape) - 2)


def square_weight(matrix):
    high, low = halves(matrix)
    one = jnp.concatenate([high, low], axis=1)
    return jnp.concatenate([one, one], axis=0)


def rows_times(value, weight):
    high, low = halves(value)
    out = dot(jnp.concatenate([high, low], axis=1), weight)
    return out[:, :128] + out[:, 128:]


def vmem(shape, dtype=F32):
    return pltpu.VMEM(shape, dtype)


def params(room=ROOM):
    return pltpu.CompilerParams(vmem_limit_bytes=room)


def full(shape):
    return pl.BlockSpec(shape, lambda *_: (0,) * len(shape))


SMEM = pl.BlockSpec(memory_space=pltpu.SMEM)
ANY = pl.BlockSpec(memory_space=pl.ANY)


def call(kernel, ins, outs, after=(), carry=(), room=ROOM, **options):
    first, last = len(ins) + len(after), len(ins) + len(after) + len(carry)

    def run(*refs):
        rest = refs[last:]
        kernel(*refs[: len(ins)], *rest[: len(outs)], *rest[len(outs) + len(carry) :])

    return pl.pallas_call(
        run,
        out_shape=[o[0] for o in outs] + [jax.ShapeDtypeStruct(c.shape, c.dtype) for c in carry],
        in_specs=[i[1] for i in ins] + [ANY] * (len(after) + len(carry)),
        out_specs=[o[1] for o in outs] + [ANY] * len(carry),
        input_output_aliases={first + n: len(outs) + n for n in range(len(carry))},
        compiler_params=params(room),
        **options,
    )(*[i[0] for i in ins], *after, *carry)


def shape_of(*shape):
    return jax.ShapeDtypeStruct(shape, F32)


def pack_kernel(fields, material, packed, ends, left, right):
    packed[0:6] = fields[...]
    packed[6] = material[...].astype(F32)
    left[...] = jnp.zeros_like(left)
    right[...] = jnp.zeros_like(right)
    left[0:448] = packed[:, :, :, 0:128].reshape(448, 128)
    right[0:448] = packed[:, :, :, 128:256].reshape(448, 128)
    for b in range(4):
        rows = slice(b * 128, (b + 1) * 128)
        first = jnp.transpose(left[rows, :])[0:8]
        last = jnp.transpose(right[rows, :])[120:128]
        ends[:, rows] = jnp.where(rows_of((8, 128)) < 4, first, last)


def pack(fields, material):
    return pl.pallas_call(
        pack_kernel,
        out_shape=[shape_of(7, 4, 16, 256), shape_of(8, 512)],
        scratch_shapes=[vmem((512, 128)), vmem((512, 128))],
        compiler_params=params(),
        name="pack",
    )(fields, material)


def here():
    return lax.axis_index("role"), lax.axis_index("rep"), lax.axis_index("tile")


def leap_kernel(
    plan,
    permittivity,
    conductivity,
    own0,
    own1,
    low0,
    low1,
    high0,
    high1,
    ends_own0,
    ends_own1,
    ends_low0,
    ends_low1,
    ends_high0,
    ends_high1,
    pool,
    out_fields,
    out_pieces,
    grid_f,
    keep,
    gain,
    dt_mask,
    edge0,
    edge1,
    sums0,
    sums1,
    reduced,
    staged,
):
    role, rep, tile = here()
    shape8 = (8, 384)
    row8 = rows_of(shape8)
    top = jnp.where((row8 < 4) & (role == 0), 1.0, 0.0)
    bottom = jnp.where((row8 >= 4) & (role == 1), 1.0, 0.0)

    def column(ends, edge):
        strip = ends[...]
        row = rows_of((8, 512))
        first = jnp.where((row < 4) & (rep == 0), strip, 0.0)
        last = jnp.where((row >= 4) & (rep == 1), strip, 0.0)
        whole = jnp.concatenate([first, jnp.zeros((112, 512), F32), last], axis=0)
        for b in range(4):
            edge[b * 128 : (b + 1) * 128, :] = jnp.transpose(whole[:, b * 128 : (b + 1) * 128])

    sources = (
        (low0, low1, ends_low0, ends_low1),
        (own0, own1, ends_own0, ends_own1),
        (high0, high1, ends_high0, ends_high1),
    )
    for number, (mine, mate, ends_mine, ends_mate) in enumerate(sources):
        column(ends_mine, edge0)
        column(ends_mate, edge1)

        def fill(n, carry, mine=mine, mate=mate, number=number):
            c = n // 4
            i = n % 4
            at = pl.multiple_of(n * 16, 16)
            plane = jnp.concatenate([mine[c, i], edge0[pl.ds(at, 16), :]], axis=1)
            other = jnp.concatenate([mate[c, i], edge1[pl.ds(at, 16), :]], axis=1)
            halo = other[0:8] * top + other[8:16] * bottom
            grid_f[c, 4 * number + i] = jnp.concatenate([plane, halo], axis=0)
            return carry

        lax.fori_loop(0, 28, fill, 0, unroll=4)

    row = rows_of((24, 384))
    lane = lanes_of((24, 384))
    row_ok = (row < 16) | ((row < 20) & (role == 0)) | ((row >= 20) & (role == 1))
    lane_ok = (lane < 256) | ((lane < 320) & (rep == 0)) | ((lane >= 320) & (rep == 1))
    inside = jnp.where(row_ok & lane_ok, 1.0, 0.0)
    dt_mask[...] = inside * STEP_TIME
    below = jnp.where(tile > 0, 1.0, 0.0)
    above = jnp.where(tile < TILES - 1, 1.0, 0.0)

    def media(p, carry):
        kind = grid_f[6, p]
        level = inside * jnp.where(p >= 8, above, 1.0)

        def choose(values):
            return jnp.where(
                kind < 0.5,
                values[0],
                jnp.where(kind < 1.5, values[1], jnp.where(kind < 2.5, values[2], values[3])),
            )

        permit = choose(permittivity)
        damping = choose(conductivity) * (0.5 * STEP_TIME) / permit
        keep[p] = (1.0 - damping) / (1.0 + damping)
        gain[p] = STEP_TIME / (permit * (1.0 + damping)) * level
        return carry

    lax.fori_loop(1, 11, media, 0, unroll=2)

    def back(value, axis):
        return pltpu.roll(value, value.shape[axis] - 1, axis)

    def step_h(p, carry):
        ex, ey, ez = grid_f[0, p], grid_f[1, p], grid_f[2, p]
        s = dt_mask[...] * below if p < 4 else dt_mask[...]
        d_zy = back(ez, 0) - ez
        d_yz = back(ey, 1) - ey
        d_xz = back(ex, 1) - ex
        d_zx = grid_f[2, p + 1] - ez
        d_yx = grid_f[1, p + 1] - ey
        d_xy = back(ex, 0) - ex
        grid_f[3, p] = grid_f[3, p] - s * (d_zy - d_yz)
        grid_f[4, p] = grid_f[4, p] - s * (d_xz - d_zx)
        grid_f[5, p] = grid_f[5, p] - s * (d_yx - d_xy)
        return carry

    def step_e(p, carry):
        hx, hy, hz = grid_f[3, p], grid_f[4, p], grid_f[5, p]
        k, g = keep[p], gain[p]
        d_zy = hz - pltpu.roll(hz, 1, 0)
        d_yz = hy - pltpu.roll(hy, 1, 1)
        d_xz = hx - pltpu.roll(hx, 1, 1)
        d_zx = hz - grid_f[5, p - 1]
        d_yx = hy - grid_f[4, p - 1]
        d_xy = hx - pltpu.roll(hx, 1, 0)
        grid_f[0, p] = k * grid_f[0, p] + g * (d_zy - d_yz)
        grid_f[1, p] = k * grid_f[1, p] + g * (d_xz - d_zx)
        grid_f[2, p] = k * grid_f[2, p] + g * (d_yx - d_xy)
        return carry

    sums0[...] = jnp.zeros_like(sums0)
    sums1[...] = jnp.zeros_like(sums1)
    for step in range(STEPS):
        for p in range(step, 11 - step):
            step_h(p, 0)
        for p in range(1 + step, 11 - step):
            step_e(p, 0)
        for x in range(2):
            for c in range(6):
                at = (x * 8 + c) * 16
                pair = grid_f[c, 4 + 2 * x, 0:16, 0:256] + grid_f[c, 5 + 2 * x, 0:16, 0:256]
                sums0[at : at + 16, :] = pair[:, 0:128]
                sums1[at : at + 16, :] = pair[:, 128:256]
        for part, sums in enumerate((sums0, sums1)):
            staged[:, part * 128 : (part + 1) * 128] = (
                sums[pl.ds(0, 128, stride=2), :] + sums[pl.ds(1, 128, stride=2), :]
            )
        reduced[step] = lax.dot_general(
            staged[...], pool[...], NN, precision=PRECISE, preferred_element_type=F32
        )
    for c in range(6):
        out_fields[c] = grid_f[c, 4:8, 0:16, 0:256]

    me = role * 2 + rep
    for d in range(4):
        out_pieces[d, 0:128] = reduced[plan[me ^ d] - 1]
        out_pieces[d, 128:256] = reduced[STEPS - 1]


def leapfrog(plan, permittivity, conductivity, blocks):
    whole = pl.BlockSpec(memory_space=pltpu.VMEM)
    return call(
        leap_kernel,
        [(v, SMEM) for v in (plan, permittivity, conductivity)]
        + [(v, whole) for v in (*blocks, jnp.asarray(POOL_Z))],
        [
            (shape_of(6, 4, 16, 256), whole),
            (shape_of(4, 256, 128), whole),
        ],
        room=LEAP_ROOM,
        scratch_shapes=[
            vmem((7, 12, 24, 384)),
            vmem((12, 24, 384)),
            vmem((12, 24, 384)),
            vmem((24, 384)),
            vmem((512, 128)),
            vmem((512, 128)),
            vmem((256, 128)),
            vmem((256, 128)),
            vmem((4, 128, 128)),
            vmem((128, 256)),
        ],
        name="leapfrog",
    )


def fold(value):
    return value[:, 0:128] + value[:, 128:256]


def coef_kernel(piece0, piece1, piece2, piece3, z_half, kron, out, d_scr):
    role, rep, _ = here()
    lane = lanes_of((16, 128))
    for flip, (one, other) in enumerate(((piece0, piece1), (piece2, piece3))):
        total = jnp.zeros((16, 128), F32)
        for z_rows, piece in ((z_half[rep], one), (z_half[1 - rep], other)):
            high, low = halves(
                jnp.concatenate([piece[pl.ds(y, 16, stride=8), :] for y in range(8)], axis=0)
            )
            out_high = dot(z_rows, high, NT)
            total = total + out_high[0:16] + out_high[16:32] + dot(z_rows[0:16], low, NT)
        for y in range(8):
            own = total if y == 0 else pltpu.roll(total, 128 - 16 * y, 1)
            at = pl.multiple_of(((role ^ flip) * 8 + y) * 16, 16)
            d_scr[pl.ds(at, 16), :] = jnp.where(lane < 16, own, 0.0)
    out[...] = dot3((kron[0], kron[1]), halves(d_scr[...]))


def input_coefs(pieces):
    return pl.pallas_call(
        coef_kernel,
        out_shape=shape_of(256, 128),
        scratch_shapes=[vmem((256, 128))],
        compiler_params=params(),
        name="input_coefs",
    )(*pieces, jnp.asarray(Z_HALF), jnp.asarray(KRON_Y))


def prep_kernel(first_row, piece0, piece1, piece2, piece3, weight, out_own, out_mixed):
    role_here, rep_here, _ = here()
    me = role_here * 2 + rep_here
    wide = square_weight(weight[...])
    lane = lanes_of((128, 128))
    for d, piece in enumerate((piece0, piece1, piece2, piece3)):
        source = me ^ d
        role, rep = source // 2, source % 2
        whole = jnp.concatenate(
            [piece[pl.ds(first_row + y, 16, stride=8), :] for y in range(8)], axis=0
        )
        turned = jnp.transpose(whole)
        for y in range(8):
            rows = pl.ds(pl.multiple_of((role * 8 + y) * 256 + rep * 128, 128), 128)
            own = turned if y == 0 else pltpu.roll(turned, 128 - 16 * y, 1)
            own = jnp.where(lane < 16, own, 0.0)
            sides = jnp.concatenate(halves(own), axis=1)
            out_own[rows, :] = sides if out_own.dtype == BF16 else own
            out_mixed[rows, :] = fold(dot(sides, wide))


def prepare(pieces, first_row, weight, as_sides, name):
    own = jax.ShapeDtypeStruct((CELLS, 256), BF16) if as_sides else shape_of(CELLS, 128)
    return pl.pallas_call(
        functools.partial(prep_kernel, first_row),
        out_shape=[own, shape_of(CELLS, 128)],
        compiler_params=params(),
        name=name,
    )(*pieces, weight)


GELU_A = math.sqrt(2.0 / math.pi)
GELU_B = 0.044715


def gelu_both(value):
    square = value * value
    t = jnp.tanh(value * (GELU_A + (GELU_A * GELU_B) * square))
    half = 0.5 + 0.5 * t
    hidden = value * half
    slope = half + hidden * (1.0 - half) * (2.0 * GELU_A + (6.0 * GELU_A * GELU_B) * square)
    return hidden, slope


BLOCK_Y = 4
BLOCK = BLOCK_Y * SZ
CHUNK = 128


def open_cells(spectrum, kron_t, c_scr):
    high, low = halves(dot3((kron_t[0], kron_t[1]), halves(spectrum[...])))
    for y in range(SY):
        lanes = slice(y % BLOCK_Y * 128, y % BLOCK_Y * 128 + 128)
        rows = slice(y * 16, y * 16 + 16)
        c_scr[y // BLOCK_Y, 0:16, lanes] = high[rows]
        c_scr[y // BLOCK_Y, 16:32, lanes] = low[rows]
        c_scr[y // BLOCK_Y, 32:48, lanes] = high[rows]


def chunk_of(wide, n):
    at = n * CHUNK
    return wide[at % SZ : at % SZ + CHUNK, at // SZ * 128 : at // SZ * 128 + 128]


def store_sides(out, rows, value):
    high, low = halves(value)
    out[rows, 0:128] = high
    out[rows, 128:256] = low


def cells_to(sides, z_rows, d_scr, step):
    for n in range(BLOCK_Y):
        out = dot(z_rows[...], sides[n * SZ : (n + 1) * SZ, :])
        at = pl.multiple_of((step * BLOCK_Y + n) * 16, 16)
        d_scr[pl.ds(at, 16), :] = out[0:16, 0:128] + out[0:16, 128:256] + out[16:32, 0:128]


def close_cells(kron, d_scr):
    return dot3((kron[0], kron[1]), halves(d_scr[...]))


def cells0_kernel(spectrum, pre, kron, kron_t, z_rows, z_cols, out_coef, out_h, out_slope, c_scr, d_scr):
    step = pl.program_id(0)

    @pl.when(step == 0)
    def _():
        open_cells(spectrum, kron_t, c_scr)

    spectral = dot(z_cols[...], c_scr[step])
    for n in range(BLOCK // CHUNK):
        rows = slice(n * CHUNK, (n + 1) * CHUNK)
        hidden, slope = gelu_both(chunk_of(spectral, n) + pre[rows, :])
        out_slope[rows, :] = slope
        store_sides(out_h, rows, hidden)
    cells_to(out_h, z_rows, d_scr, step)

    @pl.when(step == pl.num_programs(0) - 1)
    def _():
        out_coef[...] = close_cells(kron, d_scr)


def cells1_kernel(
    spectrum,
    h1,
    pull,
    w_point,
    w_square,
    kron,
    kron_t,
    z_rows,
    z_cols,
    out_coef,
    out_pre,
    out_h,
    c_scr,
    d_scr,
    wide,
    slopes,
):
    step = pl.program_id(0)

    @pl.when(step == 0)
    def _():
        open_cells(spectrum, kron_t, c_scr)
        wide[0] = square_weight(w_point[...])
        wide[1] = square_weight(w_square[...])

    spectral = dot(z_cols[...], c_scr[step])
    direct = dot(h1[...], wide[0])
    for n in range(BLOCK // CHUNK):
        rows = slice(n * CHUNK, (n + 1) * CHUNK)
        hidden, slope = gelu_both(chunk_of(spectral, n) + fold(direct[rows, :]))
        slopes[rows, :] = slope
        store_sides(out_h, rows, hidden)
    back = dot(out_h[...], wide[1])
    for n in range(BLOCK // CHUNK):
        rows = slice(n * CHUNK, (n + 1) * CHUNK)
        store_sides(out_pre, rows, (fold(back[rows, :]) - pull[rows, :]) * slopes[rows, :])
    cells_to(out_pre, z_rows, d_scr, step)

    @pl.when(step == pl.num_programs(0) - 1)
    def _():
        out_coef[...] = close_cells(kron, d_scr)


def cells2_kernel(
    spectrum,
    extra,
    grad1,
    slope0,
    w_point,
    kron,
    kron_t,
    z_rows,
    z_cols,
    out_coef,
    out_pre,
    c_scr,
    d_scr,
    wide,
):
    step = pl.program_id(0)

    @pl.when(step == 0)
    def _():
        open_cells(spectrum, kron_t, c_scr)
        wide[...] = square_weight(w_point[...])

    spectral = dot(z_cols[...], c_scr[step])
    direct = dot(grad1[...], wide[...])
    for n in range(BLOCK // CHUNK):
        rows = slice(n * CHUNK, (n + 1) * CHUNK)
        store_sides(
            out_pre, rows, (chunk_of(spectral, n) + fold(direct[rows, :])) * slope0[rows, :]
        )
    cells_to(out_pre, z_rows, d_scr, step)

    @pl.when(step == pl.num_programs(0) - 1)
    def _():
        out_coef[:, 0:8, :] = close_cells(kron, d_scr).reshape(TILES, 8, 128)
        out_coef[:, 8:16, :] = extra[...]


def cell_call(kernel, name, firsts, streams, weights, outs, scratch=(), coef=(256, 128), **order):
    def block(lanes):
        return pl.BlockSpec((BLOCK, lanes), lambda g: (g, 0))

    consts = [jnp.asarray(c) for c in (KRON_Y, KRON_YT, Z_ROWS, Z_COLS)]
    return call(
        kernel,
        [(v, full(v.shape)) for v in firsts]
        + [(v, block(v.shape[1])) for v in streams]
        + [(v, full(v.shape)) for v in (*weights, *consts)],
        [(shape_of(*coef), full(coef))]
        + [(jax.ShapeDtypeStruct((CELLS, lanes), kind), block(lanes)) for lanes, kind in outs],
        grid=(SY // BLOCK_Y,),
        scratch_shapes=[vmem((4, 48, 512), BF16), vmem((256, 128))] + list(scratch),
        name=name,
        room=CELL_ROOM,
        **order,
    )


def grads_kernel(scale, norm, grad, h1, h2, target, w_proj, out, point_acc, proj_acc, loss_acc, wide, row):
    step = pl.program_id(0)

    @pl.when(step == 0)
    def _():
        wide[...] = square_weight(w_proj[...])
        loss_acc[...] = jnp.zeros_like(loss_acc)

    point_acc[step] = dot(grad[...], h1[...], TN)
    err = fold(dot(h2[...], wide[...])) - target[...]
    loss_acc[...] += jnp.sum((err * err).reshape(BLOCK // 8, 8, 128), axis=0)
    sides = jnp.concatenate(halves(err * scale), axis=1)
    proj_acc[step] = dot(sides, h2[...], TN)

    @pl.when(step == pl.num_programs(0) - 1)
    def _():
        out[...] = jnp.zeros_like(out)
        point = sum(point_acc[n, 0:128, :] + point_acc[n, 128:256, :] for n in range(SY // BLOCK_Y))
        point = fold(point)
        picked = jnp.where(lanes_of((64, 128)) < 64, point[0:64], point[64:128])
        picked = picked + pltpu.roll(picked, 64, 1)
        out[:, 0, :] = jnp.where(lanes_of((32, 128)) < 64, picked[0:32], picked[32:64])
        proj = sum(proj_acc[n, 0:16, :] + proj_acc[n, 128:144, :] for n in range(SY // BLOCK_Y))
        proj = fold(proj)
        picked = jnp.where(lanes_of((8, 128)) < 64, proj[0:8], proj[8:16])
        turned = jnp.transpose(picked + pltpu.roll(picked, 64, 1))
        row[...] = jnp.full((32, 128), jnp.sum(loss_acc[...]) / norm)
        row[:, 0:8] = turned[0:32]
        row[:, 8:16] = turned[32:64]
        out[:, 1, :] = row[...]


def grads(norm, grad, h1, h2, target, w_proj):
    sides = pl.BlockSpec((BLOCK, 256), lambda g: (g, 0))
    return pl.pallas_call(
        functools.partial(grads_kernel, 2.0 / norm, norm),
        grid=(SY // BLOCK_Y,),
        out_shape=shape_of(TILES, 8, 128),
        in_specs=[sides, sides, sides, pl.BlockSpec((BLOCK, 128), lambda g: (g, 0)), full((128, 128))],
        out_specs=full((TILES, 8, 128)),
        scratch_shapes=[
            vmem((SY // BLOCK_Y, 256, 256)),
            vmem((SY // BLOCK_Y, 256, 256)),
            vmem((8, 128)),
            vmem((256, 256), BF16),
            vmem((32, 128)),
        ],
        compiler_params=params(),
        name="grads",
    )(grad, h1, h2, target, w_proj)


def kept_modes(counts, layer):
    row = rows_of((128, 128))
    pair = lax.axis_index("tile") * 8 + row // 16
    kept = (
        (row % 8 < counts[layer, 0])
        & (pair // 16 % 8 < counts[layer, 1])
        & (pair % 8 < counts[layer, 2])
    )
    return jnp.where(kept, 1.0, 0.0)


def pair_up(rows, low_lanes):
    picked = jnp.where(low_lanes, rows[0:128], rows[128:256])
    return picked + pltpu.roll(picked, 64, 1)


MIX_STEPS = 2
MIX_PAIRS = 8 // MIX_STEPS


def mix(g_scr, b_scr, weights, step, turned):
    row, lane = rows_of((16, 256)), lanes_of((16, 256))
    wanted = (lanes_of((16, 128)) >= 64) if turned else (lanes_of((16, 128)) < 64)
    for n in range(MIX_PAIRS):
        at = pl.multiple_of((step * MIX_PAIRS + n) * 16, 16)
        one = g_scr[pl.ds(at, 16), :]
        wide = jnp.concatenate([one, one], axis=1)
        total = jnp.zeros((32, 256), F32)
        for q in range(4):
            own = jnp.where(row == 4 * q + lane // 64, wide, 0.0)
            sides = jnp.concatenate(halves(own), axis=0)
            both = halves(weights[n, q * 256 : (q + 1) * 256, :])
            total = total + dot(sides, jnp.concatenate(both, axis=1))
        folded = fold(total[0:16]) + total[16:32, 0:128]
        folded = jnp.where(wanted, folded, 0.0)
        b_scr[pl.ds(at, 16), :] = folded + pltpu.roll(folded, 64, 1)


def close_modes(b_scr, kept, kron_t, out):
    both = b_scr[...] * kept
    low = lanes_of((128, 128)) < 64
    blocks = jnp.concatenate([jnp.where(low, both, 0.0), jnp.where(low, 0.0, both)], axis=0)
    out[...] = dot3((kron_t[0], kron_t[1]), halves(blocks))


def modes_first_kernel(counts, coef, lift, weights, kron, kron_t, out, out_in, out_a, a_scr, b_scr):
    step = pl.program_id(0)

    @pl.when(step == 0)
    def _():
        rows = dot3((kron[0], kron[1]), halves(coef[...]))
        picked = jnp.where(lanes_of((128, 128)) < 8, rows[0:128], rows[128:256])
        picked = picked * kept_modes(counts, 0)
        out_in[...] = picked
        lifted = dot3(halves(picked), halves(lift[...]))
        a_scr[...] = lifted
        out_a[...] = lifted

    mix(a_scr, b_scr, weights, step, True)

    @pl.when(step == pl.num_programs(0) - 1)
    def _():
        close_modes(b_scr, kept_modes(counts, 0), kron_t, out)


def modes_forward_kernel(counts, coef, weights, kron, kron_t, out, out_a, a_scr, b_scr):
    step = pl.program_id(0)

    @pl.when(step == 0)
    def _():
        rows = dot3((kron[0], kron[1]), halves(coef[...]))
        a = pair_up(rows, lanes_of((128, 128)) < 64) * kept_modes(counts, 1)
        a_scr[...] = a
        out_a[...] = a

    mix(a_scr, b_scr, weights, step, True)

    @pl.when(step == pl.num_programs(0) - 1)
    def _():
        close_modes(b_scr, kept_modes(counts, 1), kron_t, out)


def take_gradient(rows, kept, saved, g_scr, out_pair):
    low = lanes_of((128, 128)) < 64
    g = pair_up(rows, low) * kept
    g_scr[...] = g
    out_pair[...] = jnp.where(low, g, saved[...])


def modes_backward_kernel(
    counts, coef, saved, weights, kron, kron_t, out, out_pair, g_scr, b_scr
):
    step = pl.program_id(0)

    @pl.when(step == 0)
    def _():
        rows = dot3((kron[0], kron[1]), halves(coef[...]))
        take_gradient(rows, kept_modes(counts, 1), saved, g_scr, out_pair)

    mix(g_scr, b_scr, weights, step, False)

    @pl.when(step == pl.num_programs(0) - 1)
    def _():
        close_modes(b_scr, kept_modes(counts, 1), kron_t, out)


def modes_last_kernel(counts, coef, saved, inputs, point, weights, kron, kron_t, out, g_scr, b_scr):
    step = pl.program_id(0)

    @pl.when(step == 0)
    def _():
        value = coef[:, 0:8, :].reshape(256, 128)
        rows = dot3((kron[0], kron[1]), halves(value))
        take_gradient(rows, kept_modes(counts, 0), saved, g_scr, out.at[0:128])

    mix(g_scr, b_scr, weights, step, False)

    @pl.when(step == pl.num_programs(0) - 1)
    def _():
        turned = jnp.transpose(inputs[...])[0:16]
        lift = dot3(halves(turned), halves(b_scr[...]))
        lift = lift[0:8] + lift[8:16]
        direct = fold(point[0:16, :] + point[128:144, :])
        direct = direct[0:8] + pltpu.roll(direct[8:16], 64, 1)
        late = jnp.where(lanes_of((8, 128)) < 64, lift, pltpu.roll(direct, 64, 1))
        extra = pltpu.roll(jnp.sum(coef[:, 8:16, :], axis=0), 6, 0)
        out[128:136] = jnp.where(rows_of((8, 128)) < 6, late, extra)


def mode_call(kernel, name, layer, counts, smalls, weights, outs, **order):
    consts = [jnp.asarray(c) for c in (KRON_X, KRON_XT)]
    return call(
        kernel,
        [(counts, SMEM)]
        + [(v, full(v.shape)) for v in smalls]
        + [(weights, pl.BlockSpec((None, MIX_PAIRS, 1024, 128), lambda m: (layer, m, 0, 0)))]
        + [(v, full(v.shape)) for v in consts],
        [(shape_of(*o), full(o)) for o in outs],
        grid=(MIX_STEPS,),
        scratch_shapes=[vmem((128, 128)), vmem((128, 128))],
        name=name,
        room=MODE_ROOM,
        **order,
    )


OUTER_PAIRS = 4


def outer_kernel(*refs):
    layer = pl.program_id(0)
    out = refs[8]
    row, lane = rows_of((64, 1024)), lanes_of((64, 1024))
    own = row % 16 == lane // 64
    low = lanes_of((64, 128)) < 64
    for n in range(OUTER_PAIRS):
        rows = slice(n * 16, (n + 1) * 16)
        block = jnp.concatenate(
            [jnp.where(layer == 0, refs[d][rows, :], refs[4 + d][rows, :]) for d in range(4)],
            axis=0,
        )
        grads = halves(jnp.transpose(block)[0:64])
        twice = jnp.where(low, pltpu.roll(block, 64, 1), block)
        spread = halves(jnp.where(own, jnp.concatenate([twice] * 8, axis=1), 0.0))
        result = dot3(grads, spread)
        for r in range(16):
            out[n, r] = result[:, r * 64 : (r + 1) * 64]


def outer_products(pairs0, pairs1):
    block = pl.BlockSpec((OUTER_PAIRS * 16, 128), lambda l, m: (m, 0))
    return pl.pallas_call(
        outer_kernel,
        grid=(LAYERS, 8 // OUTER_PAIRS),
        out_shape=shape_of(LAYERS, 8, 16, 64, 64),
        in_specs=[block] * 8,
        out_specs=pl.BlockSpec((None, OUTER_PAIRS, 16, 64, 64), lambda l, m: (l, m, 0, 0, 0)),
        compiler_params=params(),
        name="outer",
    )(*pairs0, *pairs1)


def finish_kernel(late, point, lift, out_lift, out_point, out_proj, out_loss):
    by_tile = late[...]
    total = jnp.sum(by_tile, axis=0)
    total = jnp.where(rows_of((8, 128)) < 6, total, 0.0)
    through, direct = total[:, 0:64], pltpu.roll(total, 64, 1)[:, 0:64]

    def exact(a, b, dims):
        return lax.dot_general(a, b, dims, precision=PRECISE, preferred_element_type=F32)

    out_point[0] = exact(direct, lift[...], TN)
    through = through + exact(direct, point[...], NN)
    out_lift[...] = through[0:6]
    first = by_tile[:, 6, :]
    out_point[1, 0:32, :] = first[:, 0:64]
    out_point[1, 32:64, :] = first[:, 64:128]
    second = jnp.transpose(by_tile[:, 7, :])
    out_proj[:, 0:32] = second[0:6]
    out_proj[:, 32:64] = second[8:14]
    out_loss[...] = second[16:17, 0:1]


def finish(late, point, lift):
    return pl.pallas_call(
        finish_kernel,
        out_shape=[shape_of(6, 64), shape_of(2, 64, 64), shape_of(6, 64), shape_of(1, 1)],
        compiler_params=params(),
        name="finish",
    )(late, point, lift)


def passed(value, axis, by):
    length = lax.axis_size(axis)
    return lax.ppermute(value, axis, [(i, i + by) for i in range(length) if 0 <= i + by < length])


def across(value, axis):
    return lax.ppermute(value, axis, [(0, 1), (1, 0)])


def diagonal(value, by):
    pairs = []
    for q in range(2):
        for t in range(TILES):
            if 0 <= t + by < TILES:
                pairs.append((q * TILES + t, (1 - q) * TILES + t + by))
    return lax.ppermute(value, ("rep", "tile"), pairs)


def xor_group(value, d):
    return lax.ppermute(value, GROUP, [(i, i ^ d) for i in range(4)])


def parity_blocks(matrix):
    zero = jnp.zeros_like(matrix)
    return jnp.concatenate(
        [jnp.concatenate([matrix, zero], axis=1), jnp.concatenate([zero, matrix], axis=1)], axis=0
    )


def local(
    fields,
    material,
    permittivity,
    conductivity,
    plan,
    mode_counts,
    lift_weight,
    pointwise,
    spectral_weight,
    project_weight,
):
    weights = jnp.concatenate([spectral_weight, jnp.swapaxes(spectral_weight, -1, -2)], axis=-1)
    weights = weights.reshape(LAYERS, 8, 1024, 128)

    own0, ends_own0 = pack(fields.reshape(6, 4, 16, 256), material)
    low0, high0 = passed(own0, "tile", 1), passed(own0, "tile", -1)
    ends = (xor_group(ends_own0, 1), diagonal(ends_own0, 1), diagonal(ends_own0, -1))
    blocks = []
    for value in (own0, low0, high0, *ends):
        blocks += [value, across(value, "role")]
    new_fields, pieces = leapfrog(plan, permittivity, conductivity, blocks)
    pieces = [pieces[0]] + [xor_group(pieces[d], d) for d in range(1, 4)]
    coef = input_coefs(pieces)

    lift8 = jnp.pad(lift_weight.T, ((0, 2), (0, 0)))
    lift16 = jnp.concatenate([lift8, lift8], axis=0)
    lift_pad = jnp.pad(jnp.concatenate([lift16, lift16], axis=1), ((0, 112), (0, 0)))
    first8 = jnp.dot(lift8, pointwise[0].T, precision=PRECISE)
    first = jnp.pad(parity_blocks(first8), ((0, 112), (0, 0)))
    point1 = parity_blocks(pointwise[1])
    proj8 = jnp.pad(project_weight, ((0, 2), (0, 0)))
    proj_t = jnp.pad(parity_blocks(proj8), ((0, 112), (0, 0)))
    norm_count = 6.0 * SX * SY * SZ * plan.shape[0]
    scale = 2.0 / norm_count
    proj_square = jnp.dot(project_weight.T, project_weight, precision=PRECISE) * scale

    def swap(value):
        value = value.reshape(TILES, -1, 128)
        return lax.all_to_all(value, "tile", 0, 0, tiled=True)

    def swap_flat(value):
        return swap(value).reshape(256, 128)

    inputs, pre0 = prepare(pieces, 0, first, True, "prepare_inputs")
    spectrum, a_in, a0 = mode_call(
        modes_first_kernel,
        "modes_first",
        0,
        mode_counts,
        (swap_flat(coef), lift_pad),
        weights,
        ((256, 128), (128, 128), (128, 128)),
        after=(pre0,),
    )
    target, pull = prepare(pieces, 128, proj_t * scale, False, "prepare_target")
    sides, plain_out = (256, BF16), (128, F32)
    coef, h1, slope0 = cell_call(
        cells0_kernel,
        "cells0",
        (swap_flat(spectrum),),
        (pre0,),
        (),
        (sides, plain_out),
        after=(pull,),
    )
    spectrum, a1 = mode_call(
        modes_forward_kernel,
        "modes_forward",
        1,
        mode_counts,
        (swap_flat(coef),),
        weights,
        ((256, 128), (128, 128)),
    )
    coef, grad1, h2 = cell_call(
        cells1_kernel,
        "cells1",
        (swap_flat(spectrum),),
        (h1, pull),
        (point1.T, parity_blocks(proj_square)),
        (sides, sides),
        scratch=(vmem((2, 256, 256), BF16), vmem((BLOCK, 128))),
    )
    extra = grads(norm_count, grad1, h1, h2, target, proj_t.T)
    spectrum, pair1 = mode_call(
        modes_backward_kernel,
        "modes_backward",
        1,
        mode_counts,
        (swap_flat(coef), a1),
        weights,
        ((256, 128), (128, 128)),
        after=(extra,),
    )
    pairs = [pair1] + [xor_group(pair1, d) for d in range(1, 4)]
    coef, grad0 = cell_call(
        cells2_kernel,
        "cells2",
        (swap_flat(spectrum), extra),
        (grad1, slope0),
        (point1,),
        (sides,),
        scratch=(vmem((256, 256), BF16),),
        coef=(TILES, 16, 128),
        after=pairs[1:],
    )
    direct = lax.dot_general(inputs, grad0, TN, preferred_element_type=F32)
    (tail,) = mode_call(
        modes_last_kernel,
        "modes_last",
        0,
        mode_counts,
        (swap(coef), a0, a_in, direct),
        weights,
        ((136, 128),),
    )
    tails = [tail] + [xor_group(tail, d) for d in range(1, 4)]
    late = [t[128:136] for t in tails]
    late = (late[0] + late[1]) + (late[2] + late[3])
    late = swap(jnp.broadcast_to(late, (TILES, 8, 128)))
    spectral_grad = outer_products(tails, pairs)
    lift_grad, point_grad, proj_grad, loss = finish(late, pointwise[0], lift8)
    return (
        new_fields.reshape(2, 3, 4, 16, 256),
        lift_grad.T,
        point_grad,
        spectral_grad,
        proj_grad,
        loss[0, 0],
    )


def solution(mesh):
    return jax.shard_map(
        local,
        mesh=mesh,
        in_specs=(
            P(None, None, "tile", "role", "rep"),
            P("tile", "role", "rep"),
            P(),
            P(),
            P(),
            P(),
            P(),
            P(),
            P(None, "tile", None, None, None),
            P(),
        ),
        out_specs=(
            P(None, None, "tile", "role", "rep"),
            P(),
            P(),
            P(None, "tile", None, None, None),
            P(),
            P(),
        ),
        check_vma=False,
    )
```

```python
import functools
import math

import jax
import jax.numpy as jnp
import ml_dtypes
import numpy as np
from jax import lax
from jax.experimental import pallas as pl
from jax.experimental.pallas import tpu as pltpu
from jax.sharding import PartitionSpec as P

STEPS = 4
MODES = 8
LAYERS = 2
STEP_TIME = 0.5
PRECISE = lax.Precision.HIGHEST
F32 = jnp.float32
BF16 = jnp.bfloat16
NN = (((1,), (0,)), ((), ()))
NT = (((1,), (1,)), ((), ()))
TN = (((0,), (0,)), ((), ()))
ROOM = 62 * 1024 * 1024
LEAP_ROOM = 24 * 1024 * 1024
CELL_ROOM = 62 * 1024 * 1024
MODE_ROOM = 48 * 1024 * 1024
GROUP = ("role", "rep")
EVERY = ("role", "rep", "tile")
SX, SY, SZ = 64, 16, 256
CELLS = SY * SZ
TILES = 32


def basis(length):
    frequency = np.arange(MODES)[:, None]
    position = np.arange(length)[None, :]
    angles = 2.0 * np.pi * ((frequency * position) % length) / length
    return np.concatenate([np.cos(angles), np.sin(angles)], axis=0) * math.sqrt(2.0 / length)


def split_const(table):
    table = table.astype(np.float32)
    high = table.astype(ml_dtypes.bfloat16)
    low = (table - high.astype(np.float32)).astype(ml_dtypes.bfloat16)
    return high, low


def both_const(table):
    return np.stack(split_const(table))


TABLE_X, TABLE_Y, TABLE_Z = basis(SX), basis(SY), basis(SZ)
KRON_X = both_const(
    np.einsum("ptx,mn->xmptn", TABLE_X.reshape(16, TILES, 2), np.eye(8)).reshape(256, 256)
)
KRON_XT = np.ascontiguousarray(KRON_X.transpose(0, 2, 1))
KRON_Y = both_const(np.einsum("jy,kl->jkyl", TABLE_Y, np.eye(16)).reshape(256, 256))
KRON_YT = np.ascontiguousarray(KRON_Y.transpose(0, 2, 1))
Z_HIGH, Z_LOW = split_const(TABLE_Z)
Z_ROWS = np.concatenate([Z_HIGH, Z_LOW], axis=0)
Z_COLS = np.concatenate([Z_HIGH.T, Z_HIGH.T, Z_LOW.T], axis=1)
Z_HALF = np.stack([Z_ROWS[:, r * 128 : r * 128 + 128] for r in range(2)])
POOL_Z = np.kron(np.eye(128), np.full((2, 1), 0.125)).astype(np.float32)


def halves(value):
    high = value.astype(BF16)
    return high, (value - high.astype(F32)).astype(BF16)


def dot(a, b, dims=NN):
    return lax.dot_general(a, b, dims, preferred_element_type=F32)


def dot3(a, b, dims=NN):
    return dot(a[0], b[0], dims) + dot(a[0], b[1], dims) + dot(a[1], b[0], dims)


def lanes_of(shape):
    return lax.broadcasted_iota(jnp.int32, shape, len(shape) - 1)


def rows_of(shape):
    return lax.broadcasted_iota(jnp.int32, shape, len(shape) - 2)


def square_weight(matrix):
    high, low = halves(matrix)
    one = jnp.concatenate([high, low], axis=1)
    return jnp.concatenate([one, one], axis=0)


def rows_times(value, weight):
    high, low = halves(value)
    out = dot(jnp.concatenate([high, low], axis=1), weight)
    return out[:, :128] + out[:, 128:]


def vmem(shape, dtype=F32):
    return pltpu.VMEM(shape, dtype)


def params(room=ROOM):
    return pltpu.CompilerParams(vmem_limit_bytes=room)


def full(shape):
    return pl.BlockSpec(shape, lambda *_: (0,) * len(shape))


SMEM = pl.BlockSpec(memory_space=pltpu.SMEM)
ANY = pl.BlockSpec(memory_space=pl.ANY)


def call(kernel, ins, outs, after=(), carry=(), room=ROOM, **options):
    first, last = len(ins) + len(after), len(ins) + len(after) + len(carry)

    def run(*refs):
        rest = refs[last:]
        kernel(*refs[: len(ins)], *rest[: len(outs)], *rest[len(outs) + len(carry) :])

    return pl.pallas_call(
        run,
        out_shape=[o[0] for o in outs] + [jax.ShapeDtypeStruct(c.shape, c.dtype) for c in carry],
        in_specs=[i[1] for i in ins] + [ANY] * (len(after) + len(carry)),
        out_specs=[o[1] for o in outs] + [ANY] * len(carry),
        input_output_aliases={first + n: len(outs) + n for n in range(len(carry))},
        compiler_params=params(room),
        **options,
    )(*[i[0] for i in ins], *after, *carry)


def shape_of(*shape):
    return jax.ShapeDtypeStruct(shape, F32)


ONLY_AFTER = [(0, 3), (3, 3), (4, 3), (5, 3), (6, 3)]
ONLY_BEFORE = [(6, 0), (3, 0)]
PLANES = [(c, i) for c in range(7) for i in range(4)]
PLANES = (
    ONLY_AFTER + [p for p in PLANES if p not in ONLY_AFTER and p not in ONLY_BEFORE] + ONLY_BEFORE
)
FIRST, LAST = len(ONLY_AFTER), len(PLANES) - len(ONLY_BEFORE)


def ends_kernel(fields, material, ends, left, right):
    left[...] = jnp.zeros_like(left)
    right[...] = jnp.zeros_like(right)
    for c in range(7):
        rows = slice(c * 64, (c + 1) * 64)
        own = (fields[c] if c < 6 else material[...].astype(F32)).reshape(64, 256)
        left[rows, :] = own[:, 0:128]
        right[rows, :] = own[:, 128:256]
    for b in range(4):
        rows = slice(b * 128, (b + 1) * 128)
        first = jnp.transpose(left[rows, :])[0:8]
        last = jnp.transpose(right[rows, :])[120:128]
        at, lanes = b // 2 * 8, slice(b % 2 * 128, b % 2 * 128 + 128)
        ends[at : at + 8, lanes] = jnp.where(rows_of((8, 128)) < 4, first, last)


def ends_along_z(fields, material):
    return pl.pallas_call(
        ends_kernel,
        out_shape=shape_of(16, 256),
        scratch_shapes=[vmem((512, 128)), vmem((512, 128))],
        compiler_params=params(),
        name="ends",
    )(fields, material)


def pack_kernel(fields, material, ends, packed, after, before):
    for n, (c, i) in enumerate(PLANES):
        plane = fields[c, i] if c < 6 else material[i].astype(F32)
        packed[n] = plane
        if n < LAST:
            after[n] = plane
        if n >= FIRST:
            before[n - FIRST] = plane
    for out in (packed, after, before):
        out[out.shape[0] - 1] = ends[...]


def pack(fields, material, ends):
    count = len(PLANES)
    return pl.pallas_call(
        pack_kernel,
        out_shape=[
            shape_of(count + 1, 16, 256),
            shape_of(LAST + 1, 16, 256),
            shape_of(count - FIRST + 1, 16, 256),
        ],
        compiler_params=params(),
        name="pack",
    )(fields, material, ends)


def here():
    return lax.axis_index("role"), lax.axis_index("rep"), lax.axis_index("tile")


def leap_kernel(
    plan,
    permittivity,
    conductivity,
    own0,
    own1,
    low0,
    low1,
    high0,
    high1,
    pool,
    out_fields,
    out_piece0,
    out_piece1,
    out_piece2,
    out_piece3,
    grid_f,
    keep,
    gain,
    dt_mask,
    edge0,
    edge1,
    sums0,
    sums1,
    reduced,
    staged,
):
    role, rep, tile = here()
    shape8 = (8, 384)
    row8 = rows_of(shape8)
    top = jnp.where((row8 < 4) & (role == 0), 1.0, 0.0)
    bottom = jnp.where((row8 >= 4) & (role == 1), 1.0, 0.0)

    def column(planes, edge):
        ends = planes[planes.shape[0] - 1]
        strip = jnp.concatenate([ends[0:8], ends[8:16]], axis=1)
        row = rows_of((8, 512))
        first = jnp.where((row < 4) & (rep == 0), strip, 0.0)
        last = jnp.where((row >= 4) & (rep == 1), strip, 0.0)
        whole = jnp.concatenate([first, jnp.zeros((112, 512), F32), last], axis=0)
        for b in range(4):
            edge[b * 128 : (b + 1) * 128, :] = jnp.transpose(whole[:, b * 128 : (b + 1) * 128])

    for number, (mine, mate) in enumerate(((low0, low1), (own0, own1), (high0, high1))):
        column(mine, edge0)
        column(mate, edge1)

        for c in range(7):
            for i in range(4):
                n = PLANES.index((c, i)) - (FIRST if number == 2 else 0)
                if not 0 <= n < mine.shape[0] - 1:
                    grid_f[c, 4 * number + i] = jnp.zeros((24, 384), F32)
                    continue
                rows = slice((c * 4 + i) * 16, (c * 4 + i + 1) * 16)
                plane = jnp.concatenate([mine[n], edge0[rows, :]], axis=1)
                other = jnp.concatenate([mate[n], edge1[rows, :]], axis=1)
                halo = other[0:8] * top + other[8:16] * bottom
                grid_f[c, 4 * number + i] = jnp.concatenate([plane, halo], axis=0)

    row = rows_of((24, 384))
    lane = lanes_of((24, 384))
    row_ok = (row < 16) | ((row < 20) & (role == 0)) | ((row >= 20) & (role == 1))
    lane_ok = (lane < 256) | ((lane < 320) & (rep == 0)) | ((lane >= 320) & (rep == 1))
    inside = jnp.where(row_ok & lane_ok, 1.0, 0.0)
    dt_mask[...] = inside * STEP_TIME
    below = jnp.where(tile > 0, 1.0, 0.0)
    above = jnp.where(tile < TILES - 1, 1.0, 0.0)

    def media(p, carry):
        kind = grid_f[6, p]
        level = inside * jnp.where(p >= 8, above, 1.0)

        def choose(values):
            return jnp.where(
                kind < 0.5,
                values[0],
                jnp.where(kind < 1.5, values[1], jnp.where(kind < 2.5, values[2], values[3])),
            )

        permit = choose(permittivity)
        damping = choose(conductivity) * (0.5 * STEP_TIME) / permit
        keep[p] = (1.0 - damping) / (1.0 + damping)
        gain[p] = STEP_TIME / (permit * (1.0 + damping)) * level
        return carry

    lax.fori_loop(1, 11, media, 0, unroll=2)

    def back(value, axis):
        return pltpu.roll(value, value.shape[axis] - 1, axis)

    def step_h(p, carry):
        ex, ey, ez = grid_f[0, p], grid_f[1, p], grid_f[2, p]
        s = dt_mask[...] * below if p < 4 else dt_mask[...]
        d_zy = back(ez, 0) - ez
        d_yz = back(ey, 1) - ey
        d_xz = back(ex, 1) - ex
        d_zx = grid_f[2, p + 1] - ez
        d_yx = grid_f[1, p + 1] - ey
        d_xy = back(ex, 0) - ex
        grid_f[3, p] = grid_f[3, p] - s * (d_zy - d_yz)
        grid_f[4, p] = grid_f[4, p] - s * (d_xz - d_zx)
        grid_f[5, p] = grid_f[5, p] - s * (d_yx - d_xy)
        return carry

    def step_e(p, carry):
        hx, hy, hz = grid_f[3, p], grid_f[4, p], grid_f[5, p]
        k, g = keep[p], gain[p]
        d_zy = hz - pltpu.roll(hz, 1, 0)
        d_yz = hy - pltpu.roll(hy, 1, 1)
        d_xz = hx - pltpu.roll(hx, 1, 1)
        d_zx = hz - grid_f[5, p - 1]
        d_yx = hy - grid_f[4, p - 1]
        d_xy = hx - pltpu.roll(hx, 1, 0)
        grid_f[0, p] = k * grid_f[0, p] + g * (d_zy - d_yz)
        grid_f[1, p] = k * grid_f[1, p] + g * (d_xz - d_zx)
        grid_f[2, p] = k * grid_f[2, p] + g * (d_yx - d_xy)
        return carry

    sums0[...] = jnp.zeros_like(sums0)
    sums1[...] = jnp.zeros_like(sums1)
    for step in range(STEPS):
        for p in range(step, 11 - step):
            step_h(p, 0)
        for p in range(1 + step, 11 - step):
            step_e(p, 0)
        for x in range(2):
            for c in range(6):
                at = (x * 8 + c) * 16
                pair = grid_f[c, 4 + 2 * x, 0:16, 0:256] + grid_f[c, 5 + 2 * x, 0:16, 0:256]
                sums0[at : at + 16, :] = pair[:, 0:128]
                sums1[at : at + 16, :] = pair[:, 128:256]
        for part, sums in enumerate((sums0, sums1)):
            staged[:, part * 128 : (part + 1) * 128] = (
                sums[pl.ds(0, 128, stride=2), :] + sums[pl.ds(1, 128, stride=2), :]
            )
        reduced[step] = lax.dot_general(
            staged[...], pool[...], NN, precision=PRECISE, preferred_element_type=F32
        )
    for c in range(6):
        out_fields[c] = grid_f[c, 4:8, 0:16, 0:256]

    me = role * 2 + rep
    for d, out in enumerate((out_piece0, out_piece1, out_piece2, out_piece3)):
        out[0:128] = reduced[plan[me ^ d] - 1]
        out[128:256] = reduced[STEPS - 1]


def leapfrog(plan, permittivity, conductivity, blocks):
    whole = pl.BlockSpec(memory_space=pltpu.VMEM)
    return call(
        leap_kernel,
        [(v, SMEM) for v in (plan, permittivity, conductivity)]
        + [(v, whole) for v in (*blocks, jnp.asarray(POOL_Z))],
        [
            (shape_of(6, 4, 16, 256), whole),
        ]
        + [(shape_of(256, 128), whole)] * 4,
        room=LEAP_ROOM,
        scratch_shapes=[
            vmem((7, 12, 24, 384)),
            vmem((12, 24, 384)),
            vmem((12, 24, 384)),
            vmem((24, 384)),
            vmem((512, 128)),
            vmem((512, 128)),
            vmem((256, 128)),
            vmem((256, 128)),
            vmem((4, 128, 128)),
            vmem((128, 256)),
        ],
        name="leapfrog",
    )


def fold(value):
    return value[:, 0:128] + value[:, 128:256]


def coef_kernel(piece0, piece1, piece2, piece3, z_half, kron, out, d_scr):
    role, rep, _ = here()
    lane = lanes_of((16, 128))
    for flip, (one, other) in enumerate(((piece0, piece1), (piece2, piece3))):
        total = jnp.zeros((16, 128), F32)
        for z_rows, piece in ((z_half[rep], one), (z_half[1 - rep], other)):
            high, low = halves(
                jnp.concatenate([piece[pl.ds(y, 16, stride=8), :] for y in range(8)], axis=0)
            )
            out_high = dot(z_rows, high, NT)
            total = total + out_high[0:16] + out_high[16:32] + dot(z_rows[0:16], low, NT)
        for y in range(8):
            own = total if y == 0 else pltpu.roll(total, 128 - 16 * y, 1)
            at = pl.multiple_of(((role ^ flip) * 8 + y) * 16, 16)
            d_scr[pl.ds(at, 16), :] = jnp.where(lane < 16, own, 0.0)
    out[...] = dot3((kron[0], kron[1]), halves(d_scr[...]))


def input_coefs(pieces):
    return pl.pallas_call(
        coef_kernel,
        out_shape=shape_of(256, 128),
        scratch_shapes=[vmem((256, 128))],
        compiler_params=params(),
        name="input_coefs",
    )(*pieces, jnp.asarray(Z_HALF), jnp.asarray(KRON_Y))


def prep_kernel(first_row, piece0, piece1, piece2, piece3, weight, out_own, out_mixed):
    role_here, rep_here, _ = here()
    me = role_here * 2 + rep_here
    wide = square_weight(weight[...])
    lane = lanes_of((128, 128))
    for d, piece in enumerate((piece0, piece1, piece2, piece3)):
        source = me ^ d
        role, rep = source // 2, source % 2
        whole = jnp.concatenate(
            [piece[pl.ds(first_row + y, 16, stride=8), :] for y in range(8)], axis=0
        )
        turned = jnp.transpose(whole)
        for y in range(8):
            rows = pl.ds(pl.multiple_of((role * 8 + y) * 256 + rep * 128, 128), 128)
            own = turned if y == 0 else pltpu.roll(turned, 128 - 16 * y, 1)
            own = jnp.where(lane < 16, own, 0.0)
            sides = jnp.concatenate(halves(own), axis=1)
            out_own[rows, :] = sides if out_own.dtype == BF16 else own
            out_mixed[rows, :] = fold(dot(sides, wide))


def prepare(pieces, first_row, weight, as_sides, name):
    own = jax.ShapeDtypeStruct((CELLS, 256), BF16) if as_sides else shape_of(CELLS, 128)
    return pl.pallas_call(
        functools.partial(prep_kernel, first_row),
        out_shape=[own, shape_of(CELLS, 128)],
        compiler_params=params(),
        name=name,
    )(*pieces, weight)


GELU_A = math.sqrt(2.0 / math.pi)
GELU_B = 0.044715


def gelu_both(value):
    square = value * value
    t = jnp.tanh(value * (GELU_A + (GELU_A * GELU_B) * square))
    half = 0.5 + 0.5 * t
    hidden = value * half
    slope = half + hidden * (1.0 - half) * (2.0 * GELU_A + (6.0 * GELU_A * GELU_B) * square)
    return hidden, slope


BLOCK_Y = 8
BLOCK = BLOCK_Y * SZ
CHUNK = 128


def open_cells(spectrum, kron_t, c_scr):
    high, low = halves(dot3((kron_t[0], kron_t[1]), halves(spectrum[...])))
    for y in range(SY):
        lanes = slice(y % BLOCK_Y * 128, y % BLOCK_Y * 128 + 128)
        rows = slice(y * 16, y * 16 + 16)
        c_scr[y // BLOCK_Y, 0:16, lanes] = high[rows]
        c_scr[y // BLOCK_Y, 16:32, lanes] = low[rows]
        c_scr[y // BLOCK_Y, 32:48, lanes] = high[rows]


def chunk_of(wide, n):
    at = n * CHUNK
    return wide[at % SZ : at % SZ + CHUNK, at // SZ * 128 : at // SZ * 128 + 128]


def store_sides(out, rows, value):
    high, low = halves(value)
    out[rows, 0:128] = high
    out[rows, 128:256] = low


def cells_to(sides, z_rows, d_scr, step):
    for n in range(BLOCK_Y):
        out = dot(z_rows[...], sides[n * SZ : (n + 1) * SZ, :])
        at = pl.multiple_of((step * BLOCK_Y + n) * 16, 16)
        d_scr[pl.ds(at, 16), :] = out[0:16, 0:128] + out[0:16, 128:256] + out[16:32, 0:128]


def close_cells(kron, d_scr):
    return dot3((kron[0], kron[1]), halves(d_scr[...]))


def cells0_kernel(spectrum, pre, kron, kron_t, z_rows, z_cols, out_coef, out_h, out_slope, c_scr, d_scr):
    step = pl.program_id(0)

    @pl.when(step == 0)
    def _():
        open_cells(spectrum, kron_t, c_scr)

    spectral = dot(z_cols[...], c_scr[step])
    for n in range(BLOCK // CHUNK):
        rows = slice(n * CHUNK, (n + 1) * CHUNK)
        hidden, slope = gelu_both(chunk_of(spectral, n) + pre[rows, :])
        out_slope[rows, :] = slope
        store_sides(out_h, rows, hidden)
    cells_to(out_h, z_rows, d_scr, step)

    @pl.when(step == pl.num_programs(0) - 1)
    def _():
        out_coef[...] = close_cells(kron, d_scr)


def cells1_kernel(
    spectrum,
    h1,
    pull,
    w_point,
    w_square,
    kron,
    kron_t,
    z_rows,
    z_cols,
    out_coef,
    out_pre,
    out_h,
    c_scr,
    d_scr,
    wide,
    slopes,
):
    step = pl.program_id(0)

    @pl.when(step == 0)
    def _():
        open_cells(spectrum, kron_t, c_scr)
        wide[0] = square_weight(w_point[...])
        wide[1] = square_weight(w_square[...])

    spectral = dot(z_cols[...], c_scr[step])
    direct = dot(h1[...], wide[0])
    for n in range(BLOCK // CHUNK):
        rows = slice(n * CHUNK, (n + 1) * CHUNK)
        hidden, slope = gelu_both(chunk_of(spectral, n) + fold(direct[rows, :]))
        slopes[rows, :] = slope
        store_sides(out_h, rows, hidden)
    back = dot(out_h[...], wide[1])
    for n in range(BLOCK // CHUNK):
        rows = slice(n * CHUNK, (n + 1) * CHUNK)
        store_sides(out_pre, rows, (fold(back[rows, :]) - pull[rows, :]) * slopes[rows, :])
    cells_to(out_pre, z_rows, d_scr, step)

    @pl.when(step == pl.num_programs(0) - 1)
    def _():
        out_coef[...] = close_cells(kron, d_scr)


def cells2_kernel(
    spectrum,
    extra,
    grad1,
    slope0,
    w_point,
    kron,
    kron_t,
    z_rows,
    z_cols,
    out_coef,
    out_pre,
    c_scr,
    d_scr,
    wide,
):
    step = pl.program_id(0)

    @pl.when(step == 0)
    def _():
        open_cells(spectrum, kron_t, c_scr)
        wide[...] = square_weight(w_point[...])

    spectral = dot(z_cols[...], c_scr[step])
    direct = dot(grad1[...], wide[...])
    for n in range(BLOCK // CHUNK):
        rows = slice(n * CHUNK, (n + 1) * CHUNK)
        store_sides(
            out_pre, rows, (chunk_of(spectral, n) + fold(direct[rows, :])) * slope0[rows, :]
        )
    cells_to(out_pre, z_rows, d_scr, step)

    @pl.when(step == pl.num_programs(0) - 1)
    def _():
        out_coef[:, 0:8, :] = close_cells(kron, d_scr).reshape(TILES, 8, 128)
        out_coef[:, 8:16, :] = extra[...]


def cell_call(kernel, name, firsts, streams, weights, outs, scratch=(), coef=(256, 128), **order):
    def block(lanes):
        return pl.BlockSpec((BLOCK, lanes), lambda g: (g, 0))

    consts = [jnp.asarray(c) for c in (KRON_Y, KRON_YT, Z_ROWS, Z_COLS)]
    return call(
        kernel,
        [(v, full(v.shape)) for v in firsts]
        + [(v, block(v.shape[1])) for v in streams]
        + [(v, full(v.shape)) for v in (*weights, *consts)],
        [(shape_of(*coef), full(coef))]
        + [(jax.ShapeDtypeStruct((CELLS, lanes), kind), block(lanes)) for lanes, kind in outs],
        grid=(SY // BLOCK_Y,),
        scratch_shapes=[vmem((SY // BLOCK_Y, 48, BLOCK_Y * 128), BF16), vmem((256, 128))] + list(scratch),
        name=name,
        room=CELL_ROOM,
        **order,
    )


SIDES = pl.BlockSpec((BLOCK, 256), lambda g: (g, 0))


def point_grad_kernel(grad, h1, out, acc):
    step = pl.program_id(0)
    acc[step] = dot(grad[...], h1[...], TN)

    @pl.when(step == pl.num_programs(0) - 1)
    def _():
        point = sum(acc[n, 0:128, :] + acc[n, 128:256, :] for n in range(SY // BLOCK_Y))
        point = fold(point)
        picked = jnp.where(lanes_of((64, 128)) < 64, point[0:64], point[64:128])
        picked = picked + pltpu.roll(picked, 64, 1)
        out[...] = jnp.where(lanes_of((32, 128)) < 64, picked[0:32], picked[32:64])


def point_gradient(grad, h1):
    (out,) = call(
        point_grad_kernel,
        [(grad, SIDES), (h1, SIDES)],
        [(shape_of(32, 128), full((32, 128)))],
        grid=(SY // BLOCK_Y,),
        scratch_shapes=[vmem((SY // BLOCK_Y, 256, 256))],
        name="point_grad",
    )
    return out


def proj_grad_kernel(scale, norm, h2, target, w_proj, point, out, acc, loss_acc, wide, row):
    step = pl.program_id(0)

    @pl.when(step == 0)
    def _():
        wide[...] = square_weight(w_proj[...])
        loss_acc[...] = jnp.zeros_like(loss_acc)

    err = fold(dot(h2[...], wide[...])) - target[...]
    loss_acc[...] += jnp.sum((err * err).reshape(BLOCK // 8, 8, 128), axis=0)
    sides = jnp.concatenate(halves(err * scale), axis=1)
    acc[step] = dot(sides, h2[...], TN)

    @pl.when(step == pl.num_programs(0) - 1)
    def _():
        out[...] = jnp.zeros_like(out)
        out[:, 0, :] = point[...]
        proj = sum(acc[n, 0:16, :] + acc[n, 128:144, :] for n in range(SY // BLOCK_Y))
        proj = fold(proj)
        picked = jnp.where(lanes_of((8, 128)) < 64, proj[0:8], proj[8:16])
        turned = jnp.transpose(picked + pltpu.roll(picked, 64, 1))
        row[...] = jnp.full((32, 128), jnp.sum(loss_acc[...]) / norm)
        row[:, 0:8] = turned[0:32]
        row[:, 8:16] = turned[32:64]
        out[:, 1, :] = row[...]


def proj_gradient(norm, h2, target, w_proj, point, after):
    (out,) = call(
        functools.partial(proj_grad_kernel, 2.0 / norm, norm),
        [
            (h2, SIDES),
            (target, pl.BlockSpec((BLOCK, 128), lambda g: (g, 0))),
            (w_proj, full((128, 128))),
            (point, full((32, 128))),
        ],
        [(shape_of(TILES, 8, 128), full((TILES, 8, 128)))],
        after=(after,),
        grid=(SY // BLOCK_Y,),
        scratch_shapes=[
            vmem((SY // BLOCK_Y, 256, 256)),
            vmem((8, 128)),
            vmem((256, 256), BF16),
            vmem((32, 128)),
        ],
        name="proj_grad",
    )
    return out


def kept_modes(counts, layer):
    row = rows_of((128, 128))
    pair = lax.axis_index("tile") * 8 + row // 16
    kept = (
        (row % 8 < counts[layer, 0])
        & (pair // 16 % 8 < counts[layer, 1])
        & (pair % 8 < counts[layer, 2])
    )
    return jnp.where(kept, 1.0, 0.0)


def pair_up(rows, low_lanes):
    picked = jnp.where(low_lanes, rows[0:128], rows[128:256])
    return picked + pltpu.roll(picked, 64, 1)


MIX_STEPS = 2
MIX_PAIRS = 8 // MIX_STEPS


def mix(g_scr, b_scr, weights, step):
    row, lane = rows_of((16, 256)), lanes_of((16, 256))
    low = lanes_of((16, 128)) < 64
    for n in range(MIX_PAIRS):
        at = pl.multiple_of((step * MIX_PAIRS + n) * 16, 16)
        one = g_scr[pl.ds(at, 16), :]
        wide = jnp.concatenate([one, one], axis=1)
        total = jnp.zeros((32, 128), F32)
        for q in range(4):
            own = jnp.where(row == 4 * q + lane // 64, wide, 0.0)
            sides = jnp.concatenate(halves(own), axis=0)
            both = halves(weights[n, q * 256 : (q + 1) * 256, :])
            total = total + dot(sides, jnp.concatenate(both, axis=1))
        folded = total[0:16] + jnp.where(low, total[16:32], 0.0)
        b_scr[pl.ds(at, 16), :] = folded + pltpu.roll(folded, 64, 1)


def close_modes(b_scr, kept, kron_t, out):
    both = b_scr[...] * kept
    low = lanes_of((128, 128)) < 64
    blocks = jnp.concatenate([jnp.where(low, both, 0.0), jnp.where(low, 0.0, both)], axis=0)
    out[...] = dot3((kron_t[0], kron_t[1]), halves(blocks))


def modes_first_kernel(counts, coef, lift, weights, kron, kron_t, out, out_in, out_a, a_scr, b_scr):
    step = pl.program_id(0)

    @pl.when(step == 0)
    def _():
        rows = dot3((kron[0], kron[1]), halves(coef[...]))
        picked = jnp.where(lanes_of((128, 128)) < 8, rows[0:128], rows[128:256])
        picked = picked * kept_modes(counts, 0)
        out_in[...] = picked
        lifted = dot3(halves(picked), halves(lift[...]))
        a_scr[...] = lifted
        out_a[...] = lifted

    mix(a_scr, b_scr, weights, step)

    @pl.when(step == pl.num_programs(0) - 1)
    def _():
        close_modes(b_scr, kept_modes(counts, 0), kron_t, out)


def modes_forward_kernel(counts, coef, weights, kron, kron_t, out, out_a, a_scr, b_scr):
    step = pl.program_id(0)

    @pl.when(step == 0)
    def _():
        rows = dot3((kron[0], kron[1]), halves(coef[...]))
        a = pair_up(rows, lanes_of((128, 128)) < 64) * kept_modes(counts, 1)
        a_scr[...] = a
        out_a[...] = a

    mix(a_scr, b_scr, weights, step)

    @pl.when(step == pl.num_programs(0) - 1)
    def _():
        close_modes(b_scr, kept_modes(counts, 1), kron_t, out)


def take_gradient(rows, kept, saved, g_scr, out_pair):
    low = lanes_of((128, 128)) < 64
    g = pair_up(rows, low) * kept
    g_scr[...] = g
    out_pair[...] = jnp.where(low, g, saved[...])


def modes_backward_kernel(
    counts, coef, saved, weights, kron, kron_t, out, out_pair, g_scr, b_scr
):
    step = pl.program_id(0)

    @pl.when(step == 0)
    def _():
        rows = dot3((kron[0], kron[1]), halves(coef[...]))
        take_gradient(rows, kept_modes(counts, 1), saved, g_scr, out_pair)

    mix(g_scr, b_scr, weights, step)

    @pl.when(step == pl.num_programs(0) - 1)
    def _():
        close_modes(b_scr, kept_modes(counts, 1), kron_t, out)


def modes_last_kernel(
    counts, coef, saved, inputs, point, pair1, weights, kron, kron_t, out, g_scr, b_scr
):
    step = pl.program_id(0)

    @pl.when(step == 0)
    def _():
        value = coef[:, 0:8, :].reshape(256, 128)
        rows = dot3((kron[0], kron[1]), halves(value))
        take_gradient(rows, kept_modes(counts, 0), saved, g_scr, out.at[8:136])
        out[136:264] = pair1[...]

    mix(g_scr, b_scr, weights, step)

    @pl.when(step == pl.num_programs(0) - 1)
    def _():
        turned = jnp.transpose(inputs[...])[0:16]
        lift = dot3(halves(turned), halves(b_scr[...]))
        lift = lift[0:8] + lift[8:16]
        direct = fold(point[0:16, :] + point[128:144, :])
        direct = direct[0:8] + pltpu.roll(direct[8:16], 64, 1)
        late = jnp.where(lanes_of((8, 128)) < 64, lift, pltpu.roll(direct, 64, 1))
        extra = pltpu.roll(jnp.sum(coef[:, 8:16, :], axis=0), 6, 0)
        out[0:8] = jnp.where(rows_of((8, 128)) < 6, late, extra)


def mode_call(kernel, name, layer, counts, smalls, weights, outs, **order):
    consts = [jnp.asarray(c) for c in (KRON_X, KRON_XT)]
    return call(
        kernel,
        [(counts, SMEM)]
        + [(v, full(v.shape)) for v in smalls]
        + [(weights, pl.BlockSpec((None, MIX_PAIRS, 1024, 64), lambda m: (layer, m, 0, 0)))]
        + [(v, full(v.shape)) for v in consts],
        [(shape_of(*o), full(o)) for o in outs],
        grid=(MIX_STEPS,),
        scratch_shapes=[vmem((128, 128)), vmem((128, 128))],
        name=name,
        room=MODE_ROOM,
        **order,
    )


OUTER_PAIRS = 4


def outer_kernel(tail0, tail1, tail2, tail3, out):
    layer, part = pl.program_id(0), pl.program_id(1)
    row, lane = rows_of((64, 1024)), lanes_of((64, 1024))
    own = row % 16 == lane // 64
    low = lanes_of((64, 128)) < 64
    for n in range(OUTER_PAIRS):
        at = pl.multiple_of(8 + layer * 128 + (part * OUTER_PAIRS + n) * 16, 8)
        block = jnp.concatenate([t[pl.ds(at, 16), :] for t in (tail0, tail1, tail2, tail3)], axis=0)
        grads = halves(jnp.transpose(block)[0:64])
        twice = jnp.where(low, pltpu.roll(block, 64, 1), block)
        spread = halves(jnp.where(own, jnp.concatenate([twice] * 8, axis=1), 0.0))
        result = dot3(grads, spread)
        for r in range(16):
            out[n, r] = result[:, r * 64 : (r + 1) * 64]


def outer_products(tails):
    return pl.pallas_call(
        outer_kernel,
        grid=(LAYERS, 8 // OUTER_PAIRS),
        out_shape=shape_of(LAYERS, 8, 16, 64, 64),
        in_specs=[full((264, 128))] * 4,
        out_specs=pl.BlockSpec((None, OUTER_PAIRS, 16, 64, 64), lambda l, m: (l, m, 0, 0, 0)),
        compiler_params=params(),
        name="outer",
    )(*tails)


def spread_kernel(tail0, tail1, tail2, tail3, out):
    late = (tail0[...] + tail1[...]) + (tail2[...] + tail3[...])
    out[...] = jnp.broadcast_to(late[None], (TILES, 8, 128))


def spread(tails):
    return pl.pallas_call(
        spread_kernel,
        grid=(1,),
        out_shape=shape_of(TILES, 8, 128),
        in_specs=[pl.BlockSpec((8, 128), lambda n: (0, 0))] * 4,
        out_specs=full((TILES, 8, 128)),
        compiler_params=params(),
        name="spread",
    )(*tails)


def finish_kernel(late, point, lift, out_lift, out_point, out_proj, out_loss):
    by_tile = late[...]
    total = jnp.where(rows_of((8, 128)) < 6, jnp.sum(by_tile, axis=0), 0.0)
    through, direct = total[:, 0:64], pltpu.roll(total, 64, 1)[:, 0:64]

    def exact(a, b, dims):
        return lax.dot_general(a, b, dims, precision=PRECISE, preferred_element_type=F32)

    out_point[0] = exact(direct, lift[...], TN)
    through = through + exact(direct, point[...], NN)
    out_lift[...] = through[0:6]
    first = by_tile[:, 6, :]
    out_point[1, 0:32, :] = first[:, 0:64]
    out_point[1, 32:64, :] = first[:, 64:128]
    second = jnp.transpose(by_tile[:, 7, :])
    out_proj[:, 0:32] = second[0:6]
    out_proj[:, 32:64] = second[8:14]
    out_loss[...] = second[16:17, 0:1]


def finish(late, point, lift):
    return pl.pallas_call(
        finish_kernel,
        out_shape=[shape_of(6, 64), shape_of(2, 64, 64), shape_of(6, 64), shape_of(1, 1)],
        compiler_params=params(),
        name="finish",
    )(late, point, lift)


def passed(value, axis, by):
    length = lax.axis_size(axis)
    return lax.ppermute(value, axis, [(i, i + by) for i in range(length) if 0 <= i + by < length])


def across(value, axis):
    return lax.ppermute(value, axis, [(0, 1), (1, 0)])


def xor_group(value, d):
    return lax.ppermute(value, GROUP, [(i, i ^ d) for i in range(4)])


def parity_blocks(matrix):
    zero = jnp.zeros_like(matrix)
    return jnp.concatenate(
        [jnp.concatenate([matrix, zero], axis=1), jnp.concatenate([zero, matrix], axis=1)], axis=0
    )


def local(
    fields,
    material,
    permittivity,
    conductivity,
    plan,
    mode_counts,
    lift_weight,
    pointwise,
    spectral_weight,
    project_weight,
):
    plain = spectral_weight.reshape(LAYERS, 8, 1024, 64)
    turned = jnp.swapaxes(spectral_weight, -1, -2).reshape(LAYERS, 8, 1024, 64)

    fields6 = fields.reshape(6, 4, 16, 256)
    ends = xor_group(ends_along_z(fields6, material), 1)
    own0, after, before = pack(fields6, material, ends)
    low0, high0 = passed(after, "tile", 1), passed(before, "tile", -1)
    low0, high0 = call(lambda *refs: None, [], [], after=(turned,), carry=(low0, high0), name="hold")
    blocks = []
    for value in (own0, low0, high0):
        blocks += [value, across(value, "role")]
    new_fields, *pieces = leapfrog(plan, permittivity, conductivity, blocks)
    pieces = [pieces[0]] + [xor_group(pieces[d], d) for d in range(1, 4)]
    coef = input_coefs(pieces)

    lift8 = jnp.pad(lift_weight.T, ((0, 2), (0, 0)))
    lift16 = jnp.concatenate([lift8, lift8], axis=0)
    lift_pad = jnp.pad(jnp.concatenate([lift16, lift16], axis=1), ((0, 112), (0, 0)))
    first8 = jnp.dot(lift8, pointwise[0].T, precision=PRECISE)
    first = jnp.pad(parity_blocks(first8), ((0, 112), (0, 0)))
    point1 = parity_blocks(pointwise[1])
    proj8 = jnp.pad(project_weight, ((0, 2), (0, 0)))
    proj_t = jnp.pad(parity_blocks(proj8), ((0, 112), (0, 0)))
    norm_count = 6.0 * SX * SY * SZ * plan.shape[0]
    scale = 2.0 / norm_count
    proj_square = jnp.dot(project_weight.T, project_weight, precision=PRECISE) * scale

    def swap(value):
        value = value.reshape(TILES, -1, 128)
        return lax.all_to_all(value, "tile", 0, 0, tiled=True)

    def swap_flat(value):
        return swap(value).reshape(256, 128)

    inputs, pre0 = prepare(pieces, 0, first, True, "prepare_inputs")
    spectrum, a_in, a0 = mode_call(
        modes_first_kernel,
        "modes_first",
        0,
        mode_counts,
        (swap_flat(coef), lift_pad),
        turned,
        ((256, 128), (128, 128), (128, 128)),
        after=(pre0,),
    )
    target, pull = prepare(pieces, 128, proj_t * scale, False, "prepare_target")
    sides, plain_out = (256, BF16), (128, F32)
    coef, h1, slope0 = cell_call(
        cells0_kernel,
        "cells0",
        (swap_flat(spectrum),),
        (pre0,),
        (),
        (sides, plain_out),
        after=(pull,),
    )
    spectrum, a1 = mode_call(
        modes_forward_kernel,
        "modes_forward",
        1,
        mode_counts,
        (swap_flat(coef),),
        turned,
        ((256, 128), (128, 128)),
    )
    coef, grad1, h2 = cell_call(
        cells1_kernel,
        "cells1",
        (swap_flat(spectrum),),
        (h1, pull),
        (point1.T, parity_blocks(proj_square)),
        (sides, sides),
        scratch=(vmem((2, 256, 256), BF16), vmem((BLOCK, 128))),
    )
    point = point_gradient(grad1, h1)
    spectrum, pair1 = mode_call(
        modes_backward_kernel,
        "modes_backward",
        1,
        mode_counts,
        (swap_flat(coef), a1),
        plain,
        ((256, 128), (128, 128)),
        after=(point,),
    )
    extra = proj_gradient(norm_count, h2, target, proj_t.T, point, pair1)
    coef, grad0 = cell_call(
        cells2_kernel,
        "cells2",
        (swap_flat(spectrum), extra),
        (grad1, slope0),
        (point1,),
        (sides,),
        scratch=(vmem((256, 256), BF16),),
        coef=(TILES, 16, 128),
    )
    direct = lax.dot_general(inputs, grad0, TN, preferred_element_type=F32)
    (tail,) = mode_call(
        modes_last_kernel,
        "modes_last",
        0,
        mode_counts,
        (swap(coef), a0, a_in, direct, pair1),
        plain,
        ((264, 128),),
    )
    tails = [tail] + [xor_group(tail, d) for d in range(1, 4)]
    late = swap(spread(tails))
    spectral_grad = outer_products(tails)
    lift_grad, point_grad, proj_grad, loss = finish(late, pointwise[0], lift8)
    return (
        new_fields.reshape(2, 3, 4, 16, 256),
        lift_grad.T,
        point_grad,
        spectral_grad,
        proj_grad,
        loss[0, 0],
    )


def solution(mesh):
    return jax.shard_map(
        local,
        mesh=mesh,
        in_specs=(
            P(None, None, "tile", "role", "rep"),
            P("tile", "role", "rep"),
            P(),
            P(),
            P(),
            P(),
            P(),
            P(),
            P(None, "tile", None, None, None),
            P(),
        ),
        out_specs=(
            P(None, None, "tile", "role", "rep"),
            P(),
            P(),
            P(None, "tile", None, None, None),
            P(),
            P(),
        ),
        check_vma=False,
    )
```

```python
import functools
import math

import jax
import jax.numpy as jnp
import ml_dtypes
import numpy as np
from jax import lax
from jax.experimental import pallas as pl
from jax.experimental.pallas import tpu as pltpu
from jax.sharding import PartitionSpec as P

STEPS = 4
MODES = 8
LAYERS = 2
STEP_TIME = 0.5
PRECISE = lax.Precision.HIGHEST
F32 = jnp.float32
BF16 = jnp.bfloat16
NN = (((1,), (0,)), ((), ()))
NT = (((1,), (1,)), ((), ()))
TN = (((0,), (0,)), ((), ()))
ROOM = 48 * 1024 * 1024
LEAP_ROOM = 24 * 1024 * 1024
CELL_ROOM = 62 * 1024 * 1024
MODE_ROOM = 48 * 1024 * 1024
GROUP = ("role", "rep")
EVERY = ("role", "rep", "tile")
SX, SY, SZ = 64, 16, 256
CELLS = SY * SZ
TILES = 32


def basis(length):
    frequency = np.arange(MODES)[:, None]
    position = np.arange(length)[None, :]
    angles = 2.0 * np.pi * ((frequency * position) % length) / length
    return np.concatenate([np.cos(angles), np.sin(angles)], axis=0) * math.sqrt(2.0 / length)


def split_const(table):
    table = table.astype(np.float32)
    high = table.astype(ml_dtypes.bfloat16)
    low = (table - high.astype(np.float32)).astype(ml_dtypes.bfloat16)
    return high, low


def both_const(table):
    return np.stack(split_const(table))


TABLE_X, TABLE_Y, TABLE_Z = basis(SX), basis(SY), basis(SZ)
KRON_X = both_const(
    np.einsum("ptx,mn->xmptn", TABLE_X.reshape(16, TILES, 2), np.eye(8)).reshape(256, 256)
)
KRON_XT = np.ascontiguousarray(KRON_X.transpose(0, 2, 1))
KRON_Y = both_const(np.einsum("jy,kl->jkyl", TABLE_Y, np.eye(16)).reshape(256, 256))
KRON_YT = np.ascontiguousarray(KRON_Y.transpose(0, 2, 1))
Z_HIGH, Z_LOW = split_const(TABLE_Z)
Z_ROWS = np.concatenate([Z_HIGH, Z_LOW], axis=0)
Z_COLS = np.concatenate([Z_HIGH.T, Z_HIGH.T, Z_LOW.T], axis=1)
Z_HALF = np.stack([Z_ROWS[:, r * 128 : r * 128 + 128] for r in range(2)])
POOL_Z = np.kron(np.eye(128), np.full((2, 1), 0.125)).astype(np.float32)


def halves(value):
    high = value.astype(BF16)
    return high, (value - high.astype(F32)).astype(BF16)


def dot(a, b, dims=NN):
    return lax.dot_general(a, b, dims, preferred_element_type=F32)


def dot3(a, b, dims=NN):
    return dot(a[0], b[0], dims) + dot(a[0], b[1], dims) + dot(a[1], b[0], dims)


def lanes_of(shape):
    return lax.broadcasted_iota(jnp.int32, shape, len(shape) - 1)


def rows_of(shape):
    return lax.broadcasted_iota(jnp.int32, shape, len(shape) - 2)


def square_weight(matrix):
    high, low = halves(matrix)
    one = jnp.concatenate([high, low], axis=1)
    return jnp.concatenate([one, one], axis=0)


def rows_times(value, weight):
    high, low = halves(value)
    out = dot(jnp.concatenate([high, low], axis=1), weight)
    return out[:, :128] + out[:, 128:]


def vmem(shape, dtype=F32):
    return pltpu.VMEM(shape, dtype)


def params(room=ROOM):
    return pltpu.CompilerParams(vmem_limit_bytes=room)


def full(shape):
    return pl.BlockSpec(shape, lambda *_: (0,) * len(shape))


SMEM = pl.BlockSpec(memory_space=pltpu.SMEM)
ANY = pl.BlockSpec(memory_space=pl.ANY)


def call(kernel, ins, outs, after=(), carry=(), room=ROOM, **options):
    first, last = len(ins) + len(after), len(ins) + len(after) + len(carry)

    def run(*refs):
        rest = refs[last:]
        kernel(*refs[: len(ins)], *rest[: len(outs)], *rest[len(outs) + len(carry) :])

    return pl.pallas_call(
        run,
        out_shape=[o[0] for o in outs] + [jax.ShapeDtypeStruct(c.shape, c.dtype) for c in carry],
        in_specs=[i[1] for i in ins] + [ANY] * (len(after) + len(carry)),
        out_specs=[o[1] for o in outs] + [ANY] * len(carry),
        input_output_aliases={first + n: len(outs) + n for n in range(len(carry))},
        compiler_params=params(room),
        **options,
    )(*[i[0] for i in ins], *after, *carry)


def shape_of(*shape):
    return jax.ShapeDtypeStruct(shape, F32)


ONLY_AFTER = [(0, 3), (3, 3), (4, 3), (5, 3), (6, 3)]
ONLY_BEFORE = [(6, 0), (3, 0)]
PLANES = [(c, i) for c in range(7) for i in range(4)]
PLANES = (
    ONLY_AFTER + [p for p in PLANES if p not in ONLY_AFTER and p not in ONLY_BEFORE] + ONLY_BEFORE
)
FIRST, LAST = len(ONLY_AFTER), len(PLANES) - len(ONLY_BEFORE)


def ends_kernel(fields, material, ends, left, right):
    left[...] = jnp.zeros_like(left)
    right[...] = jnp.zeros_like(right)
    for c in range(7):
        rows = slice(c * 64, (c + 1) * 64)
        own = (fields[c] if c < 6 else material[...].astype(F32)).reshape(64, 256)
        left[rows, :] = own[:, 0:128]
        right[rows, :] = own[:, 128:256]
    for b in range(4):
        rows = slice(b * 128, (b + 1) * 128)
        first = jnp.transpose(left[rows, :])[0:8]
        last = jnp.transpose(right[rows, :])[120:128]
        at, lanes = b // 2 * 8, slice(b % 2 * 128, b % 2 * 128 + 128)
        ends[at : at + 8, lanes] = jnp.where(rows_of((8, 128)) < 4, first, last)


def ends_along_z(fields, material):
    return pl.pallas_call(
        ends_kernel,
        out_shape=shape_of(16, 256),
        scratch_shapes=[vmem((512, 128)), vmem((512, 128))],
        compiler_params=params(),
        name="ends",
    )(fields, material)


def pack_kernel(fields, material, ends, packed, after, before):
    for n, (c, i) in enumerate(PLANES):
        plane = fields[c, i] if c < 6 else material[i].astype(F32)
        packed[n] = plane
        if n < LAST:
            after[n] = plane
        if n >= FIRST:
            before[n - FIRST] = plane
    for out in (packed, after, before):
        out[out.shape[0] - 1] = ends[...]


def pack(fields, material, ends):
    count = len(PLANES)
    return pl.pallas_call(
        pack_kernel,
        out_shape=[
            shape_of(count + 1, 16, 256),
            shape_of(LAST + 1, 16, 256),
            shape_of(count - FIRST + 1, 16, 256),
        ],
        compiler_params=params(),
        name="pack",
    )(fields, material, ends)


def here():
    return lax.axis_index("role"), lax.axis_index("rep"), lax.axis_index("tile")


def leap_kernel(
    plan,
    permittivity,
    conductivity,
    own0,
    own1,
    low0,
    low1,
    high0,
    high1,
    pool,
    out_fields,
    out_piece0,
    out_piece1,
    out_piece2,
    out_piece3,
    grid_f,
    keep,
    gain,
    dt_mask,
    edge0,
    edge1,
    sums0,
    sums1,
    reduced,
    staged,
):
    role, rep, tile = here()
    shape8 = (8, 384)
    row8 = rows_of(shape8)
    top = jnp.where((row8 < 4) & (role == 0), 1.0, 0.0)
    bottom = jnp.where((row8 >= 4) & (role == 1), 1.0, 0.0)

    def column(planes, edge):
        ends = planes[planes.shape[0] - 1]
        strip = jnp.concatenate([ends[0:8], ends[8:16]], axis=1)
        row = rows_of((8, 512))
        first = jnp.where((row < 4) & (rep == 0), strip, 0.0)
        last = jnp.where((row >= 4) & (rep == 1), strip, 0.0)
        whole = jnp.concatenate([first, jnp.zeros((112, 512), F32), last], axis=0)
        for b in range(4):
            edge[b * 128 : (b + 1) * 128, :] = jnp.transpose(whole[:, b * 128 : (b + 1) * 128])

    for number, (mine, mate) in enumerate(((low0, low1), (own0, own1), (high0, high1))):
        column(mine, edge0)
        column(mate, edge1)

        for c in range(7):
            for i in range(4):
                n = PLANES.index((c, i)) - (FIRST if number == 2 else 0)
                if not 0 <= n < mine.shape[0] - 1:
                    grid_f[c, 4 * number + i] = jnp.zeros((24, 384), F32)
                    continue
                rows = slice((c * 4 + i) * 16, (c * 4 + i + 1) * 16)
                plane = jnp.concatenate([mine[n], edge0[rows, :]], axis=1)
                other = jnp.concatenate([mate[n], edge1[rows, :]], axis=1)
                halo = other[0:8] * top + other[8:16] * bottom
                grid_f[c, 4 * number + i] = jnp.concatenate([plane, halo], axis=0)

    row = rows_of((24, 384))
    lane = lanes_of((24, 384))
    row_ok = (row < 16) | ((row < 20) & (role == 0)) | ((row >= 20) & (role == 1))
    lane_ok = (lane < 256) | ((lane < 320) & (rep == 0)) | ((lane >= 320) & (rep == 1))
    inside = jnp.where(row_ok & lane_ok, 1.0, 0.0)
    dt_mask[...] = inside * STEP_TIME
    below = jnp.where(tile > 0, 1.0, 0.0)
    above = jnp.where(tile < TILES - 1, 1.0, 0.0)

    def media(p, carry):
        kind = grid_f[6, p]
        level = inside * jnp.where(p >= 8, above, 1.0)

        def choose(values):
            return jnp.where(
                kind < 0.5,
                values[0],
                jnp.where(kind < 1.5, values[1], jnp.where(kind < 2.5, values[2], values[3])),
            )

        permit = choose(permittivity)
        damping = choose(conductivity) * (0.5 * STEP_TIME) / permit
        keep[p] = (1.0 - damping) / (1.0 + damping)
        gain[p] = STEP_TIME / (permit * (1.0 + damping)) * level
        return carry

    lax.fori_loop(1, 11, media, 0, unroll=2)

    def back(value, axis):
        return pltpu.roll(value, value.shape[axis] - 1, axis)

    def step_h(p, carry):
        ex, ey, ez = grid_f[0, p], grid_f[1, p], grid_f[2, p]
        s = dt_mask[...] * below if p < 4 else dt_mask[...]
        d_zy = back(ez, 0) - ez
        d_yz = back(ey, 1) - ey
        d_xz = back(ex, 1) - ex
        d_zx = grid_f[2, p + 1] - ez
        d_yx = grid_f[1, p + 1] - ey
        d_xy = back(ex, 0) - ex
        grid_f[3, p] = grid_f[3, p] - s * (d_zy - d_yz)
        grid_f[4, p] = grid_f[4, p] - s * (d_xz - d_zx)
        grid_f[5, p] = grid_f[5, p] - s * (d_yx - d_xy)
        return carry

    def step_e(p, carry):
        hx, hy, hz = grid_f[3, p], grid_f[4, p], grid_f[5, p]
        k, g = keep[p], gain[p]
        d_zy = hz - pltpu.roll(hz, 1, 0)
        d_yz = hy - pltpu.roll(hy, 1, 1)
        d_xz = hx - pltpu.roll(hx, 1, 1)
        d_zx = hz - grid_f[5, p - 1]
        d_yx = hy - grid_f[4, p - 1]
        d_xy = hx - pltpu.roll(hx, 1, 0)
        grid_f[0, p] = k * grid_f[0, p] + g * (d_zy - d_yz)
        grid_f[1, p] = k * grid_f[1, p] + g * (d_xz - d_zx)
        grid_f[2, p] = k * grid_f[2, p] + g * (d_yx - d_xy)
        return carry

    sums0[...] = jnp.zeros_like(sums0)
    sums1[...] = jnp.zeros_like(sums1)
    for step in range(STEPS):
        for p in range(step, 11 - step):
            step_h(p, 0)
        for p in range(1 + step, 11 - step):
            step_e(p, 0)
        for x in range(2):
            for c in range(6):
                at = (x * 8 + c) * 16
                pair = grid_f[c, 4 + 2 * x, 0:16, 0:256] + grid_f[c, 5 + 2 * x, 0:16, 0:256]
                sums0[at : at + 16, :] = pair[:, 0:128]
                sums1[at : at + 16, :] = pair[:, 128:256]
        for part, sums in enumerate((sums0, sums1)):
            staged[:, part * 128 : (part + 1) * 128] = (
                sums[pl.ds(0, 128, stride=2), :] + sums[pl.ds(1, 128, stride=2), :]
            )
        reduced[step] = lax.dot_general(
            staged[...], pool[...], NN, precision=PRECISE, preferred_element_type=F32
        )
    for c in range(6):
        out_fields[c] = grid_f[c, 4:8, 0:16, 0:256]

    me = role * 2 + rep
    for d, out in enumerate((out_piece0, out_piece1, out_piece2, out_piece3)):
        out[0:128] = reduced[plan[me ^ d] - 1]
        out[128:256] = reduced[STEPS - 1]


def leapfrog(plan, permittivity, conductivity, blocks):
    whole = pl.BlockSpec(memory_space=pltpu.VMEM)
    return call(
        leap_kernel,
        [(v, SMEM) for v in (plan, permittivity, conductivity)]
        + [(v, whole) for v in (*blocks, jnp.asarray(POOL_Z))],
        [
            (shape_of(6, 4, 16, 256), whole),
        ]
        + [(shape_of(256, 128), whole)] * 4,
        room=LEAP_ROOM,
        scratch_shapes=[
            vmem((7, 12, 24, 384)),
            vmem((12, 24, 384)),
            vmem((12, 24, 384)),
            vmem((24, 384)),
            vmem((512, 128)),
            vmem((512, 128)),
            vmem((256, 128)),
            vmem((256, 128)),
            vmem((4, 128, 128)),
            vmem((128, 256)),
        ],
        name="leapfrog",
    )


def fold(value):
    return value[:, 0:128] + value[:, 128:256]


def coef_kernel(piece0, piece1, piece2, piece3, z_half, kron, out, d_scr):
    role, rep, _ = here()
    lane = lanes_of((16, 128))
    for flip, (one, other) in enumerate(((piece0, piece1), (piece2, piece3))):
        total = jnp.zeros((16, 128), F32)
        for z_rows, piece in ((z_half[rep], one), (z_half[1 - rep], other)):
            high, low = halves(
                jnp.concatenate([piece[pl.ds(y, 16, stride=8), :] for y in range(8)], axis=0)
            )
            out_high = dot(z_rows, high, NT)
            total = total + out_high[0:16] + out_high[16:32] + dot(z_rows[0:16], low, NT)
        for y in range(8):
            own = total if y == 0 else pltpu.roll(total, 128 - 16 * y, 1)
            at = pl.multiple_of(((role ^ flip) * 8 + y) * 16, 16)
            d_scr[pl.ds(at, 16), :] = jnp.where(lane < 16, own, 0.0)
    out[...] = dot3((kron[0], kron[1]), halves(d_scr[...]))


def input_coefs(pieces):
    return pl.pallas_call(
        coef_kernel,
        out_shape=shape_of(256, 128),
        scratch_shapes=[vmem((256, 128))],
        compiler_params=params(),
        name="input_coefs",
    )(*pieces, jnp.asarray(Z_HALF), jnp.asarray(KRON_Y))


def prep_kernel(first_row, piece0, piece1, piece2, piece3, weight, out_own, out_mixed):
    role_here, rep_here, _ = here()
    me = role_here * 2 + rep_here
    wide = square_weight(weight[...])
    lane = lanes_of((128, 128))
    for d, piece in enumerate((piece0, piece1, piece2, piece3)):
        source = me ^ d
        role, rep = source // 2, source % 2
        whole = jnp.concatenate(
            [piece[pl.ds(first_row + y, 16, stride=8), :] for y in range(8)], axis=0
        )
        turned = jnp.transpose(whole)
        for y in range(8):
            rows = pl.ds(pl.multiple_of((role * 8 + y) * 256 + rep * 128, 128), 128)
            own = turned if y == 0 else pltpu.roll(turned, 128 - 16 * y, 1)
            own = jnp.where(lane < 16, own, 0.0)
            sides = jnp.concatenate(halves(own), axis=1)
            out_own[rows, :] = sides if out_own.dtype == BF16 else own
            out_mixed[rows, :] = fold(dot(sides, wide))


def prepare(pieces, first_row, weight, as_sides, name):
    own = jax.ShapeDtypeStruct((CELLS, 256), BF16) if as_sides else shape_of(CELLS, 128)
    return pl.pallas_call(
        functools.partial(prep_kernel, first_row),
        out_shape=[own, shape_of(CELLS, 128)],
        compiler_params=params(),
        name=name,
    )(*pieces, weight)


GELU_A = math.sqrt(2.0 / math.pi)
GELU_B = 0.044715


def gelu_both(value):
    square = value * value
    t = jnp.tanh(value * (GELU_A + (GELU_A * GELU_B) * square))
    half = 0.5 + 0.5 * t
    hidden = value * half
    slope = half + hidden * (1.0 - half) * (2.0 * GELU_A + (6.0 * GELU_A * GELU_B) * square)
    return hidden, slope


BLOCK_Y = 8
BLOCK = BLOCK_Y * SZ
CHUNK = 128


def open_cells(spectrum, kron_t, c_scr):
    high, low = halves(dot3((kron_t[0], kron_t[1]), halves(spectrum[...])))
    for y in range(SY):
        lanes = slice(y % BLOCK_Y * 128, y % BLOCK_Y * 128 + 128)
        rows = slice(y * 16, y * 16 + 16)
        c_scr[y // BLOCK_Y, 0:16, lanes] = high[rows]
        c_scr[y // BLOCK_Y, 16:32, lanes] = low[rows]
        c_scr[y // BLOCK_Y, 32:48, lanes] = high[rows]


def chunk_of(wide, n):
    at = n * CHUNK
    return wide[at % SZ : at % SZ + CHUNK, at // SZ * 128 : at // SZ * 128 + 128]


def store_sides(out, rows, value):
    high, low = halves(value)
    out[rows, 0:128] = high
    out[rows, 128:256] = low


def cells_to(sides, z_rows, d_scr, step):
    for n in range(BLOCK_Y):
        out = dot(z_rows[...], sides[n * SZ : (n + 1) * SZ, :])
        at = pl.multiple_of((step * BLOCK_Y + n) * 16, 16)
        d_scr[pl.ds(at, 16), :] = out[0:16, 0:128] + out[0:16, 128:256] + out[16:32, 0:128]


def close_cells(kron, d_scr):
    return dot3((kron[0], kron[1]), halves(d_scr[...]))


def cells0_kernel(spectrum, pre, kron, kron_t, z_rows, z_cols, out_coef, out_h, out_slope, c_scr, d_scr):
    step = pl.program_id(0)

    @pl.when(step == 0)
    def _():
        open_cells(spectrum, kron_t, c_scr)

    spectral = dot(z_cols[...], c_scr[step])
    for n in range(BLOCK // CHUNK):
        rows = slice(n * CHUNK, (n + 1) * CHUNK)
        hidden, slope = gelu_both(chunk_of(spectral, n) + pre[rows, :])
        out_slope[rows, :] = slope
        store_sides(out_h, rows, hidden)
    cells_to(out_h, z_rows, d_scr, step)

    @pl.when(step == pl.num_programs(0) - 1)
    def _():
        out_coef[...] = close_cells(kron, d_scr)


def cells1_kernel(
    spectrum,
    h1,
    pull,
    w_point,
    w_square,
    kron,
    kron_t,
    z_rows,
    z_cols,
    out_coef,
    out_pre,
    out_h,
    c_scr,
    d_scr,
    wide,
    slopes,
):
    step = pl.program_id(0)

    @pl.when(step == 0)
    def _():
        open_cells(spectrum, kron_t, c_scr)
        wide[0] = square_weight(w_point[...])
        wide[1] = square_weight(w_square[...])

    spectral = dot(z_cols[...], c_scr[step])
    direct = dot(h1[...], wide[0])
    for n in range(BLOCK // CHUNK):
        rows = slice(n * CHUNK, (n + 1) * CHUNK)
        hidden, slope = gelu_both(chunk_of(spectral, n) + fold(direct[rows, :]))
        slopes[rows, :] = slope
        store_sides(out_h, rows, hidden)
    back = dot(out_h[...], wide[1])
    for n in range(BLOCK // CHUNK):
        rows = slice(n * CHUNK, (n + 1) * CHUNK)
        store_sides(out_pre, rows, (fold(back[rows, :]) - pull[rows, :]) * slopes[rows, :])
    cells_to(out_pre, z_rows, d_scr, step)

    @pl.when(step == pl.num_programs(0) - 1)
    def _():
        out_coef[...] = close_cells(kron, d_scr)


def cells2_kernel(
    spectrum,
    extra,
    grad1,
    slope0,
    w_point,
    kron,
    kron_t,
    z_rows,
    z_cols,
    out_coef,
    out_pre,
    c_scr,
    d_scr,
    wide,
):
    step = pl.program_id(0)

    @pl.when(step == 0)
    def _():
        open_cells(spectrum, kron_t, c_scr)
        wide[...] = square_weight(w_point[...])

    spectral = dot(z_cols[...], c_scr[step])
    direct = dot(grad1[...], wide[...])
    for n in range(BLOCK // CHUNK):
        rows = slice(n * CHUNK, (n + 1) * CHUNK)
        store_sides(
            out_pre, rows, (chunk_of(spectral, n) + fold(direct[rows, :])) * slope0[rows, :]
        )
    cells_to(out_pre, z_rows, d_scr, step)

    @pl.when(step == pl.num_programs(0) - 1)
    def _():
        out_coef[:, 0:8, :] = close_cells(kron, d_scr).reshape(TILES, 8, 128)
        out_coef[:, 8:16, :] = extra[...]


def cell_call(kernel, name, firsts, streams, weights, outs, scratch=(), coef=(256, 128), **order):
    def block(lanes):
        return pl.BlockSpec((BLOCK, lanes), lambda g: (g, 0))

    consts = [jnp.asarray(c) for c in (KRON_Y, KRON_YT, Z_ROWS, Z_COLS)]
    return call(
        kernel,
        [(v, full(v.shape)) for v in firsts]
        + [(v, block(v.shape[1])) for v in streams]
        + [(v, full(v.shape)) for v in (*weights, *consts)],
        [(shape_of(*coef), full(coef))]
        + [(jax.ShapeDtypeStruct((CELLS, lanes), kind), block(lanes)) for lanes, kind in outs],
        grid=(SY // BLOCK_Y,),
        scratch_shapes=[vmem((SY // BLOCK_Y, 48, BLOCK_Y * 128), BF16), vmem((256, 128))] + list(scratch),
        name=name,
        room=CELL_ROOM,
        **order,
    )


SIDES = pl.BlockSpec((BLOCK, 256), lambda g: (g, 0))


def point_grad_kernel(grad, h1, out, acc):
    step = pl.program_id(0)
    acc[step] = dot(grad[...], h1[...], TN)

    @pl.when(step == pl.num_programs(0) - 1)
    def _():
        point = sum(acc[n, 0:128, :] + acc[n, 128:256, :] for n in range(SY // BLOCK_Y))
        point = fold(point)
        picked = jnp.where(lanes_of((64, 128)) < 64, point[0:64], point[64:128])
        picked = picked + pltpu.roll(picked, 64, 1)
        out[...] = jnp.where(lanes_of((32, 128)) < 64, picked[0:32], picked[32:64])


def point_gradient(grad, h1):
    (out,) = call(
        point_grad_kernel,
        [(grad, SIDES), (h1, SIDES)],
        [(shape_of(32, 128), full((32, 128)))],
        grid=(SY // BLOCK_Y,),
        scratch_shapes=[vmem((SY // BLOCK_Y, 256, 256))],
        name="point_grad",
    )
    return out


def proj_grad_kernel(scale, norm, h2, target, w_proj, point, out, acc, loss_acc, wide, row):
    step = pl.program_id(0)

    @pl.when(step == 0)
    def _():
        wide[...] = square_weight(w_proj[...])
        loss_acc[...] = jnp.zeros_like(loss_acc)

    err = fold(dot(h2[...], wide[...])) - target[...]
    loss_acc[...] += jnp.sum((err * err).reshape(BLOCK // 8, 8, 128), axis=0)
    sides = jnp.concatenate(halves(err * scale), axis=1)
    acc[step] = dot(sides, h2[...], TN)

    @pl.when(step == pl.num_programs(0) - 1)
    def _():
        out[...] = jnp.zeros_like(out)
        out[:, 0, :] = point[...]
        proj = sum(acc[n, 0:16, :] + acc[n, 128:144, :] for n in range(SY // BLOCK_Y))
        proj = fold(proj)
        picked = jnp.where(lanes_of((8, 128)) < 64, proj[0:8], proj[8:16])
        turned = jnp.transpose(picked + pltpu.roll(picked, 64, 1))
        row[...] = jnp.full((32, 128), jnp.sum(loss_acc[...]) / norm)
        row[:, 0:8] = turned[0:32]
        row[:, 8:16] = turned[32:64]
        out[:, 1, :] = row[...]


def proj_gradient(norm, h2, target, w_proj, point, after):
    (out,) = call(
        functools.partial(proj_grad_kernel, 2.0 / norm, norm),
        [
            (h2, SIDES),
            (target, pl.BlockSpec((BLOCK, 128), lambda g: (g, 0))),
            (w_proj, full((128, 128))),
            (point, full((32, 128))),
        ],
        [(shape_of(TILES, 8, 128), full((TILES, 8, 128)))],
        after=(after,),
        grid=(SY // BLOCK_Y,),
        scratch_shapes=[
            vmem((SY // BLOCK_Y, 256, 256)),
            vmem((8, 128)),
            vmem((256, 256), BF16),
            vmem((32, 128)),
        ],
        name="proj_grad",
    )
    return out


def kept_modes(counts, layer):
    row = rows_of((128, 128))
    pair = lax.axis_index("tile") * 8 + row // 16
    kept = (
        (row % 8 < counts[layer, 0])
        & (pair // 16 % 8 < counts[layer, 1])
        & (pair % 8 < counts[layer, 2])
    )
    return jnp.where(kept, 1.0, 0.0)


def pair_up(rows, low_lanes):
    picked = jnp.where(low_lanes, rows[0:128], rows[128:256])
    return picked + pltpu.roll(picked, 64, 1)


MIX_STEPS = 2
MIX_PAIRS = 8 // MIX_STEPS


def mix(g_scr, b_scr, weights, step):
    row, lane = rows_of((16, 256)), lanes_of((16, 256))
    low = lanes_of((16, 128)) < 64
    for n in range(MIX_PAIRS):
        at = pl.multiple_of((step * MIX_PAIRS + n) * 16, 16)
        one = g_scr[pl.ds(at, 16), :]
        wide = jnp.concatenate([one, one], axis=1)
        total = jnp.zeros((32, 128), F32)
        for q in range(4):
            own = jnp.where(row == 4 * q + lane // 64, wide, 0.0)
            sides = jnp.concatenate(halves(own), axis=0)
            both = halves(weights[n, q * 256 : (q + 1) * 256, :])
            total = total + dot(sides, jnp.concatenate(both, axis=1))
        folded = total[0:16] + jnp.where(low, total[16:32], 0.0)
        b_scr[pl.ds(at, 16), :] = folded + pltpu.roll(folded, 64, 1)


def close_modes(b_scr, kept, kron_t, out):
    both = b_scr[...] * kept
    low = lanes_of((128, 128)) < 64
    blocks = jnp.concatenate([jnp.where(low, both, 0.0), jnp.where(low, 0.0, both)], axis=0)
    out[...] = dot3((kron_t[0], kron_t[1]), halves(blocks))


def modes_first_kernel(counts, coef, lift, weights, kron, kron_t, out, out_in, out_a, a_scr, b_scr):
    step = pl.program_id(0)

    @pl.when(step == 0)
    def _():
        rows = dot3((kron[0], kron[1]), halves(coef[...]))
        picked = jnp.where(lanes_of((128, 128)) < 8, rows[0:128], rows[128:256])
        picked = picked * kept_modes(counts, 0)
        out_in[...] = picked
        lifted = dot3(halves(picked), halves(lift[...]))
        a_scr[...] = lifted
        out_a[...] = lifted

    mix(a_scr, b_scr, weights, step)

    @pl.when(step == pl.num_programs(0) - 1)
    def _():
        close_modes(b_scr, kept_modes(counts, 0), kron_t, out)


def modes_forward_kernel(counts, coef, weights, kron, kron_t, out, out_a, a_scr, b_scr):
    step = pl.program_id(0)

    @pl.when(step == 0)
    def _():
        rows = dot3((kron[0], kron[1]), halves(coef[...]))
        a = pair_up(rows, lanes_of((128, 128)) < 64) * kept_modes(counts, 1)
        a_scr[...] = a
        out_a[...] = a

    mix(a_scr, b_scr, weights, step)

    @pl.when(step == pl.num_programs(0) - 1)
    def _():
        close_modes(b_scr, kept_modes(counts, 1), kron_t, out)


def take_gradient(rows, kept, saved, g_scr, out_pair):
    low = lanes_of((128, 128)) < 64
    g = pair_up(rows, low) * kept
    g_scr[...] = g
    out_pair[...] = jnp.where(low, g, saved[...])


def modes_backward_kernel(
    counts, coef, saved, weights, kron, kron_t, out, out_pair, g_scr, b_scr
):
    step = pl.program_id(0)

    @pl.when(step == 0)
    def _():
        rows = dot3((kron[0], kron[1]), halves(coef[...]))
        take_gradient(rows, kept_modes(counts, 1), saved, g_scr, out_pair)

    mix(g_scr, b_scr, weights, step)

    @pl.when(step == pl.num_programs(0) - 1)
    def _():
        close_modes(b_scr, kept_modes(counts, 1), kron_t, out)


def modes_last_kernel(
    counts, coef, saved, inputs, point, pair1, weights, kron, kron_t, out, g_scr, b_scr
):
    step = pl.program_id(0)

    @pl.when(step == 0)
    def _():
        value = coef[:, 0:8, :].reshape(256, 128)
        rows = dot3((kron[0], kron[1]), halves(value))
        take_gradient(rows, kept_modes(counts, 0), saved, g_scr, out.at[8:136])
        out[136:264] = pair1[...]

    mix(g_scr, b_scr, weights, step)

    @pl.when(step == pl.num_programs(0) - 1)
    def _():
        turned = jnp.transpose(inputs[...])[0:16]
        lift = dot3(halves(turned), halves(b_scr[...]))
        lift = lift[0:8] + lift[8:16]
        direct = fold(point[0:16, :] + point[128:144, :])
        direct = direct[0:8] + pltpu.roll(direct[8:16], 64, 1)
        late = jnp.where(lanes_of((8, 128)) < 64, lift, pltpu.roll(direct, 64, 1))
        extra = pltpu.roll(jnp.sum(coef[:, 8:16, :], axis=0), 6, 0)
        out[0:8] = jnp.where(rows_of((8, 128)) < 6, late, extra)


def mode_call(kernel, name, layer, counts, smalls, weights, outs, **order):
    consts = [jnp.asarray(c) for c in (KRON_X, KRON_XT)]
    return call(
        kernel,
        [(counts, SMEM)]
        + [(v, full(v.shape)) for v in smalls]
        + [(weights, pl.BlockSpec((None, MIX_PAIRS, 1024, 64), lambda m: (layer, m, 0, 0)))]
        + [(v, full(v.shape)) for v in consts],
        [(shape_of(*o), full(o)) for o in outs],
        grid=(MIX_STEPS,),
        scratch_shapes=[vmem((128, 128)), vmem((128, 128))],
        name=name,
        room=MODE_ROOM,
        **order,
    )


OUTER_PAIRS = 4


def outer_kernel(tail0, tail1, tail2, tail3, out):
    layer, part = pl.program_id(0), pl.program_id(1)
    row, lane = rows_of((64, 1024)), lanes_of((64, 1024))
    own = row % 16 == lane // 64
    low = lanes_of((64, 128)) < 64
    for n in range(OUTER_PAIRS):
        at = pl.multiple_of(8 + layer * 128 + (part * OUTER_PAIRS + n) * 16, 8)
        block = jnp.concatenate([t[pl.ds(at, 16), :] for t in (tail0, tail1, tail2, tail3)], axis=0)
        grads = halves(jnp.transpose(block)[0:64])
        twice = jnp.where(low, pltpu.roll(block, 64, 1), block)
        spread = halves(jnp.where(own, jnp.concatenate([twice] * 8, axis=1), 0.0))
        result = dot3(grads, spread)
        for r in range(16):
            out[n, r] = result[:, r * 64 : (r + 1) * 64]


def outer_products(tails):
    return pl.pallas_call(
        outer_kernel,
        grid=(LAYERS, 8 // OUTER_PAIRS),
        out_shape=shape_of(LAYERS, 8, 16, 64, 64),
        in_specs=[full((264, 128))] * 4,
        out_specs=pl.BlockSpec((None, OUTER_PAIRS, 16, 64, 64), lambda l, m: (l, m, 0, 0, 0)),
        compiler_params=params(),
        name="outer",
    )(*tails)


def spread_kernel(tail0, tail1, tail2, tail3, out):
    late = (tail0[...] + tail1[...]) + (tail2[...] + tail3[...])
    out[...] = jnp.broadcast_to(late[None], (TILES, 8, 128))


def spread(tails):
    return pl.pallas_call(
        spread_kernel,
        grid=(1,),
        out_shape=shape_of(TILES, 8, 128),
        in_specs=[pl.BlockSpec((8, 128), lambda n: (0, 0))] * 4,
        out_specs=full((TILES, 8, 128)),
        compiler_params=params(),
        name="spread",
    )(*tails)


def finish_kernel(late, point, lift, out_lift, out_point, out_proj, out_loss):
    by_tile = late[...]
    total = jnp.where(rows_of((8, 128)) < 6, jnp.sum(by_tile, axis=0), 0.0)
    through, direct = total[:, 0:64], pltpu.roll(total, 64, 1)[:, 0:64]

    def exact(a, b, dims):
        return lax.dot_general(a, b, dims, precision=PRECISE, preferred_element_type=F32)

    out_point[0] = exact(direct, lift[...], TN)
    through = through + exact(direct, point[...], NN)
    out_lift[...] = through[0:6]
    first = by_tile[:, 6, :]
    out_point[1, 0:32, :] = first[:, 0:64]
    out_point[1, 32:64, :] = first[:, 64:128]
    second = jnp.transpose(by_tile[:, 7, :])
    out_proj[:, 0:32] = second[0:6]
    out_proj[:, 32:64] = second[8:14]
    out_loss[...] = second[16:17, 0:1]


def finish(late, point, lift):
    return pl.pallas_call(
        finish_kernel,
        out_shape=[shape_of(6, 64), shape_of(2, 64, 64), shape_of(6, 64), shape_of(1, 1)],
        compiler_params=params(),
        name="finish",
    )(late, point, lift)


def passed(value, axis, by):
    length = lax.axis_size(axis)
    return lax.ppermute(value, axis, [(i, i + by) for i in range(length) if 0 <= i + by < length])


def across(value, axis):
    return lax.ppermute(value, axis, [(0, 1), (1, 0)])


def xor_group(value, d):
    return lax.ppermute(value, GROUP, [(i, i ^ d) for i in range(4)])


def parity_blocks(matrix):
    zero = jnp.zeros_like(matrix)
    return jnp.concatenate(
        [jnp.concatenate([matrix, zero], axis=1), jnp.concatenate([zero, matrix], axis=1)], axis=0
    )


def local(
    fields,
    material,
    permittivity,
    conductivity,
    plan,
    mode_counts,
    lift_weight,
    pointwise,
    spectral_weight,
    project_weight,
):
    plain = spectral_weight.reshape(LAYERS, 8, 1024, 64)
    turned = jnp.swapaxes(spectral_weight, -1, -2).reshape(LAYERS, 8, 1024, 64)

    fields6 = fields.reshape(6, 4, 16, 256)
    ends = xor_group(ends_along_z(fields6, material), 1)
    own0, after, before = pack(fields6, material, ends)
    low0, high0 = passed(after, "tile", 1), passed(before, "tile", -1)
    low0, high0 = call(lambda *refs: None, [], [], after=(turned,), carry=(low0, high0), name="hold")
    blocks = []
    for value in (own0, low0, high0):
        blocks += [value, across(value, "role")]
    new_fields, *pieces = leapfrog(plan, permittivity, conductivity, blocks)
    pieces = [pieces[0]] + [xor_group(pieces[d], d) for d in range(1, 4)]
    coef = input_coefs(pieces)

    lift8 = jnp.pad(lift_weight.T, ((0, 2), (0, 0)))
    lift16 = jnp.concatenate([lift8, lift8], axis=0)
    lift_pad = jnp.pad(jnp.concatenate([lift16, lift16], axis=1), ((0, 112), (0, 0)))
    first8 = jnp.dot(lift8, pointwise[0].T, precision=PRECISE)
    first = jnp.pad(parity_blocks(first8), ((0, 112), (0, 0)))
    point1 = parity_blocks(pointwise[1])
    proj8 = jnp.pad(project_weight, ((0, 2), (0, 0)))
    proj_t = jnp.pad(parity_blocks(proj8), ((0, 112), (0, 0)))
    norm_count = 6.0 * SX * SY * SZ * plan.shape[0]
    scale = 2.0 / norm_count
    proj_square = jnp.dot(project_weight.T, project_weight, precision=PRECISE) * scale

    def swap(value):
        value = value.reshape(TILES, -1, 128)
        return lax.all_to_all(value, "tile", 0, 0, tiled=True)

    def swap_flat(value):
        return swap(value).reshape(256, 128)

    inputs, pre0 = prepare(pieces, 0, first, True, "prepare_inputs")
    spectrum, a_in, a0 = mode_call(
        modes_first_kernel,
        "modes_first",
        0,
        mode_counts,
        (swap_flat(coef), lift_pad),
        turned,
        ((256, 128), (128, 128), (128, 128)),
        after=(pre0,),
    )
    target, pull = prepare(pieces, 128, proj_t * scale, False, "prepare_target")
    sides, plain_out = (256, BF16), (128, F32)
    coef, h1, slope0 = cell_call(
        cells0_kernel,
        "cells0",
        (swap_flat(spectrum),),
        (pre0,),
        (),
        (sides, plain_out),
        after=(pull,),
    )
    spectrum, a1 = mode_call(
        modes_forward_kernel,
        "modes_forward",
        1,
        mode_counts,
        (swap_flat(coef),),
        turned,
        ((256, 128), (128, 128)),
    )
    coef, grad1, h2 = cell_call(
        cells1_kernel,
        "cells1",
        (swap_flat(spectrum),),
        (h1, pull),
        (point1.T, parity_blocks(proj_square)),
        (sides, sides),
        scratch=(vmem((2, 256, 256), BF16), vmem((BLOCK, 128))),
    )
    point = point_gradient(grad1, h1)
    spectrum, pair1 = mode_call(
        modes_backward_kernel,
        "modes_backward",
        1,
        mode_counts,
        (swap_flat(coef), a1),
        plain,
        ((256, 128), (128, 128)),
        after=(point,),
    )
    extra = proj_gradient(norm_count, h2, target, proj_t.T, point, pair1)
    coef, grad0 = cell_call(
        cells2_kernel,
        "cells2",
        (swap_flat(spectrum), extra),
        (grad1, slope0),
        (point1,),
        (sides,),
        scratch=(vmem((256, 256), BF16),),
        coef=(TILES, 16, 128),
    )
    direct = lax.dot_general(inputs, grad0, TN, preferred_element_type=F32)
    (tail,) = mode_call(
        modes_last_kernel,
        "modes_last",
        0,
        mode_counts,
        (swap(coef), a0, a_in, direct, pair1),
        plain,
        ((264, 128),),
    )
    tails = [tail] + [xor_group(tail, d) for d in range(1, 4)]
    late = swap(spread(tails))
    spectral_grad = outer_products(tails)
    lift_grad, point_grad, proj_grad, loss = finish(late, pointwise[0], lift8)
    return (
        new_fields.reshape(2, 3, 4, 16, 256),
        lift_grad.T,
        point_grad,
        spectral_grad,
        proj_grad,
        loss[0, 0],
    )


def solution(mesh):
    return jax.shard_map(
        local,
        mesh=mesh,
        in_specs=(
            P(None, None, "tile", "role", "rep"),
            P("tile", "role", "rep"),
            P(),
            P(),
            P(),
            P(),
            P(),
            P(),
            P(None, "tile", None, None, None),
            P(),
        ),
        out_specs=(
            P(None, None, "tile", "role", "rep"),
            P(),
            P(),
            P(None, "tile", None, None, None),
            P(),
            P(),
        ),
        check_vma=False,
    )
```

```python
import functools
import math

import jax
import jax.numpy as jnp
import ml_dtypes
import numpy as np
from jax import lax
from jax.experimental import pallas as pl
from jax.experimental.pallas import tpu as pltpu
from jax.sharding import PartitionSpec as P

STEPS = 4
MODES = 8
LAYERS = 2
STEP_TIME = 0.5
PRECISE = lax.Precision.HIGHEST
F32 = jnp.float32
BF16 = jnp.bfloat16
NN = (((1,), (0,)), ((), ()))
NT = (((1,), (1,)), ((), ()))
TN = (((0,), (0,)), ((), ()))
ROOM = 48 * 1024 * 1024
LEAP_ROOM = 40 * 1024 * 1024
CELL_ROOM = 56 * 1024 * 1024
MODE_ROOM = 48 * 1024 * 1024
GROUP = ("role", "rep")
EVERY = ("role", "rep", "tile")
SX, SY, SZ = 64, 16, 256
CELLS = SY * SZ
TILES = 32


def basis(length):
    frequency = np.arange(MODES)[:, None]
    position = np.arange(length)[None, :]
    angles = 2.0 * np.pi * ((frequency * position) % length) / length
    return np.concatenate([np.cos(angles), np.sin(angles)], axis=0) * math.sqrt(2.0 / length)


def split_const(table):
    table = table.astype(np.float32)
    high = table.astype(ml_dtypes.bfloat16)
    low = (table - high.astype(np.float32)).astype(ml_dtypes.bfloat16)
    return high, low


def both_const(table):
    return np.stack(split_const(table))


TABLE_X, TABLE_Y, TABLE_Z = basis(SX), basis(SY), basis(SZ)
KRON_X = both_const(
    np.einsum("ptx,mn->xmptn", TABLE_X.reshape(16, TILES, 2), np.eye(8)).reshape(256, 256)
)
KRON_XT = np.ascontiguousarray(KRON_X.transpose(0, 2, 1))
KRON_Y = both_const(np.einsum("jy,kl->jkyl", TABLE_Y, np.eye(16)).reshape(256, 256))
KRON_YT = np.ascontiguousarray(KRON_Y.transpose(0, 2, 1))
Z_HIGH, Z_LOW = split_const(TABLE_Z)
Z_ROWS = np.concatenate([Z_HIGH, Z_LOW], axis=0)
Z_COLS = np.concatenate([Z_HIGH.T, Z_HIGH.T, Z_LOW.T], axis=1)
Z_HALF = np.stack([Z_ROWS[:, r * 128 : r * 128 + 128] for r in range(2)])
POOL_Z = np.kron(np.eye(128), np.full((2, 1), 0.125)).astype(np.float32)


def halves(value):
    high = value.astype(BF16)
    return high, (value - high.astype(F32)).astype(BF16)


def dot(a, b, dims=NN):
    return lax.dot_general(a, b, dims, preferred_element_type=F32)


def dot3(a, b, dims=NN):
    return dot(a[0], b[0], dims) + dot(a[0], b[1], dims) + dot(a[1], b[0], dims)


def lanes_of(shape):
    return lax.broadcasted_iota(jnp.int32, shape, len(shape) - 1)


def rows_of(shape):
    return lax.broadcasted_iota(jnp.int32, shape, len(shape) - 2)


def square_weight(matrix):
    high, low = halves(matrix)
    one = jnp.concatenate([high, low], axis=1)
    return jnp.concatenate([one, one], axis=0)


def rows_times(value, weight):
    high, low = halves(value)
    out = dot(jnp.concatenate([high, low], axis=1), weight)
    return out[:, :128] + out[:, 128:]


def vmem(shape, dtype=F32):
    return pltpu.VMEM(shape, dtype)


def params(room=ROOM):
    return pltpu.CompilerParams(vmem_limit_bytes=room)


def full(shape):
    return pl.BlockSpec(shape, lambda *_: (0,) * len(shape))


SMEM = pl.BlockSpec(memory_space=pltpu.SMEM)
ANY = pl.BlockSpec(memory_space=pl.ANY)


def call(kernel, ins, outs, after=(), carry=(), room=ROOM, **options):
    first, last = len(ins) + len(after), len(ins) + len(after) + len(carry)

    def run(*refs):
        rest = refs[last:]
        kernel(*refs[: len(ins)], *rest[: len(outs)], *rest[len(outs) + len(carry) :])

    return pl.pallas_call(
        run,
        out_shape=[o[0] for o in outs] + [jax.ShapeDtypeStruct(c.shape, c.dtype) for c in carry],
        in_specs=[i[1] for i in ins] + [ANY] * (len(after) + len(carry)),
        out_specs=[o[1] for o in outs] + [ANY] * len(carry),
        input_output_aliases={first + n: len(outs) + n for n in range(len(carry))},
        compiler_params=params(room),
        **options,
    )(*[i[0] for i in ins], *after, *carry)


def shape_of(*shape):
    return jax.ShapeDtypeStruct(shape, F32)


ONLY_AFTER = [(0, 3), (3, 3), (4, 3), (5, 3), (6, 3)]
ONLY_BEFORE = [(6, 0), (3, 0)]
PLANES = [(c, i) for c in range(7) for i in range(4)]
PLANES = (
    ONLY_AFTER + [p for p in PLANES if p not in ONLY_AFTER and p not in ONLY_BEFORE] + ONLY_BEFORE
)
FIRST, LAST = len(ONLY_AFTER), len(PLANES) - len(ONLY_BEFORE)


def ends_kernel(fields, material, ends, left, right):
    left[...] = jnp.zeros_like(left)
    right[...] = jnp.zeros_like(right)
    for c in range(7):
        rows = slice(c * 64, (c + 1) * 64)
        own = (fields[c] if c < 6 else material[...].astype(F32)).reshape(64, 256)
        left[rows, :] = own[:, 0:128]
        right[rows, :] = own[:, 128:256]
    for b in range(4):
        rows = slice(b * 128, (b + 1) * 128)
        first = jnp.transpose(left[rows, :])[0:8]
        last = jnp.transpose(right[rows, :])[120:128]
        at, lanes = b // 2 * 8, slice(b % 2 * 128, b % 2 * 128 + 128)
        ends[at : at + 8, lanes] = jnp.where(rows_of((8, 128)) < 4, first, last)


def ends_along_z(fields, material):
    return pl.pallas_call(
        ends_kernel,
        out_shape=shape_of(16, 256),
        scratch_shapes=[vmem((512, 128)), vmem((512, 128))],
        compiler_params=params(),
        name="ends",
    )(fields, material)


def pack_kernel(fields, material, ends, packed, after, before):
    for n, (c, i) in enumerate(PLANES):
        plane = fields[c, i] if c < 6 else material[i].astype(F32)
        packed[n] = plane
        if n < LAST:
            after[n] = plane
        if n >= FIRST:
            before[n - FIRST] = plane
    for out in (packed, after, before):
        out[out.shape[0] - 1] = ends[...]


def pack(fields, material, ends):
    count = len(PLANES)
    return pl.pallas_call(
        pack_kernel,
        out_shape=[
            shape_of(count + 1, 16, 256),
            shape_of(LAST + 1, 16, 256),
            shape_of(count - FIRST + 1, 16, 256),
        ],
        compiler_params=params(),
        name="pack",
    )(fields, material, ends)


def here():
    return lax.axis_index("role"), lax.axis_index("rep"), lax.axis_index("tile")


def leap_kernel(
    plan,
    permittivity,
    conductivity,
    own0,
    own1,
    low0,
    low1,
    high0,
    high1,
    pool,
    out_fields,
    out_piece0,
    out_piece1,
    out_piece2,
    out_piece3,
    grid_f,
    keep,
    gain,
    dt_mask,
    edge0,
    edge1,
    sums0,
    sums1,
    reduced,
    staged,
):
    role, rep, tile = here()
    shape8 = (8, 384)
    row8 = rows_of(shape8)
    top = jnp.where((row8 < 4) & (role == 0), 1.0, 0.0)
    bottom = jnp.where((row8 >= 4) & (role == 1), 1.0, 0.0)

    def column(planes, edge):
        ends = planes[planes.shape[0] - 1]
        strip = jnp.concatenate([ends[0:8], ends[8:16]], axis=1)
        row = rows_of((8, 512))
        first = jnp.where((row < 4) & (rep == 0), strip, 0.0)
        last = jnp.where((row >= 4) & (rep == 1), strip, 0.0)
        whole = jnp.concatenate([first, jnp.zeros((112, 512), F32), last], axis=0)
        for b in range(4):
            edge[b * 128 : (b + 1) * 128, :] = jnp.transpose(whole[:, b * 128 : (b + 1) * 128])

    for number, (mine, mate) in enumerate(((low0, low1), (own0, own1), (high0, high1))):
        column(mine, edge0)
        column(mate, edge1)

        for c in range(7):
            for i in range(4):
                n = PLANES.index((c, i)) - (FIRST if number == 2 else 0)
                if not 0 <= n < mine.shape[0] - 1:
                    grid_f[c, 4 * number + i] = jnp.zeros((24, 384), F32)
                    continue
                rows = slice((c * 4 + i) * 16, (c * 4 + i + 1) * 16)
                plane = jnp.concatenate([mine[n], edge0[rows, :]], axis=1)
                other = jnp.concatenate([mate[n], edge1[rows, :]], axis=1)
                halo = other[0:8] * top + other[8:16] * bottom
                grid_f[c, 4 * number + i] = jnp.concatenate([plane, halo], axis=0)

    row = rows_of((24, 384))
    lane = lanes_of((24, 384))
    row_ok = (row < 16) | ((row < 20) & (role == 0)) | ((row >= 20) & (role == 1))
    lane_ok = (lane < 256) | ((lane < 320) & (rep == 0)) | ((lane >= 320) & (rep == 1))
    inside = jnp.where(row_ok & lane_ok, 1.0, 0.0)
    dt_mask[...] = inside * STEP_TIME
    below = jnp.where(tile > 0, 1.0, 0.0)
    above = jnp.where(tile < TILES - 1, 1.0, 0.0)

    def media(p, carry):
        kind = grid_f[6, p]
        level = inside * jnp.where(p >= 8, above, 1.0)

        def choose(values):
            return jnp.where(
                kind < 0.5,
                values[0],
                jnp.where(kind < 1.5, values[1], jnp.where(kind < 2.5, values[2], values[3])),
            )

        permit = choose(permittivity)
        damping = choose(conductivity) * (0.5 * STEP_TIME) / permit
        keep[p] = (1.0 - damping) / (1.0 + damping)
        gain[p] = STEP_TIME / (permit * (1.0 + damping)) * level
        return carry

    lax.fori_loop(1, 11, media, 0, unroll=2)

    def back(value, axis):
        return pltpu.roll(value, value.shape[axis] - 1, axis)

    def step_h(p, carry):
        ex, ey, ez = grid_f[0, p], grid_f[1, p], grid_f[2, p]
        s = dt_mask[...] * below if p < 4 else dt_mask[...]
        d_zy = back(ez, 0) - ez
        d_yz = back(ey, 1) - ey
        d_xz = back(ex, 1) - ex
        d_zx = grid_f[2, p + 1] - ez
        d_yx = grid_f[1, p + 1] - ey
        d_xy = back(ex, 0) - ex
        grid_f[3, p] = grid_f[3, p] - s * (d_zy - d_yz)
        grid_f[4, p] = grid_f[4, p] - s * (d_xz - d_zx)
        grid_f[5, p] = grid_f[5, p] - s * (d_yx - d_xy)
        return carry

    def step_e(p, carry):
        hx, hy, hz = grid_f[3, p], grid_f[4, p], grid_f[5, p]
        k, g = keep[p], gain[p]
        d_zy = hz - pltpu.roll(hz, 1, 0)
        d_yz = hy - pltpu.roll(hy, 1, 1)
        d_xz = hx - pltpu.roll(hx, 1, 1)
        d_zx = hz - grid_f[5, p - 1]
        d_yx = hy - grid_f[4, p - 1]
        d_xy = hx - pltpu.roll(hx, 1, 0)
        grid_f[0, p] = k * grid_f[0, p] + g * (d_zy - d_yz)
        grid_f[1, p] = k * grid_f[1, p] + g * (d_xz - d_zx)
        grid_f[2, p] = k * grid_f[2, p] + g * (d_yx - d_xy)
        return carry

    sums0[...] = jnp.zeros_like(sums0)
    sums1[...] = jnp.zeros_like(sums1)
    for step in range(STEPS):
        for p in range(step, 11 - step):
            step_h(p, 0)
        for p in range(1 + step, 11 - step):
            step_e(p, 0)
        for x in range(2):
            for c in range(6):
                at = (x * 8 + c) * 16
                pair = grid_f[c, 4 + 2 * x, 0:16, 0:256] + grid_f[c, 5 + 2 * x, 0:16, 0:256]
                sums0[at : at + 16, :] = pair[:, 0:128]
                sums1[at : at + 16, :] = pair[:, 128:256]
        for part, sums in enumerate((sums0, sums1)):
            staged[:, part * 128 : (part + 1) * 128] = (
                sums[pl.ds(0, 128, stride=2), :] + sums[pl.ds(1, 128, stride=2), :]
            )
        reduced[step] = lax.dot_general(
            staged[...], pool[...], NN, precision=PRECISE, preferred_element_type=F32
        )
    for c in range(6):
        out_fields[c] = grid_f[c, 4:8, 0:16, 0:256]

    me = role * 2 + rep
    for d, out in enumerate((out_piece0, out_piece1, out_piece2, out_piece3)):
        out[0:128] = reduced[plan[me ^ d] - 1]
        out[128:256] = reduced[STEPS - 1]


def leapfrog(plan, permittivity, conductivity, blocks):
    whole = pl.BlockSpec(memory_space=pltpu.VMEM)
    return call(
        leap_kernel,
        [(v, SMEM) for v in (plan, permittivity, conductivity)]
        + [(v, whole) for v in (*blocks, jnp.asarray(POOL_Z))],
        [
            (shape_of(6, 4, 16, 256), whole),
        ]
        + [(shape_of(256, 128), whole)] * 4,
        room=LEAP_ROOM,
        scratch_shapes=[
            vmem((7, 12, 24, 384)),
            vmem((12, 24, 384)),
            vmem((12, 24, 384)),
            vmem((24, 384)),
            vmem((512, 128)),
            vmem((512, 128)),
            vmem((256, 128)),
            vmem((256, 128)),
            vmem((4, 128, 128)),
            vmem((128, 256)),
        ],
        name="leapfrog",
    )


def fold(value):
    return value[:, 0:128] + value[:, 128:256]


def coef_kernel(piece0, piece1, piece2, piece3, z_half, kron, out, d_scr):
    role, rep, _ = here()
    lane = lanes_of((16, 128))
    for flip, (one, other) in enumerate(((piece0, piece1), (piece2, piece3))):
        total = jnp.zeros((16, 128), F32)
        for z_rows, piece in ((z_half[rep], one), (z_half[1 - rep], other)):
            high, low = halves(
                jnp.concatenate([piece[pl.ds(y, 16, stride=8), :] for y in range(8)], axis=0)
            )
            out_high = dot(z_rows, high, NT)
            total = total + out_high[0:16] + out_high[16:32] + dot(z_rows[0:16], low, NT)
        for y in range(8):
            own = total if y == 0 else pltpu.roll(total, 128 - 16 * y, 1)
            at = pl.multiple_of(((role ^ flip) * 8 + y) * 16, 16)
            d_scr[pl.ds(at, 16), :] = jnp.where(lane < 16, own, 0.0)
    out[...] = dot3((kron[0], kron[1]), halves(d_scr[...]))


def input_coefs(pieces):
    return pl.pallas_call(
        coef_kernel,
        out_shape=shape_of(256, 128),
        scratch_shapes=[vmem((256, 128))],
        compiler_params=params(),
        name="input_coefs",
    )(*pieces, jnp.asarray(Z_HALF), jnp.asarray(KRON_Y))


def prep_kernel(first_row, piece0, piece1, piece2, piece3, weight, out_own, out_mixed):
    role_here, rep_here, _ = here()
    me = role_here * 2 + rep_here
    wide = square_weight(weight[...])
    lane = lanes_of((128, 128))
    for d, piece in enumerate((piece0, piece1, piece2, piece3)):
        source = me ^ d
        role, rep = source // 2, source % 2
        whole = jnp.concatenate(
            [piece[pl.ds(first_row + y, 16, stride=8), :] for y in range(8)], axis=0
        )
        turned = jnp.transpose(whole)
        for y in range(8):
            rows = pl.ds(pl.multiple_of((role * 8 + y) * 256 + rep * 128, 128), 128)
            own = turned if y == 0 else pltpu.roll(turned, 128 - 16 * y, 1)
            own = jnp.where(lane < 16, own, 0.0)
            sides = jnp.concatenate(halves(own), axis=1)
            out_own[rows, :] = sides if out_own.dtype == BF16 else own
            out_mixed[rows, :] = fold(dot(sides, wide))


def prepare(pieces, first_row, weight, as_sides, name):
    own = jax.ShapeDtypeStruct((CELLS, 256), BF16) if as_sides else shape_of(CELLS, 128)
    return pl.pallas_call(
        functools.partial(prep_kernel, first_row),
        out_shape=[own, shape_of(CELLS, 128)],
        compiler_params=params(),
        name=name,
    )(*pieces, weight)


GELU_A = math.sqrt(2.0 / math.pi)
GELU_B = 0.044715


def gelu_both(value):
    square = value * value
    t = jnp.tanh(value * (GELU_A + (GELU_A * GELU_B) * square))
    half = 0.5 + 0.5 * t
    hidden = value * half
    slope = half + hidden * (1.0 - half) * (2.0 * GELU_A + (6.0 * GELU_A * GELU_B) * square)
    return hidden, slope


BLOCK_Y = 8
BLOCK = BLOCK_Y * SZ
CHUNK = 128


def open_cells(spectrum, kron_t, c_scr):
    high, low = halves(dot3((kron_t[0], kron_t[1]), halves(spectrum[...])))
    for y in range(SY):
        lanes = slice(y % BLOCK_Y * 128, y % BLOCK_Y * 128 + 128)
        rows = slice(y * 16, y * 16 + 16)
        c_scr[y // BLOCK_Y, 0:16, lanes] = high[rows]
        c_scr[y // BLOCK_Y, 16:32, lanes] = low[rows]
        c_scr[y // BLOCK_Y, 32:48, lanes] = high[rows]


def chunk_of(wide, n):
    at = n * CHUNK
    return wide[at % SZ : at % SZ + CHUNK, at // SZ * 128 : at // SZ * 128 + 128]


def store_sides(out, rows, value):
    high, low = halves(value)
    out[rows, 0:128] = high
    out[rows, 128:256] = low


def cells_to(sides, z_rows, d_scr, step):
    for n in range(BLOCK_Y):
        out = dot(z_rows[...], sides[n * SZ : (n + 1) * SZ, :])
        at = pl.multiple_of((step * BLOCK_Y + n) * 16, 16)
        d_scr[pl.ds(at, 16), :] = out[0:16, 0:128] + out[0:16, 128:256] + out[16:32, 0:128]


def close_cells(kron, d_scr):
    return dot3((kron[0], kron[1]), halves(d_scr[...]))


def cells0_kernel(spectrum, pre, kron, kron_t, z_rows, z_cols, out_coef, out_h, out_slope, c_scr, d_scr):
    step = pl.program_id(0)

    @pl.when(step == 0)
    def _():
        open_cells(spectrum, kron_t, c_scr)

    spectral = dot(z_cols[...], c_scr[step])
    for n in range(BLOCK // CHUNK):
        rows = slice(n * CHUNK, (n + 1) * CHUNK)
        hidden, slope = gelu_both(chunk_of(spectral, n) + pre[rows, :])
        out_slope[rows, :] = slope
        store_sides(out_h, rows, hidden)
    cells_to(out_h, z_rows, d_scr, step)

    @pl.when(step == pl.num_programs(0) - 1)
    def _():
        out_coef[...] = close_cells(kron, d_scr)


def cells1_kernel(
    spectrum,
    h1,
    pull,
    w_point,
    w_square,
    kron,
    kron_t,
    z_rows,
    z_cols,
    out_coef,
    out_pre,
    out_h,
    c_scr,
    d_scr,
    wide,
    slopes,
):
    step = pl.program_id(0)

    @pl.when(step == 0)
    def _():
        open_cells(spectrum, kron_t, c_scr)
        wide[0] = square_weight(w_point[...])
        wide[1] = square_weight(w_square[...])

    spectral = dot(z_cols[...], c_scr[step])
    direct = dot(h1[...], wide[0])
    for n in range(BLOCK // CHUNK):
        rows = slice(n * CHUNK, (n + 1) * CHUNK)
        hidden, slope = gelu_both(chunk_of(spectral, n) + fold(direct[rows, :]))
        slopes[rows, :] = slope
        store_sides(out_h, rows, hidden)
    back = dot(out_h[...], wide[1])
    for n in range(BLOCK // CHUNK):
        rows = slice(n * CHUNK, (n + 1) * CHUNK)
        store_sides(out_pre, rows, (fold(back[rows, :]) - pull[rows, :]) * slopes[rows, :])
    cells_to(out_pre, z_rows, d_scr, step)

    @pl.when(step == pl.num_programs(0) - 1)
    def _():
        out_coef[...] = close_cells(kron, d_scr)


def cells2_kernel(
    spectrum,
    extra,
    grad1,
    slope0,
    w_point,
    kron,
    kron_t,
    z_rows,
    z_cols,
    out_coef,
    out_pre,
    c_scr,
    d_scr,
    wide,
):
    step = pl.program_id(0)

    @pl.when(step == 0)
    def _():
        open_cells(spectrum, kron_t, c_scr)
        wide[...] = square_weight(w_point[...])

    spectral = dot(z_cols[...], c_scr[step])
    direct = dot(grad1[...], wide[...])
    for n in range(BLOCK // CHUNK):
        rows = slice(n * CHUNK, (n + 1) * CHUNK)
        store_sides(
            out_pre, rows, (chunk_of(spectral, n) + fold(direct[rows, :])) * slope0[rows, :]
        )
    cells_to(out_pre, z_rows, d_scr, step)

    @pl.when(step == pl.num_programs(0) - 1)
    def _():
        out_coef[:, 0:8, :] = close_cells(kron, d_scr).reshape(TILES, 8, 128)
        out_coef[:, 8:16, :] = extra[...]


def cell_call(kernel, name, firsts, streams, weights, outs, scratch=(), coef=(256, 128), **order):
    def block(lanes):
        return pl.BlockSpec((BLOCK, lanes), lambda g: (g, 0))

    consts = [jnp.asarray(c) for c in (KRON_Y, KRON_YT, Z_ROWS, Z_COLS)]
    return call(
        kernel,
        [(v, full(v.shape)) for v in firsts]
        + [(v, block(v.shape[1])) for v in streams]
        + [(v, full(v.shape)) for v in (*weights, *consts)],
        [(shape_of(*coef), full(coef))]
        + [(jax.ShapeDtypeStruct((CELLS, lanes), kind), block(lanes)) for lanes, kind in outs],
        grid=(SY // BLOCK_Y,),
        scratch_shapes=[vmem((SY // BLOCK_Y, 48, BLOCK_Y * 128), BF16), vmem((256, 128))] + list(scratch),
        name=name,
        room=CELL_ROOM,
        **order,
    )


SIDES = pl.BlockSpec((BLOCK, 256), lambda g: (g, 0))


def point_grad_kernel(grad, h1, out, acc):
    step = pl.program_id(0)
    acc[step] = dot(grad[...], h1[...], TN)

    @pl.when(step == pl.num_programs(0) - 1)
    def _():
        point = sum(acc[n, 0:128, :] + acc[n, 128:256, :] for n in range(SY // BLOCK_Y))
        point = fold(point)
        picked = jnp.where(lanes_of((64, 128)) < 64, point[0:64], point[64:128])
        picked = picked + pltpu.roll(picked, 64, 1)
        out[...] = jnp.where(lanes_of((32, 128)) < 64, picked[0:32], picked[32:64])


def point_gradient(grad, h1):
    (out,) = call(
        point_grad_kernel,
        [(grad, SIDES), (h1, SIDES)],
        [(shape_of(32, 128), full((32, 128)))],
        grid=(SY // BLOCK_Y,),
        scratch_shapes=[vmem((SY // BLOCK_Y, 256, 256))],
        name="point_grad",
    )
    return out


def proj_grad_kernel(scale, norm, h2, target, w_proj, point, out, acc, loss_acc, wide, row):
    step = pl.program_id(0)

    @pl.when(step == 0)
    def _():
        wide[...] = square_weight(w_proj[...])
        loss_acc[...] = jnp.zeros_like(loss_acc)

    err = fold(dot(h2[...], wide[...])) - target[...]
    loss_acc[...] += jnp.sum((err * err).reshape(BLOCK // 8, 8, 128), axis=0)
    sides = jnp.concatenate(halves(err * scale), axis=1)
    acc[step] = dot(sides, h2[...], TN)

    @pl.when(step == pl.num_programs(0) - 1)
    def _():
        out[...] = jnp.zeros_like(out)
        out[:, 0, :] = point[...]
        proj = sum(acc[n, 0:16, :] + acc[n, 128:144, :] for n in range(SY // BLOCK_Y))
        proj = fold(proj)
        picked = jnp.where(lanes_of((8, 128)) < 64, proj[0:8], proj[8:16])
        turned = jnp.transpose(picked + pltpu.roll(picked, 64, 1))
        row[...] = jnp.full((32, 128), jnp.sum(loss_acc[...]) / norm)
        row[:, 0:8] = turned[0:32]
        row[:, 8:16] = turned[32:64]
        out[:, 1, :] = row[...]


def proj_gradient(norm, h2, target, w_proj, point, after):
    (out,) = call(
        functools.partial(proj_grad_kernel, 2.0 / norm, norm),
        [
            (h2, SIDES),
            (target, pl.BlockSpec((BLOCK, 128), lambda g: (g, 0))),
            (w_proj, full((128, 128))),
            (point, full((32, 128))),
        ],
        [(shape_of(TILES, 8, 128), full((TILES, 8, 128)))],
        after=(after,),
        grid=(SY // BLOCK_Y,),
        scratch_shapes=[
            vmem((SY // BLOCK_Y, 256, 256)),
            vmem((8, 128)),
            vmem((256, 256), BF16),
            vmem((32, 128)),
        ],
        name="proj_grad",
    )
    return out


def kept_modes(counts, layer):
    row = rows_of((128, 128))
    pair = lax.axis_index("tile") * 8 + row // 16
    kept = (
        (row % 8 < counts[layer, 0])
        & (pair // 16 % 8 < counts[layer, 1])
        & (pair % 8 < counts[layer, 2])
    )
    return jnp.where(kept, 1.0, 0.0)


def pair_up(rows, low_lanes):
    picked = jnp.where(low_lanes, rows[0:128], rows[128:256])
    return picked + pltpu.roll(picked, 64, 1)


MIX_STEPS = 2
MIX_PAIRS = 8 // MIX_STEPS


def mix(g_scr, b_scr, weights, step):
    row, lane = rows_of((16, 256)), lanes_of((16, 256))
    low = lanes_of((16, 128)) < 64
    for n in range(MIX_PAIRS):
        at = pl.multiple_of((step * MIX_PAIRS + n) * 16, 16)
        one = g_scr[pl.ds(at, 16), :]
        wide = jnp.concatenate([one, one], axis=1)
        total = jnp.zeros((32, 128), F32)
        for q in range(4):
            own = jnp.where(row == 4 * q + lane // 64, wide, 0.0)
            sides = jnp.concatenate(halves(own), axis=0)
            both = halves(weights[n, q * 256 : (q + 1) * 256, :])
            total = total + dot(sides, jnp.concatenate(both, axis=1))
        folded = total[0:16] + jnp.where(low, total[16:32], 0.0)
        b_scr[pl.ds(at, 16), :] = folded + pltpu.roll(folded, 64, 1)


def close_modes(b_scr, kept, kron_t, out):
    both = b_scr[...] * kept
    low = lanes_of((128, 128)) < 64
    blocks = jnp.concatenate([jnp.where(low, both, 0.0), jnp.where(low, 0.0, both)], axis=0)
    out[...] = dot3((kron_t[0], kron_t[1]), halves(blocks))


def modes_first_kernel(counts, coef, lift, weights, kron, kron_t, out, out_in, out_a, a_scr, b_scr):
    step = pl.program_id(0)

    @pl.when(step == 0)
    def _():
        rows = dot3((kron[0], kron[1]), halves(coef[...]))
        picked = jnp.where(lanes_of((128, 128)) < 8, rows[0:128], rows[128:256])
        picked = picked * kept_modes(counts, 0)
        out_in[...] = picked
        lifted = dot3(halves(picked), halves(lift[...]))
        a_scr[...] = lifted
        out_a[...] = lifted

    mix(a_scr, b_scr, weights, step)

    @pl.when(step == pl.num_programs(0) - 1)
    def _():
        close_modes(b_scr, kept_modes(counts, 0), kron_t, out)


def modes_forward_kernel(counts, coef, weights, kron, kron_t, out, out_a, a_scr, b_scr):
    step = pl.program_id(0)

    @pl.when(step == 0)
    def _():
        rows = dot3((kron[0], kron[1]), halves(coef[...]))
        a = pair_up(rows, lanes_of((128, 128)) < 64) * kept_modes(counts, 1)
        a_scr[...] = a
        out_a[...] = a

    mix(a_scr, b_scr, weights, step)

    @pl.when(step == pl.num_programs(0) - 1)
    def _():
        close_modes(b_scr, kept_modes(counts, 1), kron_t, out)


def take_gradient(rows, kept, saved, g_scr, out_pair):
    low = lanes_of((128, 128)) < 64
    g = pair_up(rows, low) * kept
    g_scr[...] = g
    out_pair[...] = jnp.where(low, g, saved[...])


def modes_backward_kernel(
    counts, coef, saved, weights, kron, kron_t, out, out_pair, g_scr, b_scr
):
    step = pl.program_id(0)

    @pl.when(step == 0)
    def _():
        rows = dot3((kron[0], kron[1]), halves(coef[...]))
        take_gradient(rows, kept_modes(counts, 1), saved, g_scr, out_pair)

    mix(g_scr, b_scr, weights, step)

    @pl.when(step == pl.num_programs(0) - 1)
    def _():
        close_modes(b_scr, kept_modes(counts, 1), kron_t, out)


def modes_last_kernel(
    counts, coef, saved, inputs, point, pair1, weights, kron, kron_t, out, g_scr, b_scr
):
    step = pl.program_id(0)

    @pl.when(step == 0)
    def _():
        value = coef[:, 0:8, :].reshape(256, 128)
        rows = dot3((kron[0], kron[1]), halves(value))
        take_gradient(rows, kept_modes(counts, 0), saved, g_scr, out.at[8:136])
        out[136:264] = pair1[...]

    mix(g_scr, b_scr, weights, step)

    @pl.when(step == pl.num_programs(0) - 1)
    def _():
        turned = jnp.transpose(inputs[...])[0:16]
        lift = dot3(halves(turned), halves(b_scr[...]))
        lift = lift[0:8] + lift[8:16]
        direct = fold(point[0:16, :] + point[128:144, :])
        direct = direct[0:8] + pltpu.roll(direct[8:16], 64, 1)
        late = jnp.where(lanes_of((8, 128)) < 64, lift, pltpu.roll(direct, 64, 1))
        extra = pltpu.roll(jnp.sum(coef[:, 8:16, :], axis=0), 6, 0)
        out[0:8] = jnp.where(rows_of((8, 128)) < 6, late, extra)


def mode_call(kernel, name, layer, counts, smalls, weights, outs, **order):
    consts = [jnp.asarray(c) for c in (KRON_X, KRON_XT)]
    return call(
        kernel,
        [(counts, SMEM)]
        + [(v, full(v.shape)) for v in smalls]
        + [(weights, pl.BlockSpec((None, MIX_PAIRS, 1024, 64), lambda m: (layer, m, 0, 0)))]
        + [(v, full(v.shape)) for v in consts],
        [(shape_of(*o), full(o)) for o in outs],
        grid=(MIX_STEPS,),
        scratch_shapes=[vmem((128, 128)), vmem((128, 128))],
        name=name,
        room=MODE_ROOM,
        **order,
    )


OUTER_PAIRS = 4


def outer_kernel(tail0, tail1, tail2, tail3, out):
    layer, part = pl.program_id(0), pl.program_id(1)
    row, lane = rows_of((64, 1024)), lanes_of((64, 1024))
    own = row % 16 == lane // 64
    low = lanes_of((64, 128)) < 64
    for n in range(OUTER_PAIRS):
        at = pl.multiple_of(8 + layer * 128 + (part * OUTER_PAIRS + n) * 16, 8)
        block = jnp.concatenate([t[pl.ds(at, 16), :] for t in (tail0, tail1, tail2, tail3)], axis=0)
        grads = halves(jnp.transpose(block)[0:64])
        twice = jnp.where(low, pltpu.roll(block, 64, 1), block)
        spread = halves(jnp.where(own, jnp.concatenate([twice] * 8, axis=1), 0.0))
        result = dot3(grads, spread)
        for r in range(16):
            out[n, r] = result[:, r * 64 : (r + 1) * 64]


def outer_products(tails):
    return pl.pallas_call(
        outer_kernel,
        grid=(LAYERS, 8 // OUTER_PAIRS),
        out_shape=shape_of(LAYERS, 8, 16, 64, 64),
        in_specs=[full((264, 128))] * 4,
        out_specs=pl.BlockSpec((None, OUTER_PAIRS, 16, 64, 64), lambda l, m: (l, m, 0, 0, 0)),
        compiler_params=params(),
        name="outer",
    )(*tails)


def spread_kernel(tail0, tail1, tail2, tail3, out):
    late = (tail0[...] + tail1[...]) + (tail2[...] + tail3[...])
    out[...] = jnp.broadcast_to(late[None], (TILES, 8, 128))


def spread(tails):
    return pl.pallas_call(
        spread_kernel,
        grid=(1,),
        out_shape=shape_of(TILES, 8, 128),
        in_specs=[pl.BlockSpec((8, 128), lambda n: (0, 0))] * 4,
        out_specs=full((TILES, 8, 128)),
        compiler_params=params(),
        name="spread",
    )(*tails)


def finish_kernel(late, point, lift, out_lift, out_point, out_proj, out_loss):
    by_tile = late[...]
    total = jnp.where(rows_of((8, 128)) < 6, jnp.sum(by_tile, axis=0), 0.0)
    through, direct = total[:, 0:64], pltpu.roll(total, 64, 1)[:, 0:64]

    def exact(a, b, dims):
        return lax.dot_general(a, b, dims, precision=PRECISE, preferred_element_type=F32)

    out_point[0] = exact(direct, lift[...], TN)
    through = through + exact(direct, point[...], NN)
    out_lift[...] = through[0:6]
    first = by_tile[:, 6, :]
    out_point[1, 0:32, :] = first[:, 0:64]
    out_point[1, 32:64, :] = first[:, 64:128]
    second = jnp.transpose(by_tile[:, 7, :])
    out_proj[:, 0:32] = second[0:6]
    out_proj[:, 32:64] = second[8:14]
    out_loss[...] = second[16:17, 0:1]


def finish(late, point, lift):
    return pl.pallas_call(
        finish_kernel,
        out_shape=[shape_of(6, 64), shape_of(2, 64, 64), shape_of(6, 64), shape_of(1, 1)],
        compiler_params=params(),
        name="finish",
    )(late, point, lift)


def passed(value, axis, by):
    length = lax.axis_size(axis)
    return lax.ppermute(value, axis, [(i, i + by) for i in range(length) if 0 <= i + by < length])


def across(value, axis):
    return lax.ppermute(value, axis, [(0, 1), (1, 0)])


def xor_group(value, d):
    return lax.ppermute(value, GROUP, [(i, i ^ d) for i in range(4)])


def parity_blocks(matrix):
    zero = jnp.zeros_like(matrix)
    return jnp.concatenate(
        [jnp.concatenate([matrix, zero], axis=1), jnp.concatenate([zero, matrix], axis=1)], axis=0
    )


def local(
    fields,
    material,
    permittivity,
    conductivity,
    plan,
    mode_counts,
    lift_weight,
    pointwise,
    spectral_weight,
    project_weight,
):
    plain = spectral_weight.reshape(LAYERS, 8, 1024, 64)
    turned = jnp.swapaxes(spectral_weight, -1, -2).reshape(LAYERS, 8, 1024, 64)

    fields6 = fields.reshape(6, 4, 16, 256)
    ends = xor_group(ends_along_z(fields6, material), 1)
    own0, after, before = pack(fields6, material, ends)
    low0, high0 = passed(after, "tile", 1), passed(before, "tile", -1)
    low0, high0 = call(lambda *refs: None, [], [], after=(turned,), carry=(low0, high0), name="hold")
    blocks = []
    for value in (own0, low0, high0):
        blocks += [value, across(value, "role")]
    new_fields, *pieces = leapfrog(plan, permittivity, conductivity, blocks)
    pieces = [pieces[0]] + [xor_group(pieces[d], d) for d in range(1, 4)]
    coef = input_coefs(pieces)

    lift8 = jnp.pad(lift_weight.T, ((0, 2), (0, 0)))
    lift16 = jnp.concatenate([lift8, lift8], axis=0)
    lift_pad = jnp.pad(jnp.concatenate([lift16, lift16], axis=1), ((0, 112), (0, 0)))
    first8 = jnp.dot(lift8, pointwise[0].T, precision=PRECISE)
    first = jnp.pad(parity_blocks(first8), ((0, 112), (0, 0)))
    point1 = parity_blocks(pointwise[1])
    proj8 = jnp.pad(project_weight, ((0, 2), (0, 0)))
    proj_t = jnp.pad(parity_blocks(proj8), ((0, 112), (0, 0)))
    norm_count = 6.0 * SX * SY * SZ * plan.shape[0]
    scale = 2.0 / norm_count
    proj_square = jnp.dot(project_weight.T, project_weight, precision=PRECISE) * scale

    def swap(value):
        value = value.reshape(TILES, -1, 128)
        return lax.all_to_all(value, "tile", 0, 0, tiled=True)

    def swap_flat(value):
        return swap(value).reshape(256, 128)

    inputs, pre0 = prepare(pieces, 0, first, True, "prepare_inputs")
    spectrum, a_in, a0 = mode_call(
        modes_first_kernel,
        "modes_first",
        0,
        mode_counts,
        (swap_flat(coef), lift_pad),
        turned,
        ((256, 128), (128, 128), (128, 128)),
        after=(pre0,),
    )
    target, pull = prepare(pieces, 128, proj_t * scale, False, "prepare_target")
    sides, plain_out = (256, BF16), (128, F32)
    coef, h1, slope0 = cell_call(
        cells0_kernel,
        "cells0",
        (swap_flat(spectrum),),
        (pre0,),
        (),
        (sides, plain_out),
        after=(pull,),
    )
    spectrum, a1 = mode_call(
        modes_forward_kernel,
        "modes_forward",
        1,
        mode_counts,
        (swap_flat(coef),),
        turned,
        ((256, 128), (128, 128)),
    )
    coef, grad1, h2 = cell_call(
        cells1_kernel,
        "cells1",
        (swap_flat(spectrum),),
        (h1, pull),
        (point1.T, parity_blocks(proj_square)),
        (sides, sides),
        scratch=(vmem((2, 256, 256), BF16), vmem((BLOCK, 128))),
    )
    point = point_gradient(grad1, h1)
    spectrum, pair1 = mode_call(
        modes_backward_kernel,
        "modes_backward",
        1,
        mode_counts,
        (swap_flat(coef), a1),
        plain,
        ((256, 128), (128, 128)),
        after=(point,),
    )
    extra = proj_gradient(norm_count, h2, target, proj_t.T, point, pair1)
    coef, grad0 = cell_call(
        cells2_kernel,
        "cells2",
        (swap_flat(spectrum), extra),
        (grad1, slope0),
        (point1,),
        (sides,),
        scratch=(vmem((256, 256), BF16),),
        coef=(TILES, 16, 128),
    )
    direct = lax.dot_general(inputs, grad0, TN, preferred_element_type=F32)
    (tail,) = mode_call(
        modes_last_kernel,
        "modes_last",
        0,
        mode_counts,
        (swap(coef), a0, a_in, direct, pair1),
        plain,
        ((264, 128),),
    )
    tails = [tail] + [xor_group(tail, d) for d in range(1, 4)]
    late = swap(spread(tails))
    spectral_grad = outer_products(tails)
    lift_grad, point_grad, proj_grad, loss = finish(late, pointwise[0], lift8)
    return (
        new_fields.reshape(2, 3, 4, 16, 256),
        lift_grad.T,
        point_grad,
        spectral_grad,
        proj_grad,
        loss[0, 0],
    )


def solution(mesh):
    return jax.shard_map(
        local,
        mesh=mesh,
        in_specs=(
            P(None, None, "tile", "role", "rep"),
            P("tile", "role", "rep"),
            P(),
            P(),
            P(),
            P(),
            P(),
            P(),
            P(None, "tile", None, None, None),
            P(),
        ),
        out_specs=(
            P(None, None, "tile", "role", "rep"),
            P(),
            P(),
            P(None, "tile", None, None, None),
            P(),
            P(),
        ),
        check_vma=False,
    )
```

```python
import functools
import math

import jax
import jax.numpy as jnp
import ml_dtypes
import numpy as np
from jax import lax
from jax.experimental import pallas as pl
from jax.experimental.pallas import tpu as pltpu
from jax.sharding import PartitionSpec as P

STEPS = 4
MODES = 8
LAYERS = 2
STEP_TIME = 0.5
PRECISE = lax.Precision.HIGHEST
F32 = jnp.float32
BF16 = jnp.bfloat16
NN = (((1,), (0,)), ((), ()))
NT = (((1,), (1,)), ((), ()))
TN = (((0,), (0,)), ((), ()))
ROOM = 48 * 1024 * 1024
LEAP_ROOM = 40 * 1024 * 1024
CELL_ROOM = 56 * 1024 * 1024
MODE_ROOM = 48 * 1024 * 1024
GROUP = ("role", "rep")
EVERY = ("role", "rep", "tile")
SX, SY, SZ = 64, 16, 256
CELLS = SY * SZ
TILES = 32


def basis(length):
    frequency = np.arange(MODES)[:, None]
    position = np.arange(length)[None, :]
    angles = 2.0 * np.pi * ((frequency * position) % length) / length
    return np.concatenate([np.cos(angles), np.sin(angles)], axis=0) * math.sqrt(2.0 / length)


def split_const(table):
    table = table.astype(np.float32)
    high = table.astype(ml_dtypes.bfloat16)
    low = (table - high.astype(np.float32)).astype(ml_dtypes.bfloat16)
    return high, low


def both_const(table):
    return np.stack(split_const(table))


TABLE_X, TABLE_Y, TABLE_Z = basis(SX), basis(SY), basis(SZ)
KRON_X = both_const(
    np.einsum("ptx,mn->xmptn", TABLE_X.reshape(16, TILES, 2), np.eye(8)).reshape(256, 256)
)
KRON_XT = np.ascontiguousarray(KRON_X.transpose(0, 2, 1))
KRON_Y = both_const(np.einsum("jy,kl->jkyl", TABLE_Y, np.eye(16)).reshape(256, 256))
KRON_YT = np.ascontiguousarray(KRON_Y.transpose(0, 2, 1))
Z_HIGH, Z_LOW = split_const(TABLE_Z)
Z_ROWS = np.concatenate([Z_HIGH, Z_LOW], axis=0)
Z_COLS = np.concatenate([Z_HIGH.T, Z_HIGH.T, Z_LOW.T], axis=1)
Z_HALF = np.stack([Z_ROWS[:, r * 128 : r * 128 + 128] for r in range(2)])
POOL_Z = np.kron(np.eye(128), np.full((2, 1), 0.125)).astype(np.float32)


def halves(value):
    high = value.astype(BF16)
    return high, (value - high.astype(F32)).astype(BF16)


def dot(a, b, dims=NN):
    return lax.dot_general(a, b, dims, preferred_element_type=F32)


def dot3(a, b, dims=NN):
    return dot(a[0], b[0], dims) + dot(a[0], b[1], dims) + dot(a[1], b[0], dims)


def lanes_of(shape):
    return lax.broadcasted_iota(jnp.int32, shape, len(shape) - 1)


def rows_of(shape):
    return lax.broadcasted_iota(jnp.int32, shape, len(shape) - 2)


def square_weight(matrix):
    high, low = halves(matrix)
    one = jnp.concatenate([high, low], axis=1)
    return jnp.concatenate([one, one], axis=0)


def rows_times(value, weight):
    high, low = halves(value)
    out = dot(jnp.concatenate([high, low], axis=1), weight)
    return out[:, :128] + out[:, 128:]


def vmem(shape, dtype=F32):
    return pltpu.VMEM(shape, dtype)


def params(room=ROOM):
    return pltpu.CompilerParams(vmem_limit_bytes=room)


def full(shape):
    return pl.BlockSpec(shape, lambda *_: (0,) * len(shape))


SMEM = pl.BlockSpec(memory_space=pltpu.SMEM)
ANY = pl.BlockSpec(memory_space=pl.ANY)


def call(kernel, ins, outs, after=(), carry=(), room=ROOM, **options):
    first, last = len(ins) + len(after), len(ins) + len(after) + len(carry)

    def run(*refs):
        rest = refs[last:]
        kernel(*refs[: len(ins)], *rest[: len(outs)], *rest[len(outs) + len(carry) :])

    return pl.pallas_call(
        run,
        out_shape=[o[0] for o in outs] + [jax.ShapeDtypeStruct(c.shape, c.dtype) for c in carry],
        in_specs=[i[1] for i in ins] + [ANY] * (len(after) + len(carry)),
        out_specs=[o[1] for o in outs] + [ANY] * len(carry),
        input_output_aliases={first + n: len(outs) + n for n in range(len(carry))},
        compiler_params=params(room),
        **options,
    )(*[i[0] for i in ins], *after, *carry)


def shape_of(*shape):
    return jax.ShapeDtypeStruct(shape, F32)


ONLY_AFTER = [(0, 3), (3, 3), (4, 3), (5, 3), (6, 3)]
ONLY_BEFORE = [(6, 0), (3, 0)]
PLANES = [(c, i) for c in range(7) for i in range(4)]
PLANES = (
    ONLY_AFTER + [p for p in PLANES if p not in ONLY_AFTER and p not in ONLY_BEFORE] + ONLY_BEFORE
)
FIRST, LAST = len(ONLY_AFTER), len(PLANES) - len(ONLY_BEFORE)


def ends_kernel(fields, material, ends, left, right):
    left[...] = jnp.zeros_like(left)
    right[...] = jnp.zeros_like(right)
    for c in range(7):
        rows = slice(c * 64, (c + 1) * 64)
        own = (fields[c] if c < 6 else material[...].astype(F32)).reshape(64, 256)
        left[rows, :] = own[:, 0:128]
        right[rows, :] = own[:, 128:256]
    for b in range(4):
        rows = slice(b * 128, (b + 1) * 128)
        first = jnp.transpose(left[rows, :])[0:8]
        last = jnp.transpose(right[rows, :])[120:128]
        at, lanes = b // 2 * 8, slice(b % 2 * 128, b % 2 * 128 + 128)
        ends[at : at + 8, lanes] = jnp.where(rows_of((8, 128)) < 4, first, last)


def ends_along_z(fields, material):
    return pl.pallas_call(
        ends_kernel,
        out_shape=shape_of(16, 256),
        scratch_shapes=[vmem((512, 128)), vmem((512, 128))],
        compiler_params=params(),
        name="ends",
    )(fields, material)


def pack_kernel(fields, material, ends, packed, after, before):
    for n, (c, i) in enumerate(PLANES):
        plane = fields[c, i] if c < 6 else material[i].astype(F32)
        packed[n] = plane
        if n < LAST:
            after[n] = plane
        if n >= FIRST:
            before[n - FIRST] = plane
    for out in (packed, after, before):
        out[out.shape[0] - 1] = ends[...]


def pack(fields, material, ends):
    count = len(PLANES)
    return pl.pallas_call(
        pack_kernel,
        out_shape=[
            shape_of(count + 1, 16, 256),
            shape_of(LAST + 1, 16, 256),
            shape_of(count - FIRST + 1, 16, 256),
        ],
        compiler_params=params(),
        name="pack",
    )(fields, material, ends)


def here():
    return lax.axis_index("role"), lax.axis_index("rep"), lax.axis_index("tile")


def leap_kernel(
    plan,
    permittivity,
    conductivity,
    own0,
    own1,
    low0,
    low1,
    high0,
    high1,
    pool,
    out_fields,
    out_piece0,
    out_piece1,
    out_piece2,
    out_piece3,
    grid_f,
    keep,
    gain,
    dt_mask,
    edge0,
    edge1,
    sums0,
    sums1,
    reduced,
    staged,
):
    role, rep, tile = here()
    shape8 = (8, 384)
    row8 = rows_of(shape8)
    top = jnp.where((row8 < 4) & (role == 0), 1.0, 0.0)
    bottom = jnp.where((row8 >= 4) & (role == 1), 1.0, 0.0)

    def column(planes, edge):
        ends = planes[planes.shape[0] - 1]
        strip = jnp.concatenate([ends[0:8], ends[8:16]], axis=1)
        row = rows_of((8, 512))
        first = jnp.where((row < 4) & (rep == 0), strip, 0.0)
        last = jnp.where((row >= 4) & (rep == 1), strip, 0.0)
        whole = jnp.concatenate([first, jnp.zeros((112, 512), F32), last], axis=0)
        for b in range(4):
            edge[b * 128 : (b + 1) * 128, :] = jnp.transpose(whole[:, b * 128 : (b + 1) * 128])

    for number, (mine, mate) in enumerate(((low0, low1), (own0, own1), (high0, high1))):
        column(mine, edge0)
        column(mate, edge1)

        for c in range(7):
            for i in range(4):
                n = PLANES.index((c, i)) - (FIRST if number == 2 else 0)
                if not 0 <= n < mine.shape[0] - 1:
                    grid_f[c, 4 * number + i] = jnp.zeros((24, 384), F32)
                    continue
                rows = slice((c * 4 + i) * 16, (c * 4 + i + 1) * 16)
                plane = jnp.concatenate([mine[n], edge0[rows, :]], axis=1)
                other = jnp.concatenate([mate[n], edge1[rows, :]], axis=1)
                halo = other[0:8] * top + other[8:16] * bottom
                grid_f[c, 4 * number + i] = jnp.concatenate([plane, halo], axis=0)

    row = rows_of((24, 384))
    lane = lanes_of((24, 384))
    row_ok = (row < 16) | ((row < 20) & (role == 0)) | ((row >= 20) & (role == 1))
    lane_ok = (lane < 256) | ((lane < 320) & (rep == 0)) | ((lane >= 320) & (rep == 1))
    inside = jnp.where(row_ok & lane_ok, 1.0, 0.0)
    dt_mask[...] = inside * STEP_TIME
    below = jnp.where(tile > 0, 1.0, 0.0)
    above = jnp.where(tile < TILES - 1, 1.0, 0.0)

    def media(p, carry):
        kind = grid_f[6, p]
        level = inside * jnp.where(p >= 8, above, 1.0)

        def choose(values):
            return jnp.where(
                kind < 0.5,
                values[0],
                jnp.where(kind < 1.5, values[1], jnp.where(kind < 2.5, values[2], values[3])),
            )

        permit = choose(permittivity)
        damping = choose(conductivity) * (0.5 * STEP_TIME) / permit
        keep[p] = (1.0 - damping) / (1.0 + damping)
        gain[p] = STEP_TIME / (permit * (1.0 + damping)) * level
        return carry

    lax.fori_loop(1, 11, media, 0, unroll=2)

    def back(value, axis):
        return pltpu.roll(value, value.shape[axis] - 1, axis)

    def step_h(p, carry):
        ex, ey, ez = grid_f[0, p], grid_f[1, p], grid_f[2, p]
        s = dt_mask[...] * below if p < 4 else dt_mask[...]
        d_zy = back(ez, 0) - ez
        d_yz = back(ey, 1) - ey
        d_xz = back(ex, 1) - ex
        d_zx = grid_f[2, p + 1] - ez
        d_yx = grid_f[1, p + 1] - ey
        d_xy = back(ex, 0) - ex
        grid_f[3, p] = grid_f[3, p] - s * (d_zy - d_yz)
        grid_f[4, p] = grid_f[4, p] - s * (d_xz - d_zx)
        grid_f[5, p] = grid_f[5, p] - s * (d_yx - d_xy)
        return carry

    def step_e(p, carry):
        hx, hy, hz = grid_f[3, p], grid_f[4, p], grid_f[5, p]
        k, g = keep[p], gain[p]
        d_zy = hz - pltpu.roll(hz, 1, 0)
        d_yz = hy - pltpu.roll(hy, 1, 1)
        d_xz = hx - pltpu.roll(hx, 1, 1)
        d_zx = hz - grid_f[5, p - 1]
        d_yx = hy - grid_f[4, p - 1]
        d_xy = hx - pltpu.roll(hx, 1, 0)
        grid_f[0, p] = k * grid_f[0, p] + g * (d_zy - d_yz)
        grid_f[1, p] = k * grid_f[1, p] + g * (d_xz - d_zx)
        grid_f[2, p] = k * grid_f[2, p] + g * (d_yx - d_xy)
        return carry

    sums0[...] = jnp.zeros_like(sums0)
    sums1[...] = jnp.zeros_like(sums1)
    for step in range(STEPS):
        for p in range(step, 11 - step):
            step_h(p, 0)
        for p in range(1 + step, 11 - step):
            step_e(p, 0)
        for x in range(2):
            for c in range(6):
                at = (x * 8 + c) * 16
                pair = grid_f[c, 4 + 2 * x, 0:16, 0:256] + grid_f[c, 5 + 2 * x, 0:16, 0:256]
                sums0[at : at + 16, :] = pair[:, 0:128]
                sums1[at : at + 16, :] = pair[:, 128:256]
        for part, sums in enumerate((sums0, sums1)):
            staged[:, part * 128 : (part + 1) * 128] = (
                sums[pl.ds(0, 128, stride=2), :] + sums[pl.ds(1, 128, stride=2), :]
            )
        reduced[step] = lax.dot_general(
            staged[...], pool[...], NN, precision=PRECISE, preferred_element_type=F32
        )
    for c in range(6):
        out_fields[c] = grid_f[c, 4:8, 0:16, 0:256]

    me = role * 2 + rep
    for d, out in enumerate((out_piece0, out_piece1, out_piece2, out_piece3)):
        out[0:128] = reduced[plan[me ^ d] - 1]
        out[128:256] = reduced[STEPS - 1]


def leapfrog(plan, permittivity, conductivity, blocks):
    whole = pl.BlockSpec(memory_space=pltpu.VMEM)
    return call(
        leap_kernel,
        [(v, SMEM) for v in (plan, permittivity, conductivity)]
        + [(v, whole) for v in (*blocks, jnp.asarray(POOL_Z))],
        [
            (shape_of(6, 4, 16, 256), whole),
        ]
        + [(shape_of(256, 128), whole)] * 4,
        room=LEAP_ROOM,
        scratch_shapes=[
            vmem((7, 12, 24, 384)),
            vmem((12, 24, 384)),
            vmem((12, 24, 384)),
            vmem((24, 384)),
            vmem((512, 128)),
            vmem((512, 128)),
            vmem((256, 128)),
            vmem((256, 128)),
            vmem((4, 128, 128)),
            vmem((128, 256)),
        ],
        name="leapfrog",
    )


def fold(value):
    return value[:, 0:128] + value[:, 128:256]


def coef_kernel(piece0, piece1, piece2, piece3, z_half, kron, out, d_scr):
    role, rep, _ = here()
    lane = lanes_of((16, 128))
    for flip, (one, other) in enumerate(((piece0, piece1), (piece2, piece3))):
        total = jnp.zeros((16, 128), F32)
        for z_rows, piece in ((z_half[rep], one), (z_half[1 - rep], other)):
            high, low = halves(
                jnp.concatenate([piece[pl.ds(y, 16, stride=8), :] for y in range(8)], axis=0)
            )
            out_high = dot(z_rows, high, NT)
            total = total + out_high[0:16] + out_high[16:32] + dot(z_rows[0:16], low, NT)
        for y in range(8):
            own = total if y == 0 else pltpu.roll(total, 128 - 16 * y, 1)
            at = pl.multiple_of(((role ^ flip) * 8 + y) * 16, 16)
            d_scr[pl.ds(at, 16), :] = jnp.where(lane < 16, own, 0.0)
    out[...] = dot3((kron[0], kron[1]), halves(d_scr[...]))


def input_coefs(pieces):
    return pl.pallas_call(
        coef_kernel,
        out_shape=shape_of(256, 128),
        scratch_shapes=[vmem((256, 128))],
        compiler_params=params(),
        name="input_coefs",
    )(*pieces, jnp.asarray(Z_HALF), jnp.asarray(KRON_Y))


def prep_kernel(first_row, piece0, piece1, piece2, piece3, weight, out_own, out_mixed):
    role_here, rep_here, _ = here()
    me = role_here * 2 + rep_here
    wide = square_weight(weight[...])
    lane = lanes_of((128, 128))
    for d, piece in enumerate((piece0, piece1, piece2, piece3)):
        source = me ^ d
        role, rep = source // 2, source % 2
        whole = jnp.concatenate(
            [piece[pl.ds(first_row + y, 16, stride=8), :] for y in range(8)], axis=0
        )
        turned = jnp.transpose(whole)
        for y in range(8):
            rows = pl.ds(pl.multiple_of((role * 8 + y) * 256 + rep * 128, 128), 128)
            own = turned if y == 0 else pltpu.roll(turned, 128 - 16 * y, 1)
            own = jnp.where(lane < 16, own, 0.0)
            sides = jnp.concatenate(halves(own), axis=1)
            out_own[rows, :] = sides if out_own.dtype == BF16 else own
            out_mixed[rows, :] = fold(dot(sides, wide))


def prepare(pieces, first_row, weight, as_sides, name):
    own = jax.ShapeDtypeStruct((CELLS, 256), BF16) if as_sides else shape_of(CELLS, 128)
    return pl.pallas_call(
        functools.partial(prep_kernel, first_row),
        out_shape=[own, shape_of(CELLS, 128)],
        compiler_params=params(),
        name=name,
    )(*pieces, weight)


GELU_A = math.sqrt(2.0 / math.pi)
GELU_B = 0.044715


def gelu_both(value):
    square = value * value
    t = jnp.tanh(value * (GELU_A + (GELU_A * GELU_B) * square))
    half = 0.5 + 0.5 * t
    hidden = value * half
    slope = half + hidden * (1.0 - half) * (2.0 * GELU_A + (6.0 * GELU_A * GELU_B) * square)
    return hidden, slope


BLOCK_Y = 8
BLOCK = BLOCK_Y * SZ
CHUNK = 128


def open_cells(spectrum, kron_t, c_scr):
    high, low = halves(dot3((kron_t[0], kron_t[1]), halves(spectrum[...])))
    for y in range(SY):
        lanes = slice(y % BLOCK_Y * 128, y % BLOCK_Y * 128 + 128)
        rows = slice(y * 16, y * 16 + 16)
        c_scr[y // BLOCK_Y, 0:16, lanes] = high[rows]
        c_scr[y // BLOCK_Y, 16:32, lanes] = low[rows]
        c_scr[y // BLOCK_Y, 32:48, lanes] = high[rows]


def chunk_of(wide, n):
    at = n * CHUNK
    return wide[at % SZ : at % SZ + CHUNK, at // SZ * 128 : at // SZ * 128 + 128]


def store_sides(out, rows, value):
    high, low = halves(value)
    out[rows, 0:128] = high
    out[rows, 128:256] = low


def cells_to(sides, z_rows, d_scr, step):
    for n in range(BLOCK_Y):
        out = dot(z_rows[...], sides[n * SZ : (n + 1) * SZ, :])
        at = pl.multiple_of((step * BLOCK_Y + n) * 16, 16)
        d_scr[pl.ds(at, 16), :] = out[0:16, 0:128] + out[0:16, 128:256] + out[16:32, 0:128]


def close_cells(kron, d_scr):
    return dot3((kron[0], kron[1]), halves(d_scr[...]))


def cells0_kernel(spectrum, pre, kron, kron_t, z_rows, z_cols, out_coef, out_h, out_slope, c_scr, d_scr):
    step = pl.program_id(0)

    @pl.when(step == 0)
    def _():
        open_cells(spectrum, kron_t, c_scr)

    spectral = dot(z_cols[...], c_scr[step])
    for n in range(BLOCK // CHUNK):
        rows = slice(n * CHUNK, (n + 1) * CHUNK)
        hidden, slope = gelu_both(chunk_of(spectral, n) + pre[rows, :])
        out_slope[rows, :] = slope
        store_sides(out_h, rows, hidden)
    cells_to(out_h, z_rows, d_scr, step)

    @pl.when(step == pl.num_programs(0) - 1)
    def _():
        out_coef[...] = close_cells(kron, d_scr)


def cells1_kernel(
    spectrum,
    h1,
    pull,
    w_point,
    w_square,
    kron,
    kron_t,
    z_rows,
    z_cols,
    out_coef,
    out_pre,
    out_h,
    c_scr,
    d_scr,
    wide,
    slopes,
):
    step = pl.program_id(0)

    @pl.when(step == 0)
    def _():
        open_cells(spectrum, kron_t, c_scr)
        wide[0] = square_weight(w_point[...])
        wide[1] = square_weight(w_square[...])

    spectral = dot(z_cols[...], c_scr[step])
    direct = dot(h1[...], wide[0])
    for n in range(BLOCK // CHUNK):
        rows = slice(n * CHUNK, (n + 1) * CHUNK)
        hidden, slope = gelu_both(chunk_of(spectral, n) + fold(direct[rows, :]))
        slopes[rows, :] = slope
        store_sides(out_h, rows, hidden)
    back = dot(out_h[...], wide[1])
    for n in range(BLOCK // CHUNK):
        rows = slice(n * CHUNK, (n + 1) * CHUNK)
        store_sides(out_pre, rows, (fold(back[rows, :]) - pull[rows, :]) * slopes[rows, :])
    cells_to(out_pre, z_rows, d_scr, step)

    @pl.when(step == pl.num_programs(0) - 1)
    def _():
        out_coef[...] = close_cells(kron, d_scr)


def cells2_kernel(
    spectrum,
    extra,
    grad1,
    slope0,
    w_point,
    kron,
    kron_t,
    z_rows,
    z_cols,
    out_coef,
    out_pre,
    c_scr,
    d_scr,
    wide,
):
    step = pl.program_id(0)

    @pl.when(step == 0)
    def _():
        open_cells(spectrum, kron_t, c_scr)
        wide[...] = square_weight(w_point[...])

    spectral = dot(z_cols[...], c_scr[step])
    direct = dot(grad1[...], wide[...])
    for n in range(BLOCK // CHUNK):
        rows = slice(n * CHUNK, (n + 1) * CHUNK)
        store_sides(
            out_pre, rows, (chunk_of(spectral, n) + fold(direct[rows, :])) * slope0[rows, :]
        )
    cells_to(out_pre, z_rows, d_scr, step)

    @pl.when(step == pl.num_programs(0) - 1)
    def _():
        out_coef[:, 0:8, :] = close_cells(kron, d_scr).reshape(TILES, 8, 128)
        out_coef[:, 8:16, :] = extra[...]


def cell_call(kernel, name, firsts, streams, weights, outs, scratch=(), coef=(256, 128), **order):
    def block(lanes):
        return pl.BlockSpec((BLOCK, lanes), lambda g: (g, 0))

    consts = [jnp.asarray(c) for c in (KRON_Y, KRON_YT, Z_ROWS, Z_COLS)]
    return call(
        kernel,
        [(v, full(v.shape)) for v in firsts]
        + [(v, block(v.shape[1])) for v in streams]
        + [(v, full(v.shape)) for v in (*weights, *consts)],
        [(shape_of(*coef), full(coef))]
        + [(jax.ShapeDtypeStruct((CELLS, lanes), kind), block(lanes)) for lanes, kind in outs],
        grid=(SY // BLOCK_Y,),
        scratch_shapes=[vmem((SY // BLOCK_Y, 48, BLOCK_Y * 128), BF16), vmem((256, 128))] + list(scratch),
        name=name,
        room=CELL_ROOM,
        **order,
    )


SIDES = pl.BlockSpec((BLOCK, 256), lambda g: (g, 0))


def point_grad_kernel(grad, h1, out, acc):
    step = pl.program_id(0)
    acc[step] = dot(grad[...], h1[...], TN)

    @pl.when(step == pl.num_programs(0) - 1)
    def _():
        point = sum(acc[n, 0:128, :] + acc[n, 128:256, :] for n in range(SY // BLOCK_Y))
        point = fold(point)
        picked = jnp.where(lanes_of((64, 128)) < 64, point[0:64], point[64:128])
        picked = picked + pltpu.roll(picked, 64, 1)
        out[...] = jnp.where(lanes_of((32, 128)) < 64, picked[0:32], picked[32:64])


def point_gradient(grad, h1):
    (out,) = call(
        point_grad_kernel,
        [(grad, SIDES), (h1, SIDES)],
        [(shape_of(32, 128), full((32, 128)))],
        grid=(SY // BLOCK_Y,),
        scratch_shapes=[vmem((SY // BLOCK_Y, 256, 256))],
        name="point_grad",
    )
    return out


def proj_grad_kernel(scale, norm, h2, target, w_proj, point, out, acc, loss_acc, wide, row):
    step = pl.program_id(0)

    @pl.when(step == 0)
    def _():
        wide[...] = square_weight(w_proj[...])
        loss_acc[...] = jnp.zeros_like(loss_acc)

    err = fold(dot(h2[...], wide[...])) - target[...]
    loss_acc[...] += jnp.sum((err * err).reshape(BLOCK // 8, 8, 128), axis=0)
    sides = jnp.concatenate(halves(err * scale), axis=1)
    acc[step] = dot(sides, h2[...], TN)

    @pl.when(step == pl.num_programs(0) - 1)
    def _():
        out[...] = jnp.zeros_like(out)
        out[:, 0, :] = point[...]
        proj = sum(acc[n, 0:16, :] + acc[n, 128:144, :] for n in range(SY // BLOCK_Y))
        proj = fold(proj)
        picked = jnp.where(lanes_of((8, 128)) < 64, proj[0:8], proj[8:16])
        turned = jnp.transpose(picked + pltpu.roll(picked, 64, 1))
        row[...] = jnp.full((32, 128), jnp.sum(loss_acc[...]) / norm)
        row[:, 0:8] = turned[0:32]
        row[:, 8:16] = turned[32:64]
        out[:, 1, :] = row[...]


def proj_gradient(norm, h2, target, w_proj, point, after):
    (out,) = call(
        functools.partial(proj_grad_kernel, 2.0 / norm, norm),
        [
            (h2, SIDES),
            (target, pl.BlockSpec((BLOCK, 128), lambda g: (g, 0))),
            (w_proj, full((128, 128))),
            (point, full((32, 128))),
        ],
        [(shape_of(TILES, 8, 128), full((TILES, 8, 128)))],
        after=(after,),
        grid=(SY // BLOCK_Y,),
        scratch_shapes=[
            vmem((SY // BLOCK_Y, 256, 256)),
            vmem((8, 128)),
            vmem((256, 256), BF16),
            vmem((32, 128)),
        ],
        name="proj_grad",
    )
    return out


def kept_modes(counts, layer):
    row = rows_of((128, 128))
    pair = lax.axis_index("tile") * 8 + row // 16
    kept = (
        (row % 8 < counts[layer, 0])
        & (pair // 16 % 8 < counts[layer, 1])
        & (pair % 8 < counts[layer, 2])
    )
    return jnp.where(kept, 1.0, 0.0)


def pair_up(rows, low_lanes):
    picked = jnp.where(low_lanes, rows[0:128], rows[128:256])
    return picked + pltpu.roll(picked, 64, 1)


MIX_STEPS = 2
MIX_PAIRS = 8 // MIX_STEPS


def mix(g_scr, b_scr, weights, step):
    row, lane = rows_of((16, 256)), lanes_of((16, 256))
    low = lanes_of((16, 128)) < 64
    for n in range(MIX_PAIRS):
        at = pl.multiple_of((step * MIX_PAIRS + n) * 16, 16)
        one = g_scr[pl.ds(at, 16), :]
        wide = jnp.concatenate([one, one], axis=1)
        total = jnp.zeros((32, 128), F32)
        for q in range(4):
            own = jnp.where(row == 4 * q + lane // 64, wide, 0.0)
            sides = jnp.concatenate(halves(own), axis=0)
            both = halves(weights[n, q * 256 : (q + 1) * 256, :])
            total = total + dot(sides, jnp.concatenate(both, axis=1))
        folded = total[0:16] + jnp.where(low, total[16:32], 0.0)
        b_scr[pl.ds(at, 16), :] = folded + pltpu.roll(folded, 64, 1)


def close_modes(b_scr, kept, kron_t, out):
    both = b_scr[...] * kept
    low = lanes_of((128, 128)) < 64
    blocks = jnp.concatenate([jnp.where(low, both, 0.0), jnp.where(low, 0.0, both)], axis=0)
    out[...] = dot3((kron_t[0], kron_t[1]), halves(blocks))


def modes_first_kernel(counts, coef, lift, weights, kron, kron_t, out, out_a, a_scr, b_scr):
    step = pl.program_id(0)

    @pl.when(step == 0)
    def _():
        rows = dot3((kron[0], kron[1]), halves(coef[...]))
        picked = jnp.where(lanes_of((128, 128)) < 8, rows[0:128], rows[128:256])
        picked = picked * kept_modes(counts, 0)
        lifted = dot3(halves(picked), halves(lift[...]))
        a_scr[...] = lifted
        out_a[...] = jnp.where(lanes_of((128, 128)) < 64, picked, lifted)

    mix(a_scr, b_scr, weights, step)

    @pl.when(step == pl.num_programs(0) - 1)
    def _():
        close_modes(b_scr, kept_modes(counts, 0), kron_t, out)


def modes_forward_kernel(counts, coef, weights, kron, kron_t, out, out_a, a_scr, b_scr):
    step = pl.program_id(0)

    @pl.when(step == 0)
    def _():
        rows = dot3((kron[0], kron[1]), halves(coef[...]))
        a = pair_up(rows, lanes_of((128, 128)) < 64) * kept_modes(counts, 1)
        a_scr[...] = a
        out_a[...] = a

    mix(a_scr, b_scr, weights, step)

    @pl.when(step == pl.num_programs(0) - 1)
    def _():
        close_modes(b_scr, kept_modes(counts, 1), kron_t, out)


def take_gradient(rows, kept, saved, g_scr, out_pair):
    low = lanes_of((128, 128)) < 64
    g = pair_up(rows, low) * kept
    g_scr[...] = g
    out_pair[...] = jnp.where(low, g, saved[...])


def modes_backward_kernel(
    counts, coef, saved, weights, kron, kron_t, out, out_pair, g_scr, b_scr
):
    step = pl.program_id(0)

    @pl.when(step == 0)
    def _():
        rows = dot3((kron[0], kron[1]), halves(coef[...]))
        take_gradient(rows, kept_modes(counts, 1), saved, g_scr, out_pair)

    mix(g_scr, b_scr, weights, step)

    @pl.when(step == pl.num_programs(0) - 1)
    def _():
        close_modes(b_scr, kept_modes(counts, 1), kron_t, out)


def modes_last_kernel(
    counts, coef, saved, point, pair1, weights, kron, kron_t, out, g_scr, b_scr
):
    step = pl.program_id(0)

    @pl.when(step == 0)
    def _():
        value = coef[:, 0:8, :].reshape(256, 128)
        rows = dot3((kron[0], kron[1]), halves(value))
        take_gradient(rows, kept_modes(counts, 0), saved, g_scr, out.at[8:136])
        out[136:264] = pair1[...]

    mix(g_scr, b_scr, weights, step)

    @pl.when(step == pl.num_programs(0) - 1)
    def _():
        turned = jnp.transpose(saved[...])[0:16]
        lift = dot3(halves(turned), halves(b_scr[...]))
        lift = lift[0:8] + lift[8:16]
        direct = fold(point[0:16, :] + point[128:144, :])
        direct = direct[0:8] + pltpu.roll(direct[8:16], 64, 1)
        late = jnp.where(lanes_of((8, 128)) < 64, lift, pltpu.roll(direct, 64, 1))
        extra = pltpu.roll(jnp.sum(coef[:, 8:16, :], axis=0), 6, 0)
        out[0:8] = jnp.where(rows_of((8, 128)) < 6, late, extra)


def mode_call(kernel, name, layer, counts, smalls, weights, outs, **order):
    consts = [jnp.asarray(c) for c in (KRON_X, KRON_XT)]
    return call(
        kernel,
        [(counts, SMEM)]
        + [(v, full(v.shape)) for v in smalls]
        + [(weights, pl.BlockSpec((None, MIX_PAIRS, 1024, 64), lambda m: (layer, m, 0, 0)))]
        + [(v, full(v.shape)) for v in consts],
        [(shape_of(*o), full(o)) for o in outs],
        grid=(MIX_STEPS,),
        scratch_shapes=[vmem((128, 128)), vmem((128, 128))],
        name=name,
        room=MODE_ROOM,
        **order,
    )


OUTER_PAIRS = 4


def outer_kernel(tail0, tail1, tail2, tail3, out):
    layer, part = pl.program_id(0), pl.program_id(1)
    row, lane = rows_of((64, 1024)), lanes_of((64, 1024))
    own = row % 16 == lane // 64
    low = lanes_of((64, 128)) < 64
    for n in range(OUTER_PAIRS):
        at = pl.multiple_of(8 + layer * 128 + (part * OUTER_PAIRS + n) * 16, 8)
        block = jnp.concatenate([t[pl.ds(at, 16), :] for t in (tail0, tail1, tail2, tail3)], axis=0)
        grads = halves(jnp.transpose(block)[0:64])
        twice = jnp.where(low, pltpu.roll(block, 64, 1), block)
        spread = halves(jnp.where(own, jnp.concatenate([twice] * 8, axis=1), 0.0))
        result = dot3(grads, spread)
        for r in range(16):
            out[n, r] = result[:, r * 64 : (r + 1) * 64]


def outer_products(tails):
    return pl.pallas_call(
        outer_kernel,
        grid=(LAYERS, 8 // OUTER_PAIRS),
        out_shape=shape_of(LAYERS, 8, 16, 64, 64),
        in_specs=[full((264, 128))] * 4,
        out_specs=pl.BlockSpec((None, OUTER_PAIRS, 16, 64, 64), lambda l, m: (l, m, 0, 0, 0)),
        compiler_params=params(),
        name="outer",
    )(*tails)


def spread_kernel(tail0, tail1, tail2, tail3, out):
    late = (tail0[...] + tail1[...]) + (tail2[...] + tail3[...])
    out[...] = jnp.broadcast_to(late[None], (TILES, 8, 128))


def spread(tails):
    return pl.pallas_call(
        spread_kernel,
        grid=(1,),
        out_shape=shape_of(TILES, 8, 128),
        in_specs=[pl.BlockSpec((8, 128), lambda n: (0, 0))] * 4,
        out_specs=full((TILES, 8, 128)),
        compiler_params=params(),
        name="spread",
    )(*tails)


def finish_kernel(late, point, lift, out_lift, out_point, out_proj, out_loss):
    by_tile = late[...]
    total = jnp.where(rows_of((8, 128)) < 6, jnp.sum(by_tile, axis=0), 0.0)
    through, direct = total[:, 0:64], pltpu.roll(total, 64, 1)[:, 0:64]

    def exact(a, b, dims):
        return lax.dot_general(a, b, dims, precision=PRECISE, preferred_element_type=F32)

    out_point[0] = exact(direct, lift[...], TN)
    through = through + exact(direct, point[...], NN)
    out_lift[...] = through[0:6]
    first = by_tile[:, 6, :]
    out_point[1, 0:32, :] = first[:, 0:64]
    out_point[1, 32:64, :] = first[:, 64:128]
    second = jnp.transpose(by_tile[:, 7, :])
    out_proj[:, 0:32] = second[0:6]
    out_proj[:, 32:64] = second[8:14]
    out_loss[...] = second[16:17, 0:1]


def finish(late, point, lift):
    return pl.pallas_call(
        finish_kernel,
        out_shape=[shape_of(6, 64), shape_of(2, 64, 64), shape_of(6, 64), shape_of(1, 1)],
        compiler_params=params(),
        name="finish",
    )(late, point, lift)


def passed(value, axis, by):
    length = lax.axis_size(axis)
    return lax.ppermute(value, axis, [(i, i + by) for i in range(length) if 0 <= i + by < length])


def across(value, axis):
    return lax.ppermute(value, axis, [(0, 1), (1, 0)])


def xor_group(value, d):
    return lax.ppermute(value, GROUP, [(i, i ^ d) for i in range(4)])


def parity_blocks(matrix):
    zero = jnp.zeros_like(matrix)
    return jnp.concatenate(
        [jnp.concatenate([matrix, zero], axis=1), jnp.concatenate([zero, matrix], axis=1)], axis=0
    )


def local(
    fields,
    material,
    permittivity,
    conductivity,
    plan,
    mode_counts,
    lift_weight,
    pointwise,
    spectral_weight,
    project_weight,
):
    plain = spectral_weight.reshape(LAYERS, 8, 1024, 64)
    turned = jnp.swapaxes(spectral_weight, -1, -2).reshape(LAYERS, 8, 1024, 64)

    fields6 = fields.reshape(6, 4, 16, 256)
    ends = xor_group(ends_along_z(fields6, material), 1)
    own0, after, before = pack(fields6, material, ends)
    low0, high0 = passed(after, "tile", 1), passed(before, "tile", -1)
    low0, high0 = call(lambda *refs: None, [], [], after=(turned,), carry=(low0, high0), name="hold")
    blocks = []
    for value in (own0, low0, high0):
        blocks += [value, across(value, "role")]
    new_fields, *pieces = leapfrog(plan, permittivity, conductivity, blocks)
    pieces = [pieces[0]] + [xor_group(pieces[d], d) for d in range(1, 4)]
    coef = input_coefs(pieces)

    lift8 = jnp.pad(lift_weight.T, ((0, 2), (0, 0)))
    lift16 = jnp.concatenate([lift8, lift8], axis=0)
    lift_pad = jnp.pad(jnp.concatenate([lift16, lift16], axis=1), ((0, 112), (0, 0)))
    first8 = jnp.dot(lift8, pointwise[0].T, precision=PRECISE)
    first = jnp.pad(parity_blocks(first8), ((0, 112), (0, 0)))
    point1 = parity_blocks(pointwise[1])
    proj8 = jnp.pad(project_weight, ((0, 2), (0, 0)))
    proj_t = jnp.pad(parity_blocks(proj8), ((0, 112), (0, 0)))
    norm_count = 6.0 * SX * SY * SZ * plan.shape[0]
    scale = 2.0 / norm_count
    proj_square = jnp.dot(project_weight.T, project_weight, precision=PRECISE) * scale

    def swap(value):
        value = value.reshape(TILES, -1, 128)
        return lax.all_to_all(value, "tile", 0, 0, tiled=True)

    def swap_flat(value):
        return swap(value).reshape(256, 128)

    inputs, pre0 = prepare(pieces, 0, first, True, "prepare_inputs")
    spectrum, a0 = mode_call(
        modes_first_kernel,
        "modes_first",
        0,
        mode_counts,
        (swap_flat(coef), lift_pad),
        turned,
        ((256, 128), (128, 128)),
        after=(pre0,),
    )
    target, pull = prepare(pieces, 128, proj_t * scale, False, "prepare_target")
    sides, plain_out = (256, BF16), (128, F32)
    coef, h1, slope0 = cell_call(
        cells0_kernel,
        "cells0",
        (swap_flat(spectrum),),
        (pre0,),
        (),
        (sides, plain_out),
        after=(pull,),
    )
    spectrum, a1 = mode_call(
        modes_forward_kernel,
        "modes_forward",
        1,
        mode_counts,
        (swap_flat(coef),),
        turned,
        ((256, 128), (128, 128)),
    )
    coef, grad1, h2 = cell_call(
        cells1_kernel,
        "cells1",
        (swap_flat(spectrum),),
        (h1, pull),
        (point1.T, parity_blocks(proj_square)),
        (sides, sides),
        scratch=(vmem((2, 256, 256), BF16), vmem((BLOCK, 128))),
    )
    point = point_gradient(grad1, h1)
    spectrum, pair1 = mode_call(
        modes_backward_kernel,
        "modes_backward",
        1,
        mode_counts,
        (swap_flat(coef), a1),
        plain,
        ((256, 128), (128, 128)),
        after=(point,),
    )
    extra = proj_gradient(norm_count, h2, target, proj_t.T, point, pair1)
    coef, grad0 = cell_call(
        cells2_kernel,
        "cells2",
        (swap_flat(spectrum), extra),
        (grad1, slope0),
        (point1,),
        (sides,),
        scratch=(vmem((256, 256), BF16),),
        coef=(TILES, 16, 128),
    )
    direct = lax.dot_general(inputs, grad0, TN, preferred_element_type=F32)
    (tail,) = mode_call(
        modes_last_kernel,
        "modes_last",
        0,
        mode_counts,
        (swap(coef), a0, direct, pair1),
        plain,
        ((264, 128),),
    )
    tails = [tail] + [xor_group(tail, d) for d in range(1, 4)]
    late = swap(spread(tails))
    spectral_grad = outer_products(tails)
    lift_grad, point_grad, proj_grad, loss = finish(late, pointwise[0], lift8)
    return (
        new_fields.reshape(2, 3, 4, 16, 256),
        lift_grad.T,
        point_grad,
        spectral_grad,
        proj_grad,
        loss[0, 0],
    )


def solution(mesh):
    return jax.shard_map(
        local,
        mesh=mesh,
        in_specs=(
            P(None, None, "tile", "role", "rep"),
            P("tile", "role", "rep"),
            P(),
            P(),
            P(),
            P(),
            P(),
            P(),
            P(None, "tile", None, None, None),
            P(),
        ),
        out_specs=(
            P(None, None, "tile", "role", "rep"),
            P(),
            P(),
            P(None, "tile", None, None, None),
            P(),
            P(),
        ),
        check_vma=False,
    )
```
